128 devices in a mesh: grp: 4 (over x), seq: 32 (over z, y, core).
Axes of the slice: x: 4, y: 4, z: 4, core: 2. Of those that a mesh axis runs over, the one named last changes fastest.
Arguments:
- video_q: bfloat16 [65536, 1536], P(('grp', 'seq')), may hold values from -30 to 30
- video_k: bfloat16 [65536, 1536], P(('grp', 'seq')), may hold values from -30 to 30
- video_v: bfloat16 [65536, 1536], P(('grp', 'seq')), may hold values from -6 to 6
- audio_q: bfloat16 [8192, 1536], P(('grp', 'seq')), may hold values from -30 to 30
- audio_k: bfloat16 [8192, 1536], P(('grp', 'seq')), may hold values from -30 to 30
- audio_v: bfloat16 [8192, 1536], P(('grp', 'seq')), may hold values from -6 to 6
- video_clip: int32 [65536], P(('grp', 'seq')), may hold values from 0 to 35, as said below
- audio_clip: int32 [8192], P(('grp', 'seq')), may hold values from 0 to 35, as said below
Outputs:
- video_out: bfloat16 [65536, 1536], P(('grp', 'seq'))
- audio_out: bfloat16 [8192, 1536], P(('grp', 'seq'))
The draws below stay inside these ranges and needn't reach their ends.
Inputs may be any that keep to these rules, and one draw needn't show every extreme that they name: `video_clip`: group g (0 to 3) holds clips g * 9 to g * 9 + 8. Its audio tokens are the block of 2048 rows from ((g + 1) mod 4) * 64 * 32 on, in clip order; in every group one clip has exactly (17) * 64 audio tokens and each other clip has 64 to 128. Its video tokens are rows g * 512 * 32 onward, in clip order, each clip with exactly 8 times as many video tokens as audio tokens. `audio_clip`: see video_clip.
All inputs are finite; a program needn't handle non-finite values.
Results may differ from the reference program's by a relative error of at most 0.018.
Values may be sent and summed in bfloat16 or wider, within the bound.
A program may use at most 256 MiB of HBM per device.

```python
import math
import jax
import jax.numpy as jnp
from jax import lax

HEADS = 12
HD = 128
VT_DEV = 512
AT_DEV = 64
CLIPS = 9
RATIO = 8
WIDTH = 1536
VID_TOK = 65536
AUD_TOK = 8192
N_GRP = 4
N_SEQ = 32
DEVICES = 128


def audio_starts(key):
    base_key = jax.random.fold_in(key, 101)
    slots = (CLIPS - 1) * AT_DEV
    spare = AT_DEV * (N_SEQ // 4 - 1)

    def per_group(index):
        group_key = jax.random.fold_in(base_key, index)
        widest = jax.random.randint(jax.random.fold_in(group_key, 1), (), 0, CLIPS)
        order = jax.random.permutation(jax.random.fold_in(group_key, 2), slots)
        chosen = (order < spare).astype(jnp.int32)
        others = jnp.sum(chosen.reshape(CLIPS - 1, AT_DEV), axis=1)
        clip_ids = jnp.arange(CLIPS)
        below = jnp.concatenate([others, jnp.zeros((1,), jnp.int32)])
        above = jnp.concatenate([jnp.zeros((1,), jnp.int32), others])
        extra = jnp.where(clip_ids < widest, below, jnp.where(clip_ids > widest, above, N_SEQ // 2 * AT_DEV))
        lengths = AT_DEV + extra
        return jnp.cumsum(lengths) - lengths
    return jax.vmap(per_group)(jnp.arange(N_GRP)).astype(jnp.int32)


def clip_labels(starts, total):
    position = jnp.arange(total)
    inside = jnp.sum(position[None, :, None] >= starts[:, None, 1:], axis=2)
    return (jnp.arange(N_GRP)[:, None] * CLIPS + inside).astype(jnp.int32)


def background(key, rows):
    return jnp.clip(jax.random.normal(key, (rows, HEADS * HD)), -5.0, 5.0)


def draw_video_clip(key, part):
    total = VT_DEV * N_SEQ
    return clip_labels(audio_starts(key) * RATIO, total).reshape(-1)


def draw_audio_clip(key, part):
    total = AT_DEV * N_SEQ
    return jnp.roll(clip_labels(audio_starts(key), total), 1, axis=0).reshape(-1)


def draw_video_q(key, part):
    key = jax.random.fold_in(key, 11)
    values = background(key, VT_DEV * DEVICES)
    return values.astype(jnp.bfloat16)


def draw_audio_k(key, part):
    key = jax.random.fold_in(key, 12)
    values = background(key, AT_DEV * DEVICES)
    return values.astype(jnp.bfloat16)


def draw_audio_q(key, part):
    key = jax.random.fold_in(key, 13)
    values = background(key, AT_DEV * DEVICES)
    return values.astype(jnp.bfloat16)


def draw_video_k(key, part):
    key = jax.random.fold_in(key, 14)
    values = background(key, VT_DEV * DEVICES)
    return values.astype(jnp.bfloat16)


def level_of(own_key, shape, shards, smallest, top_value):
    def one(dim, blocks):
        heights = jax.random.uniform(jax.random.fold_in(jax.random.fold_in(own_key, 6), dim), (blocks,), jnp.float32, smallest / len(shards), top_value / len(shards))
        return jnp.repeat(jnp.exp(heights), shape[dim] // blocks).reshape((-1,) + (1,) * (len(shape) - dim - 1))

    level = one(*shards[0])
    for cut in shards[1:]:
        level = level * one(*cut)
    return level


def centred(key, shape, deviation, reach, shards=(), held_as=jnp.bfloat16):
    values = jax.random.normal(key, shape, jnp.float32) * deviation
    if len(shards) > 0:
        values = level_of(key, shape, shards, -0.22, 0.18) * values
    return jnp.clip(values, min=-reach, max=reach).astype(held_as)


def setup_inputs(seed: int = 0) -> dict:
    seeds = jax.random.split(jax.random.key(seed), 9)
    return {
        "video_q": draw_video_q(jax.random.fold_in(seeds[8], 71), 0),
        "video_k": draw_video_k(jax.random.fold_in(seeds[8], 71), 0),
        "video_v": centred(seeds[2], (VID_TOK, WIDTH), 1.0, 6.0, ((0, 128),)),
        "audio_q": draw_audio_q(jax.random.fold_in(seeds[8], 71), 0),
        "audio_k": draw_audio_k(jax.random.fold_in(seeds[8], 71), 0),
        "audio_v": centred(seeds[5], (AUD_TOK, WIDTH), 1.0, 6.0, ((0, 128),)),
        "video_clip": draw_video_clip(jax.random.fold_in(seeds[8], 71), 0),
        "audio_clip": draw_audio_clip(jax.random.fold_in(seeds[8], 71), 0),
    }


def attend(query, keys, values, query_clip, key_clip):
    same_clip = query_clip[:, None] == key_clip[None, :]
    score_scale = 1.0 / math.sqrt(HD)

    def one_head(operands):
        head_q, head_k, head_v = operands
        scores = jnp.dot(head_q, head_k.T, preferred_element_type=jnp.float32) * score_scale
        scores = jnp.where(same_clip, scores, -jnp.inf)
        maxima = lax.optimization_barrier(jnp.max(scores, axis=1, keepdims=True))
        weights = jnp.exp(scores - maxima)
        denominator = lax.optimization_barrier(jnp.sum(weights, axis=1, keepdims=True))
        output = jnp.dot(weights.astype(jnp.bfloat16), head_v, preferred_element_type=jnp.float32)
        return (output / denominator).astype(jnp.bfloat16)
    rows = query.shape[0]
    split_q = query.reshape(rows, HEADS, HD).transpose(1, 0, 2)
    split_k = keys.reshape(keys.shape[0], HEADS, HD).transpose(1, 0, 2)
    split_v = values.reshape(values.shape[0], HEADS, HD).transpose(1, 0, 2)
    result = lax.map(one_head, (split_q, split_k, split_v))
    return result.transpose(1, 0, 2).reshape(rows, HEADS * HD)

def reference(video_q, video_k, video_v, audio_q, audio_k, audio_v, video_clip, audio_clip):
    groups = N_GRP
    video_len = VT_DEV * N_SEQ
    audio_len = AT_DEV * N_SEQ
    width = HEADS * HD

    def video_group(array):
        return array.reshape((groups, video_len) + array.shape[1:])

    def audio_group(array):
        return jnp.roll(array.reshape((groups, audio_len) + array.shape[1:]), -1, axis=0)
    grouped_vq = video_group(video_q)
    grouped_vk = video_group(video_k)
    grouped_vv = video_group(video_v)
    grouped_vc = video_group(video_clip)
    grouped_aq = audio_group(audio_q)
    grouped_ak = audio_group(audio_k)
    grouped_av = audio_group(audio_v)
    grouped_ac = audio_group(audio_clip)
    video_out = lax.map(lambda operands: attend(*operands), (grouped_vq, grouped_ak, grouped_av, grouped_vc, grouped_ac))
    audio_here = lax.map(lambda operands: attend(*operands), (grouped_aq, grouped_vk, grouped_vv, grouped_ac, grouped_vc))
    audio_out = jnp.roll(audio_here, 1, axis=0)
    return (video_out.reshape(groups * video_len, width), audio_out.reshape(groups * audio_len, width))
```

```python
import math

import jax
import jax.numpy as jnp
from jax import lax
from jax.experimental import pallas as pl
from jax.experimental.pallas import tpu as pltpu
from jax.sharding import PartitionSpec as P

MESH = pl.DeviceIdType.MESH
BF = jnp.bfloat16
F32 = jnp.float32
HD = 128
CLIPS = 9
SCALE = math.log2(math.e) / math.sqrt(HD)
FAR = -1048576.0
LOW = -32768.0
BLOCKS = 10
STAT = 3 * HD
ROWS = STAT + 16


def kernel(
    first_ref, vq_hbm, vk_hbm, vv_hbm, ve_hbm, aq_hbm, ak_hbm, av_hbm,
    vout_hbm, aout_hbm,
    vq, vk, vv, ve, aq, ak, av, vt, window, part, got1, got2, vo, ao,
    x_send, x_recv, g_send, g_recv, v_send, v_recv, v_local, r_send, r_recv, o_send, o_recv, o_local,
):
    g = lax.axis_index("grp")
    s = lax.axis_index("seq")
    core = lax.rem(s, 2)
    chip = s // 2
    z, y = chip // 4, lax.rem(chip, 4)
    zp, zm, z2 = lax.rem(z + 1, 4), lax.rem(z + 3, 4), lax.rem(z + 2, 4)
    yp, ym, y2 = lax.rem(y + 1, 4), lax.rem(y + 3, 4), lax.rem(y + 2, 4)
    gp, gm = lax.rem(g + 1, 4), lax.rem(g + 3, 4)

    def device(grp, zz, yy, cc):
        return (grp, (zz * 4 + yy) * 2 + cc)

    other = device(g, z, y, 1 - core)
    to_yp, to_ym, to_y2 = (device(g, z, b, core) for b in (yp, ym, y2))
    to_zp, to_zm, to_z2 = (device(g, b, y, core) for b in (zp, zm, z2))
    before = lax.rem(chip + 15, 16)
    after = lax.rem(chip + 1, 16)
    result_low = (gp, chip * 2)
    result_high = (gp, before * 2 + 1)

    barrier = pltpu.get_barrier_semaphore()

    def greet(dev):
        pl.semaphore_signal(barrier, inc=1, device_id=dev, device_id_type=MESH)

    for dev in (other, to_yp, to_ym, to_y2, to_zp, to_zm, to_z2):
        greet(dev)
    for cc in (0, 1):
        greet(device(gm, z, y, cc))
        greet(device(gp, z, y, cc))
    greet(result_high)

    @pl.when(core == 1)
    def _():
        greet((gm, after * 2))
        greet((gm, after * 2 + 1))

    pl.semaphore_wait(barrier, 12 + 2 * core)

    def remote(src, dst, ssem, rsem, dev):
        return pltpu.make_async_remote_copy(
            src_ref=src, dst_ref=dst, send_sem=ssem, recv_sem=rsem, device_id=dev, device_id_type=MESH
        )

    def columns(half, width):
        return pl.ds(pl.multiple_of(half * width, 128), width)

    tensors = ((aq_hbm, aq, 896), (ak_hbm, ak, 768), (av_hbm, av, 768))

    def x_step(t):
        src, dst, width = tensors[t]
        return [
            remote(
                src.at[:, pl.ds(cc * width, width)], dst.at[core, z, y], x_send.at[t, cc],
                x_recv.at[t, core], device(gm, z, y, cc),
            )
            for cc in (0, 1)
        ]

    def x_wait(t):
        src, dst, width = tensors[t]
        for cc in (0, 1):
            remote(
                src.at[:, pl.ds(cc * width, width)], dst.at[cc, z, y], x_send.at[t, cc],
                x_recv.at[t, cc], device(gm, z, y, cc),
            ).wait_recv()

    def gather(t, stage):
        x = tensors[t][1]
        low, high = pl.ds(0, 32), pl.ds(32, 32)
        first, last = pl.ds(0, 2), pl.ds(2, 2)
        plan = (
            (x.at[0, z, y], to_yp),
            (x.at[0, z, y], to_ym),
            (x.at[1, z, y], to_zp),
            (x.at[1, z, y], to_zm),
        ), (
            (x.at[0, z, ym, low], to_yp),
            (x.at[0, z, yp, high], to_ym),
            (x.at[1, zm, y, low], to_zp),
            (x.at[1, zp, y, high], to_zm),
        ), (
            (x.at[0, z], to_zp),
            (x.at[0, z], to_zm),
            (x.at[1, :, y], to_yp),
            (x.at[1, :, y], to_ym),
        ), (
            (x.at[0, zm, first], to_zp),
            (x.at[0, zp, last], to_zm),
            (x.at[1, first, ym], to_yp),
            (x.at[1, last, yp], to_ym),
        )
        return [
            remote(ref, ref, g_send.at[t, stage * 4 + i], g_recv.at[t, stage * 4 + i], dev)
            for i, (ref, dev) in enumerate(plan[stage])
        ]

    def start(copies):
        for copy in copies:
            copy.start()

    def arrive(copies):
        for copy in copies:
            copy.wait_recv()

    def sent(copies):
        for copy in copies:
            copy.wait_send()

    video = ((vk_hbm, vk), (vv_hbm, vv), (vq_hbm, vq))
    own_rows = pl.ds(pl.multiple_of(core * 512, 512), 512)
    other_rows = pl.ds(pl.multiple_of((1 - core) * 512, 512), 512)

    def swap(i):
        if i == 3:
            return (
                remote(ve_hbm, ve.at[own_rows], v_send.at[3], v_recv.at[3], other),
                pltpu.make_async_copy(ve_hbm, ve.at[own_rows], v_local.at[3]),
            )
        src, dst = video[i]
        return (
            remote(src.at[:, columns(1 - core, 768)], dst.at[own_rows], v_send.at[i], v_recv.at[i], other),
            pltpu.make_async_copy(src.at[:, columns(core, 768)], dst.at[own_rows], v_local.at[i]),
        )

    def swap_start(i):
        away, here = swap(i)
        away.start()
        here.start()

    def swap_wait(i):
        away, here = swap(i)
        away.wait_recv()
        here.wait()

    start(x_step(0))
    swap_start(3)
    swap_start(0)
    swap_start(1)
    start(x_step(1))
    start(x_step(2))
    swap_start(2)

    x_wait(0)
    start(gather(0, 0))
    arrive(gather(0, 0))
    start(gather(0, 1))
    arrive(gather(0, 1))
    start(gather(0, 2))
    x_wait(1)
    start(gather(1, 0))

    swap_wait(1)

    def turn(h, carry):
        cols = pl.ds(pl.multiple_of(h * HD, HD), HD)
        vt[h, pl.ds(0, HD), :] = vv[:, cols].T
        vt[h, pl.ds(HD, 16), :] = jnp.ones((16, 1024), BF)
        return carry

    lax.fori_loop(0, 6, turn, 0)
    swap_wait(0)
    swap_wait(3)

    arrive(gather(1, 0))
    start(gather(1, 1))
    arrive(gather(0, 2))
    start(gather(0, 3))
    arrive(gather(1, 1))
    start(gather(1, 2))
    x_wait(2)
    start(gather(2, 0))
    arrive(gather(0, 3))

    first = first_ref[0]

    def block(i):
        return jnp.bitwise_and(first + i, 15)

    def pieces(ref, i, cols):
        b, a = block(i - 1), block(i)
        return [ref[1, b // 4, jnp.bitwise_and(b, 3), :, cols], ref[0, a // 4, jnp.bitwise_and(a, 3), :, cols]]

    marks = pl.ds(768, HD)

    def audio_step(step, carry):
        half, tile = step // 5, lax.rem(step, 5)
        mark = jnp.concatenate(pieces(aq, 2 * tile, marks) + pieces(aq, 2 * tile + 1, marks), axis=0)
        tops, sums = [], []
        for hh in range(3):
            h = half * 3 + hh
            cols = pl.ds(pl.multiple_of(h * HD, HD), HD)
            q = jnp.concatenate(pieces(aq, 2 * tile, cols) + pieces(aq, 2 * tile + 1, cols), axis=0)
            q = jnp.concatenate([q, mark], axis=1)
            k = jnp.concatenate([vk[:, cols], ve[...]], axis=1)
            scores = lax.dot_general(k, q, (((1,), (1,)), ((), ())), preferred_element_type=F32) * SCALE
            top = jnp.maximum(jnp.max(scores, axis=0, keepdims=True), LOW).astype(BF).astype(F32)
            weights = jnp.exp2(scores - top).astype(BF)
            out = jnp.dot(vt[h], weights, preferred_element_type=F32)
            tops.append(top)
            sums.append(out[HD : HD + 1])
            for b in range(2):
                window[half, 2 * tile + b, pl.ds(hh * HD, HD), :] = out[:HD, b * HD : (b + 1) * HD].astype(BF)
        top, total = jnp.concatenate(tops, axis=0), jnp.concatenate(sums, axis=0)
        high = total.astype(BF).astype(F32)
        gap = jnp.zeros((1, 256), F32)
        stats = jnp.concatenate([top, gap, total - high, gap, high, jnp.zeros((5, 256), F32)], axis=0)
        for b in range(2):
            window[half, 2 * tile + b, pl.ds(STAT, 16), :] = stats[:, b * HD : (b + 1) * HD].astype(BF)

        @pl.when(step == 2)
        def _():
            arrive(gather(2, 0))
            start(gather(2, 1))

        @pl.when(step == 5)
        def _():
            arrive(gather(1, 2))
            start(gather(1, 3))
            arrive(gather(2, 1))
            start(gather(2, 2))

        return carry

    lax.fori_loop(0, 10, audio_step, 0)

    empty = jnp.where(lax.broadcasted_iota(jnp.int32, (16, HD), 0) < 3, LOW, 0.0)

    def place(b, carry):
        at = jnp.bitwise_and(b - first, 15)
        inside = (at < BLOCKS).astype(F32)
        at = jnp.minimum(at, BLOCKS - 1)
        bz, by = b // 4, lax.rem(b, 4)
        for half in range(2):
            body = window[half, at, pl.ds(0, STAT), :].astype(F32)
            part[half, bz, by, pl.ds(0, STAT), :] = (body * inside).astype(BF)
            stats = window[half, at, pl.ds(STAT, 16), :].astype(F32)
            part[half, bz, by, pl.ds(STAT, 16), :] = (stats * inside + empty * (1.0 - inside)).astype(BF)
        return carry

    lax.fori_loop(0, 16, place, 0)

    def slab(half, where, lo):
        if half == 0:
            return part.at[0, where, pl.ds(lo, 2)]
        return part.at[1, pl.ds(lo, 2), where]

    axes = ((z, zp, zm, z2, to_zp, to_zm), (y, yp, ym, y2, to_yp, to_ym))
    crosses = ((y, yp, ym, y2, to_yp, to_ym, to_y2), (z, zp, zm, z2, to_zp, to_zm, to_z2))

    def reduce1(half):
        _, p, m, two, to_p, to_m = axes[half]
        plan = (
            (slab(half, two, 0), to_p), (slab(half, two, 2), to_m),
            (slab(half, p, 2), to_p), (slab(half, m, 0), to_m),
            (slab(half, p, 0), to_p), (slab(half, m, 2), to_m),
        )
        return [
            remote(ref, got1.at[half, i], r_send.at[half, i], r_recv.at[half, i], dev)
            for i, (ref, dev) in enumerate(plan)
        ]

    def one(half, u):
        if half == 0:
            return part.at[0, z, u]
        return part.at[1, u, y]

    def reduce2(half):
        _, p, m, two, to_p, to_m, to_2 = crosses[half]
        return [
            remote(one(half, u), got2.at[half, i], r_send.at[half, 6 + i], r_recv.at[half, 6 + i], dev)
            for i, (u, dev) in enumerate(((p, to_p), (m, to_m), (two, to_2)))
        ]

    def merged(refs):
        stats = [ref[pl.ds(STAT, 16), :].astype(F32) for ref in refs]
        tops = [x[0:3] for x in stats]
        top = tops[0]
        for x in tops[1:]:
            top = jnp.maximum(top, x)
        factors = [jnp.exp2(x - top) for x in tops]
        total = sum((x[8:11] + x[4:7]) * f for x, f in zip(stats, factors))
        outs = [
            sum(ref[pl.ds(hh * HD, HD), :].astype(F32) * f[hh : hh + 1] for ref, f in zip(refs, factors))
            for hh in range(3)
        ]
        return outs, top, total

    def merge_into(target, sources):
        outs, top, total = merged([target] + sources)
        for hh in range(3):
            target[pl.ds(hh * HD, HD), :] = outs[hh].astype(BF)
        high = total.astype(BF).astype(F32)
        gap = jnp.zeros((1, HD), F32)
        stats = jnp.concatenate([top, gap, total - high, gap, high, jnp.zeros((5, HD), F32)], axis=0)
        target[pl.ds(STAT, 16), :] = stats.astype(BF)

    def merge_slab(half, where, lo, slots):
        def body(i, carry):
            target = part.at[0, where, lo + i] if half == 0 else part.at[1, lo + i, where]
            merge_into(target, [got1.at[half, slot, i] for slot in slots])
            return carry

        lax.fori_loop(0, 2, body, 0)

    def reduce_start(half):
        start(reduce1(half)[:4])

    def reduce_pass(half):
        _, p, m, *_ = axes[half]
        copies = reduce1(half)
        copies[0].wait_recv()
        merge_slab(half, p, 0, (0,))
        copies[4].start()
        copies[1].wait_recv()
        merge_slab(half, m, 2, (1,))
        copies[5].start()

    def reduce_cross(half):
        own = axes[half][0]
        arrive(reduce1(half)[2:])
        merge_slab(half, own, 0, (3, 4))
        merge_slab(half, own, 2, (2, 5))
        start(reduce2(half))

    def reduce_end(half):
        own = crosses[half][0]
        arrive(reduce2(half))
        outs, _, total = merged([one(half, own)] + [got2.at[half, i] for i in range(3)])
        scale = 1.0 / total
        for hh in range(3):
            done = (outs[hh] * scale[hh : hh + 1]).T
            ao[:, pl.ds((half * 3 + hh) * HD, HD)] = done.astype(BF)

    def results():
        mine = columns(core, 768)
        return [
            remote(ao.at[pl.ds(64, 64)], aout_hbm.at[:, mine], o_send.at[0], o_recv.at[core], result_low),
            remote(ao.at[pl.ds(0, 64)], aout_hbm.at[:, mine], o_send.at[1], o_recv.at[core], result_high),
        ]

    arrive(gather(2, 2))
    start(gather(2, 3))
    reduce_start(0)
    reduce_start(1)
    swap_wait(2)
    arrive(gather(1, 3))
    arrive(gather(2, 3))

    def video_step(h, carry):
        cols = pl.ds(pl.multiple_of(h * HD, HD), HD)

        def rows(ref, cc):
            return jnp.concatenate([piece for i in range(BLOCKS) for piece in pieces(ref, i, cc)], axis=0)

        k = jnp.concatenate([rows(ak, cols), rows(aq, marks)], axis=1)
        v = jnp.concatenate([rows(av, cols).T, jnp.ones((16, BLOCKS * HD), BF)], axis=0)
        for tile in range(4):
            here = pl.ds(tile * 256, 256)
            q = jnp.concatenate([vq[here, cols], ve[here, :]], axis=1)
            scores = lax.dot_general(k, q, (((1,), (1,)), ((), ())), preferred_element_type=F32) * SCALE
            top = jnp.max(scores, axis=0, keepdims=True)
            weights = jnp.exp2(scores - top).astype(BF)
            out = jnp.dot(v, weights, preferred_element_type=F32)
            done = out[:HD] * (1.0 / out[HD : HD + 1])
            vo[here, cols] = done.T.astype(BF)

        @pl.when(h == 0)
        def _():
            reduce_pass(0)
            reduce_pass(1)

        @pl.when(h == 2)
        def _():
            reduce_cross(0)
            reduce_cross(1)

        @pl.when(h == 4)
        def _():
            reduce_end(0)
            reduce_end(1)
            start(results())

        return carry

    lax.fori_loop(0, 6, video_step, 0)

    mine = columns(core, 768)
    away = remote(vo.at[other_rows], vout_hbm.at[:, mine], o_send.at[2], o_recv.at[2], other)
    here = pltpu.make_async_copy(vo.at[own_rows], vout_hbm.at[:, mine], o_local)
    away.start()
    here.start()

    for t in range(3):
        sent(x_step(t))
        for stage in range(4):
            sent(gather(t, stage))
    for i in range(4):
        swap(i)[0].wait_send()
    for half in range(2):
        sent(reduce1(half))
        sent(reduce2(half))
    sent(results())
    for cc in (0, 1):
        remote(
            ao.at[pl.ds(0, 64)], aout_hbm.at[:, pl.ds(cc * 768, 768)], o_send.at[0], o_recv.at[cc], result_low
        ).wait_recv()
    here.wait()
    away.wait()


def on_device(video_q, video_k, video_v, audio_q, audio_k, audio_v, video_clip, audio_clip):
    core = lax.rem(lax.axis_index("seq"), 2)
    video_mark, audio_mark = lax.rem(video_clip, CLIPS), lax.rem(audio_clip, CLIPS)
    lanes = jnp.arange(HD, dtype=jnp.int32)[None, :]
    video_extra = jnp.where(video_mark[:, None] == lanes, 0.0, FAR).astype(BF)
    audio_extra = (audio_mark[:, None] == lanes).astype(BF)
    audio_q = jnp.concatenate([audio_q[:, :768], audio_extra, audio_q[:, 768:], audio_extra], axis=1)
    first = jnp.where(core == 0, video_mark[0], video_mark[-1] - 1).reshape(1)
    anywhere = pl.BlockSpec(memory_space=pl.ANY)
    dma = pltpu.SemaphoreType.DMA
    return pl.pallas_call(
        kernel,
        out_shape=(
            jax.ShapeDtypeStruct(video_q.shape, BF),
            jax.ShapeDtypeStruct(audio_k.shape, BF),
        ),
        in_specs=[pl.BlockSpec(memory_space=pltpu.SMEM)] + [anywhere] * 7,
        out_specs=(anywhere, anywhere),
        scratch_shapes=[
            pltpu.VMEM((1024, 768), BF),
            pltpu.VMEM((1024, 768), BF),
            pltpu.VMEM((1024, 768), BF),
            pltpu.VMEM((1024, HD), BF),
            pltpu.VMEM((2, 4, 4, 64, 896), BF),
            pltpu.VMEM((2, 4, 4, 64, 768), BF),
            pltpu.VMEM((2, 4, 4, 64, 768), BF),
            pltpu.VMEM((6, HD + 16, 1024), BF),
            pltpu.VMEM((2, BLOCKS, ROWS, HD), BF),
            pltpu.VMEM((2, 4, 4, ROWS, HD), BF),
            pltpu.VMEM((2, 6, 2, ROWS, HD), BF),
            pltpu.VMEM((2, 3, ROWS, HD), BF),
            pltpu.VMEM((1024, 768), BF),
            pltpu.VMEM((HD, 768), BF),
            dma((3, 2)),
            dma((3, 2)),
            dma((3, 16)),
            dma((3, 16)),
            dma((4,)),
            dma((4,)),
            dma((4,)),
            dma((2, 9)),
            dma((2, 9)),
            dma((3,)),
            dma((3,)),
            dma,
        ],
        compiler_params=pltpu.CompilerParams(
            collective_id=0, has_side_effects=True, vmem_limit_bytes=56 * 1024 * 1024
        ),
    )(first, video_q, video_k, video_v, video_extra, audio_q, audio_k, audio_v)


def solution(mesh):
    spread = P(("grp", "seq"), None)
    return jax.shard_map(
        on_device,
        mesh=mesh,
        in_specs=(spread,) * 6 + (P(("grp", "seq")),) * 2,
        out_specs=(spread, spread),
        check_vma=False,
    )
```

```python
import math

import jax
import jax.numpy as jnp
from jax import lax
from jax.experimental import pallas as pl
from jax.experimental.pallas import tpu as pltpu
from jax.sharding import PartitionSpec as P

MESH = pl.DeviceIdType.MESH
BF = jnp.bfloat16
F32 = jnp.float32
HD = 128
CLIPS = 9
SCALE = math.log2(math.e) / math.sqrt(HD)
FAR = -1048576.0
LOW = -32768.0
BLOCKS = 10
STAT = 3 * HD
ROWS = STAT + 16


def kernel(
    clip_smem, video_clip, audio_clip, vq_hbm, vk_hbm, vv_hbm, aq_hbm, ak_hbm, av_hbm,
    vout_hbm, aout_hbm,
    vq, vk, vv, ve, aq, ak, av, mk, am, mk_own, vt, wt, buf_a, buf_b, tops, sums, window, part, got1, got2, vo, ao,
    x_send, x_recv, g_send, g_recv, v_send, v_recv, v_local, r_send, r_recv, o_send, o_recv, w_send, w_recv, w_local,
):
    g = lax.axis_index("grp")
    s = lax.axis_index("seq")
    core = lax.rem(s, 2)
    chip = s // 2
    z, y = chip // 4, lax.rem(chip, 4)
    zp, zm, z2 = lax.rem(z + 1, 4), lax.rem(z + 3, 4), lax.rem(z + 2, 4)
    yp, ym, y2 = lax.rem(y + 1, 4), lax.rem(y + 3, 4), lax.rem(y + 2, 4)
    gp, gm = lax.rem(g + 1, 4), lax.rem(g + 3, 4)

    def device(grp, zz, yy, cc):
        return (grp, (zz * 4 + yy) * 2 + cc)

    other = device(g, z, y, 1 - core)
    to_yp, to_ym, to_y2 = (device(g, z, b, core) for b in (yp, ym, y2))
    to_zp, to_zm, to_z2 = (device(g, b, y, core) for b in (zp, zm, z2))
    before = lax.rem(chip + 15, 16)
    after = lax.rem(chip + 1, 16)
    result_low = (gp, chip * 2)
    result_high = (gp, before * 2 + 1)

    barrier = pltpu.get_barrier_semaphore()

    def greet(dev):
        pl.semaphore_signal(barrier, inc=1, device_id=dev, device_id_type=MESH)

    for dev in (other, to_yp, to_ym, to_y2, to_zp, to_zm, to_z2):
        greet(dev)
    for cc in (0, 1):
        greet(device(gm, z, y, cc))
        greet(device(gp, z, y, cc))
    greet(result_high)

    @pl.when(core == 1)
    def _():
        greet((gm, after * 2))
        greet((gm, after * 2 + 1))

    pl.semaphore_wait(barrier, 12 + 2 * core)

    def remote(src, dst, ssem, rsem, dev):
        return pltpu.make_async_remote_copy(
            src_ref=src, dst_ref=dst, send_sem=ssem, recv_sem=rsem, device_id=dev, device_id_type=MESH
        )

    def columns(half, width):
        return pl.ds(pl.multiple_of(half * width, 128), width)

    tensors = ((aq_hbm, aq), (ak_hbm, ak), (av_hbm, av), (mk_own, mk))

    def x_copies(t, sender):
        src, dst = tensors[t]
        return [
            remote(
                src if t == 3 else src.at[:, pl.ds(cc * 768, 768)], dst.at[sender, z, y], x_send.at[t, cc],
                x_recv.at[t, sender], device(gm, z, y, cc),
            )
            for cc in (0, 1)
        ]

    def x_step(t):
        return x_copies(t, core)

    def x_wait(t):
        for cc in (0, 1):
            x_copies(t, cc)[0].wait_recv()

    def gather(t, stage):
        x = tensors[t][1]
        rows = x.shape[3] // 2
        low, high = pl.ds(0, rows), pl.ds(rows, rows)
        first, last = pl.ds(0, 2), pl.ds(2, 2)
        plan = (
            (x.at[0, z, y], to_yp),
            (x.at[0, z, y], to_ym),
            (x.at[1, z, y], to_zp),
            (x.at[1, z, y], to_zm),
        ), (
            (x.at[0, z, ym, low], to_yp),
            (x.at[0, z, yp, high], to_ym),
            (x.at[1, zm, y, low], to_zp),
            (x.at[1, zp, y, high], to_zm),
        ), (
            (x.at[0, z], to_zp),
            (x.at[0, z], to_zm),
            (x.at[1, :, y], to_yp),
            (x.at[1, :, y], to_ym),
        ), (
            (x.at[0, zm, first], to_zp),
            (x.at[0, zp, last], to_zm),
            (x.at[1, first, ym], to_yp),
            (x.at[1, last, yp], to_ym),
        )
        return [
            remote(ref, ref, g_send.at[t, stage * 4 + i], g_recv.at[t, stage * 4 + i], dev)
            for i, (ref, dev) in enumerate(plan[stage])
        ]

    def start(copies):
        for copy in copies:
            copy.start()

    def arrive(copies):
        for copy in copies:
            copy.wait_recv()

    def sent(copies):
        for copy in copies:
            copy.wait_send()

    video = ((vk_hbm, vk), (vv_hbm, vv), (vq_hbm, vq))
    own_rows = pl.ds(pl.multiple_of(core * 512, 512), 512)
    other_rows = pl.ds(pl.multiple_of((1 - core) * 512, 512), 512)

    def swap(i):
        src, dst = video[i]
        return (
            remote(src.at[:, columns(1 - core, 768)], dst.at[own_rows], v_send.at[i], v_recv.at[i], other),
            pltpu.make_async_copy(src.at[:, columns(core, 768)], dst.at[own_rows], v_local.at[i]),
        )

    def swap_start(i):
        away, here = swap(i)
        away.start()
        here.start()

    def swap_wait(i):
        away, here = swap(i)
        away.wait_recv()
        here.wait()

    def swap_marks():
        return remote(ve.at[own_rows], ve.at[own_rows], v_send.at[3], v_recv.at[3], other)

    start(x_step(0))
    swap_start(0)
    swap_start(1)

    numbers = (audio_clip[...] - gm * CLIPS).astype(F32)
    numbers = jnp.concatenate([numbers, numbers], axis=1)
    mk_own[...] = jnp.broadcast_to(numbers, (32, HD)).astype(BF)
    start(x_step(3))
    clips = lax.broadcasted_iota(jnp.int32, (HD, HD), 0)
    for i in range(4):
        same = video_clip[i : i + 1, :] - g * CLIPS == clips
        at = pl.multiple_of(core * 512 + i * HD, HD)
        ve[pl.ds(at, HD), :] = jnp.where(same, 0.0, FAR).T.astype(BF)
    swap_marks().start()

    x_wait(3)
    start(gather(3, 0))
    x_wait(0)
    start(gather(0, 0))
    start(x_step(1))
    arrive(gather(3, 0))
    start(gather(3, 1))
    arrive(gather(0, 0))
    start(gather(0, 1))
    arrive(gather(3, 1))
    start(gather(3, 2))
    arrive(gather(0, 1))
    start(gather(0, 2))
    x_wait(1)
    start(gather(1, 0))
    start(x_step(2))
    swap_start(2)

    swap_wait(1)

    def turn(h, carry):
        cols = pl.ds(pl.multiple_of(h * HD, HD), HD)
        vt[h, pl.ds(0, HD), :] = vv[:, cols].T
        vt[h, pl.ds(HD, 16), :] = jnp.ones((16, 1024), BF)
        return carry

    lax.fori_loop(0, 6, turn, 0)
    x_wait(2)
    start(gather(2, 0))
    arrive(gather(3, 2))
    start(gather(3, 3))
    arrive(gather(1, 0))
    start(gather(1, 1))
    arrive(gather(2, 0))
    start(gather(2, 1))
    arrive(gather(0, 2))
    start(gather(0, 3))
    arrive(gather(1, 1))
    start(gather(1, 2))
    arrive(gather(2, 1))
    start(gather(2, 2))
    arrive(gather(3, 3))

    lanes = lax.broadcasted_iota(jnp.int32, (HD, HD), 0).astype(F32)

    def expand(i, carry):
        bz, by = i // 4, lax.rem(i, 4)
        for cc in (0, 1):
            numbers = mk[cc, bz, by, pl.ds(0, 16), :].astype(F32)[0:1]
            am[cc, bz, by] = jnp.where(numbers == lanes, 1.0, 0.0).T[0:64].astype(BF)
        return carry

    lax.fori_loop(0, 16, expand, 0)
    swap_wait(0)
    swap_marks().wait_recv()
    arrive(gather(0, 3))

    first = jnp.where(core == 0, clip_smem[0], clip_smem[511] - 1) - g * CLIPS

    def block(i):
        return jnp.bitwise_and(first + i, 15)

    def pieces(ref, i, cols):
        b, a = block(i - 1), block(i)
        return [ref[1, b // 4, jnp.bitwise_and(b, 3), :, cols], ref[0, a // 4, jnp.bitwise_and(a, 3), :, cols]]

    marks = pl.ds(0, HD)

    def packed(top, total):
        high = total.astype(BF).astype(F32)
        gap = jnp.zeros((1, HD), F32)
        return jnp.concatenate([top, gap, total - high, gap, high, jnp.zeros((5, HD), F32)], axis=0)

    def pipeline(units, sizes, scores_of, finish, events):
        def both(u_scores, u_out, buf_scores, buf_out, top):
            q, k_of = scores_of(u_scores)
            if u_out is not None:
                top = jnp.max(top, axis=0, keepdims=True) * SCALE
                top, v_of, store = finish(u_out, top)
            high, total = None, None
            for c in range(sizes):
                rows = pl.ds(c * 256, 256)
                scores = lax.dot_general(k_of(c), q, (((1,), (1,)), ((), ())), preferred_element_type=F32)
                buf_scores[rows, :] = scores
                best = jnp.max(scores.reshape(32, 8, 256), axis=0)
                high = best if high is None else jnp.maximum(high, best)
                if u_out is not None:
                    weights = jnp.exp2(buf_out[rows, :] * SCALE - top).astype(BF)
                    out = jnp.dot(v_of(c), weights, preferred_element_type=F32)
                    total = out if total is None else total + out
            if u_out is not None:
                store(total, top)
            return high

        def body(i, top):
            u = 2 * i
            top = both(u + 1, u, buf_b, buf_a, top)
            top = both(jnp.minimum(u + 2, units - 1), u + 1, buf_a, buf_b, top)
            for at, event in events:
                pl.when(i == at)(event)
            return top

        lax.fori_loop(0, units // 2, body, both(0, None, buf_a, None, None))

    def audio_scores(u):
        h, tile = u // 5, lax.rem(u, 5)
        cols = pl.ds(pl.multiple_of(h * HD, HD), HD)
        mark = jnp.concatenate(pieces(am, 2 * tile, marks) + pieces(am, 2 * tile + 1, marks), axis=0)
        q = jnp.concatenate(pieces(aq, 2 * tile, cols) + pieces(aq, 2 * tile + 1, cols), axis=0)

        def k_of(c):
            rows = pl.ds(c * 256, 256)
            return jnp.concatenate([vk[rows, cols], ve[rows, :]], axis=1)

        return jnp.concatenate([q, mark], axis=1), k_of

    def audio_finish(u, top):
        h, tile = u // 5, lax.rem(u, 5)
        top = jnp.maximum(top, LOW).astype(BF).astype(F32)

        def v_of(c):
            return vt[h, :, pl.ds(c * 256, 256)]

        def store(out, top):
            where = pl.ds(pl.multiple_of(lax.rem(h, 3) * HD, HD), HD)
            for b in range(2):
                window[h // 3, 2 * tile + b, where, :] = out[:HD, b * HD : (b + 1) * HD].astype(BF)
                tops[h, 2 * tile + b] = jnp.broadcast_to(top[:, b * HD : (b + 1) * HD], (8, HD))
                sums[h, 2 * tile + b] = jnp.broadcast_to(out[HD : HD + 1, b * HD : (b + 1) * HD], (8, HD))

        return top, v_of, store

    empty = jnp.where(lax.broadcasted_iota(jnp.int32, (16, HD), 0) < 3, LOW, 0.0)

    def place(half, b):
        at = jnp.bitwise_and(b - first, 15)
        inside = (at < BLOCKS).astype(F32)
        at = jnp.minimum(at, BLOCKS - 1)
        bz, by = b // 4, lax.rem(b, 4)
        body = window[half, at, :, :].astype(F32)
        part[half, bz, by, pl.ds(0, STAT), :] = (body * inside).astype(BF)
        top = jnp.concatenate([tops[half * 3 + hh, at][0:1] for hh in range(3)], axis=0)
        total = jnp.concatenate([sums[half * 3 + hh, at][0:1] for hh in range(3)], axis=0)
        stats = packed(top, total)
        part[half, bz, by, pl.ds(STAT, 16), :] = (stats * inside + empty * (1.0 - inside)).astype(BF)

    def place_all(half):
        def body(b, carry):
            place(half, b)
            return carry

        lax.fori_loop(0, 16, body, 0)

    def slab(half, where, lo):
        if half == 0:
            return part.at[0, where, pl.ds(lo, 2)]
        return part.at[1, pl.ds(lo, 2), where]

    axes = ((z, zp, zm, z2, to_zp, to_zm), (y, yp, ym, y2, to_yp, to_ym))
    crosses = ((y, yp, ym, y2, to_yp, to_ym, to_y2), (z, zp, zm, z2, to_zp, to_zm, to_z2))

    def reduce1(half):
        _, p, m, two, to_p, to_m = axes[half]
        plan = (
            (slab(half, two, 0), to_p), (slab(half, two, 2), to_m),
            (slab(half, p, 2), to_p), (slab(half, m, 0), to_m),
            (slab(half, p, 0), to_p), (slab(half, m, 2), to_m),
        )
        return [
            remote(ref, got1.at[half, i], r_send.at[half, i], r_recv.at[half, i], dev)
            for i, (ref, dev) in enumerate(plan)
        ]

    def one(half, u):
        if half == 0:
            return part.at[0, z, u]
        return part.at[1, u, y]

    def reduce2(half):
        _, p, m, two, to_p, to_m, to_2 = crosses[half]
        return [
            remote(one(half, u), got2.at[half, i], r_send.at[half, 6 + i], r_recv.at[half, 6 + i], dev)
            for i, (u, dev) in enumerate(((p, to_p), (m, to_m), (two, to_2)))
        ]

    def merged(refs):
        stats = [ref[pl.ds(STAT, 16), :].astype(F32) for ref in refs]
        tops = [x[0:3] for x in stats]
        top = tops[0]
        for x in tops[1:]:
            top = jnp.maximum(top, x)
        factors = [jnp.exp2(x - top) for x in tops]
        total = sum((x[8:11] + x[4:7]) * f for x, f in zip(stats, factors))
        outs = [
            sum(ref[pl.ds(hh * HD, HD), :].astype(F32) * f[hh : hh + 1] for ref, f in zip(refs, factors))
            for hh in range(3)
        ]
        return outs, top, total

    def merge_into(target, sources):
        outs, top, total = merged([target] + sources)
        for hh in range(3):
            target[pl.ds(hh * HD, HD), :] = outs[hh].astype(BF)
        target[pl.ds(STAT, 16), :] = packed(top, total).astype(BF)

    def merge_slab(half, where, lo, slots):
        def body(i, carry):
            target = part.at[0, where, lo + i] if half == 0 else part.at[1, lo + i, where]
            merge_into(target, [got1.at[half, slot, i] for slot in slots])
            return carry

        lax.fori_loop(0, 2, body, 0)

    def reduce_start(half):
        start(reduce1(half)[:4])

    def reduce_pass(half):
        _, p, m, *_ = axes[half]
        copies = reduce1(half)
        copies[0].wait_recv()
        merge_slab(half, p, 0, (0,))
        copies[4].start()
        copies[1].wait_recv()
        merge_slab(half, m, 2, (1,))
        copies[5].start()

    def reduce_cross(half):
        own = axes[half][0]
        arrive(reduce1(half)[2:])
        merge_slab(half, own, 0, (3, 4))
        merge_slab(half, own, 2, (2, 5))
        start(reduce2(half))

    def reduce_end(half):
        own = crosses[half][0]
        arrive(reduce2(half))
        outs, _, total = merged([one(half, own)] + [got2.at[half, i] for i in range(3)])
        scale = 1.0 / total
        for hh in range(3):
            done = (outs[hh] * scale[hh : hh + 1]).T
            ao[:, pl.ds((half * 3 + hh) * HD, HD)] = done.astype(BF)

    def results(half):
        mine = pl.ds(pl.multiple_of(core * 768 + half * 384, 128), 384)
        cols = pl.ds(half * 384, 384)
        return [
            remote(
                ao.at[rows, cols], aout_hbm.at[:, mine], o_send.at[half, i], o_recv.at[half, core], dev
            )
            for i, (rows, dev) in enumerate(((pl.ds(64, 64), result_low), (pl.ds(0, 64), result_high)))
        ]

    def event_first():
        place_all(0)
        reduce_start(0)

    def event_k():
        arrive(gather(1, 2))
        start(gather(1, 3))

    def event_v():
        arrive(gather(2, 2))
        start(gather(2, 3))

    pipeline(30, 4, audio_scores, audio_finish, ((7, event_first), (9, event_k), (12, event_v)))
    place_all(1)
    reduce_start(1)
    reduce_pass(0)
    swap_wait(2)
    arrive(gather(1, 3))
    arrive(gather(2, 3))

    def turn_window(h, carry):
        cols = pl.ds(pl.multiple_of(h * HD, HD), HD)
        for i in range(BLOCKS):
            wt[h, pl.ds(0, HD), pl.ds(i * HD, HD)] = jnp.concatenate(pieces(av, i, cols), axis=0).T
        wt[h, pl.ds(HD, 16), :] = jnp.ones((16, BLOCKS * HD), BF)
        return carry

    lax.fori_loop(0, 6, turn_window, 0)

    def video_scores(u):
        h, tile = u // 4, lax.rem(u, 4)
        cols = pl.ds(pl.multiple_of(h * HD, HD), HD)
        here = pl.ds(pl.multiple_of(tile * 256, 256), 256)

        def k_of(c):
            k = pieces(ak, 2 * c, cols) + pieces(ak, 2 * c + 1, cols)
            mark = pieces(am, 2 * c, marks) + pieces(am, 2 * c + 1, marks)
            return jnp.concatenate([jnp.concatenate(k, axis=0), jnp.concatenate(mark, axis=0)], axis=1)

        return jnp.concatenate([vq[here, cols], ve[here, :]], axis=1), k_of

    def video_finish(u, top):
        h, tile = u // 4, lax.rem(u, 4)
        cols = pl.ds(pl.multiple_of(h * HD, HD), HD)
        here = pl.ds(pl.multiple_of(tile * 256, 256), 256)

        def v_of(c):
            return wt[h, :, pl.ds(c * 256, 256)]

        def store(out, top):
            done = out[:HD] * (1.0 / out[HD : HD + 1])
            vo[here, cols] = done.T.astype(BF)

        return top, v_of, store

    def video_copies(i):
        cols = pl.ds(i * 256, 256)
        mine = pl.ds(pl.multiple_of(core * 768 + i * 256, 128), 256)
        return (
            remote(vo.at[other_rows, cols], vout_hbm.at[:, mine], w_send.at[i], w_recv.at[i], other),
            pltpu.make_async_copy(vo.at[own_rows, cols], vout_hbm.at[:, mine], w_local.at[i]),
        )

    def event_pass():
        reduce_pass(1)

    def event_cross0():
        reduce_cross(0)

    def event_cross1():
        reduce_cross(1)
        start(video_copies(0))

    def event_end0():
        reduce_end(0)
        start(results(0))

    def event_end1():
        reduce_end(1)
        start(results(1))
        start(video_copies(1))

    pipeline(
        24, 5, video_scores, video_finish,
        ((0, event_pass), (2, event_cross0), (4, event_cross1), (6, event_end0), (8, event_end1)),
    )
    start(video_copies(2))

    for t in range(4):
        sent(x_step(t))
        for stage in range(4):
            sent(gather(t, stage))
    for i in range(3):
        swap(i)[0].wait_send()
    swap_marks().wait_send()
    for half in range(2):
        sent(reduce1(half))
        sent(reduce2(half))
        sent(results(half))
        for cc in (0, 1):
            mine = pl.ds(cc * 768 + half * 384, 384)
            remote(
                ao.at[pl.ds(0, 64), pl.ds(half * 384, 384)], aout_hbm.at[:, mine], o_send.at[half, 0],
                o_recv.at[half, cc], result_low,
            ).wait_recv()
    for i in range(3):
        away, here = video_copies(i)
        here.wait()
        away.wait()


def on_device(video_q, video_k, video_v, audio_q, audio_k, audio_v, video_clip, audio_clip):
    anywhere = pl.BlockSpec(memory_space=pl.ANY)
    dma = pltpu.SemaphoreType.DMA
    return pl.pallas_call(
        kernel,
        out_shape=(
            jax.ShapeDtypeStruct(video_q.shape, BF),
            jax.ShapeDtypeStruct(audio_k.shape, BF),
        ),
        in_specs=[
            pl.BlockSpec(memory_space=pltpu.SMEM),
            pl.BlockSpec(memory_space=pltpu.VMEM),
            pl.BlockSpec(memory_space=pltpu.VMEM),
        ]
        + [anywhere] * 6,
        out_specs=(anywhere, anywhere),
        scratch_shapes=[
            pltpu.VMEM((1024, 768), BF),
            pltpu.VMEM((1024, 768), BF),
            pltpu.VMEM((1024, 768), BF),
            pltpu.VMEM((1024, HD), BF),
            pltpu.VMEM((2, 4, 4, 64, 768), BF),
            pltpu.VMEM((2, 4, 4, 64, 768), BF),
            pltpu.VMEM((2, 4, 4, 64, 768), BF),
            pltpu.VMEM((2, 4, 4, 32, HD), BF),
            pltpu.VMEM((2, 4, 4, 64, HD), BF),
            pltpu.VMEM((32, HD), BF),
            pltpu.VMEM((6, HD + 16, 1024), BF),
            pltpu.VMEM((6, HD + 16, BLOCKS * HD), BF),
            pltpu.VMEM((BLOCKS * HD, 256), F32),
            pltpu.VMEM((BLOCKS * HD, 256), F32),
            pltpu.VMEM((6, BLOCKS, 8, HD), F32),
            pltpu.VMEM((6, BLOCKS, 8, HD), F32),
            pltpu.VMEM((2, BLOCKS, STAT, HD), BF),
            pltpu.VMEM((2, 4, 4, ROWS, HD), BF),
            pltpu.VMEM((2, 6, 2, ROWS, HD), BF),
            pltpu.VMEM((2, 3, ROWS, HD), BF),
            pltpu.VMEM((1024, 768), BF),
            pltpu.VMEM((HD, 768), BF),
            dma((4, 2)),
            dma((4, 2)),
            dma((4, 16)),
            dma((4, 16)),
            dma((4,)),
            dma((4,)),
            dma((3,)),
            dma((2, 9)),
            dma((2, 9)),
            dma((2, 2)),
            dma((2, 2)),
            dma((3,)),
            dma((3,)),
            dma((3,)),
        ],
        compiler_params=pltpu.CompilerParams(
            collective_id=0, has_side_effects=True, vmem_limit_bytes=56 * 1024 * 1024
        ),
    )(
        video_clip, video_clip.reshape(4, HD), audio_clip.reshape(1, 64), video_q, video_k, video_v, audio_q, audio_k,
        audio_v,
    )


def solution(mesh):
    spread = P(("grp", "seq"), None)
    return jax.shard_map(
        on_device,
        mesh=mesh,
        in_specs=(spread,) * 6 + (P(("grp", "seq")),) * 2,
        out_specs=(spread, spread),
        check_vma=False,
    )
```

```python
import math

import jax
import jax.numpy as jnp
from jax import lax
from jax.experimental import pallas as pl
from jax.experimental.pallas import tpu as pltpu
from jax.sharding import PartitionSpec as P

MESH = pl.DeviceIdType.MESH
BF = jnp.bfloat16
F32 = jnp.float32
HD = 128
CLIPS = 9
SCALE = math.log2(math.e) / math.sqrt(HD)
FAR = -1048576.0
LOW = -32768.0
BLOCKS = 10
STAT = 3 * HD
ROWS = STAT + 16


def kernel(
    clip_smem, video_clip, audio_clip, vq_hbm, vk_hbm, vv_hbm, aq_hbm, ak_hbm, av_hbm,
    vout_hbm, aout_hbm,
    vq, vk, vv, ve, aq, ak, av, mk, am, mk_own, vt, wt, buf_a, buf_b, tops, sums, window, part, got1, got2, vo, ao,
    x_send, x_recv, g_send, g_recv, v_send, v_recv, v_local, r_send, r_recv, o_send, o_recv, w_send, w_recv, w_local,
):
    g = lax.axis_index("grp")
    s = lax.axis_index("seq")
    core = lax.rem(s, 2)
    chip = s // 2
    z, y = chip // 4, lax.rem(chip, 4)
    zp, zm, z2 = lax.rem(z + 1, 4), lax.rem(z + 3, 4), lax.rem(z + 2, 4)
    yp, ym, y2 = lax.rem(y + 1, 4), lax.rem(y + 3, 4), lax.rem(y + 2, 4)
    gp, gm = lax.rem(g + 1, 4), lax.rem(g + 3, 4)

    def device(grp, zz, yy, cc):
        return (grp, (zz * 4 + yy) * 2 + cc)

    other = device(g, z, y, 1 - core)
    to_yp, to_ym = (device(g, z, b, core) for b in (yp, ym))
    to_zp, to_zm = (device(g, b, y, core) for b in (zp, zm))
    before = lax.rem(chip + 15, 16)
    after = lax.rem(chip + 1, 16)
    result_low = (gp, chip * 2)
    result_high = (gp, before * 2 + 1)

    barrier = pltpu.get_barrier_semaphore()

    def greet(dev):
        pl.semaphore_signal(barrier, inc=1, device_id=dev, device_id_type=MESH)

    for dev in (other, to_yp, to_ym, to_zp, to_zm):
        greet(dev)
    for cc in (0, 1):
        greet(device(gm, z, y, cc))
        greet(device(gp, z, y, cc))
    greet(result_high)

    @pl.when(core == 1)
    def _():
        greet((gm, after * 2))
        greet((gm, after * 2 + 1))

    pl.semaphore_wait(barrier, 10 + 2 * core)

    def remote(src, dst, ssem, rsem, dev):
        return pltpu.make_async_remote_copy(
            src_ref=src, dst_ref=dst, send_sem=ssem, recv_sem=rsem, device_id=dev, device_id_type=MESH
        )

    def columns(half, width):
        return pl.ds(pl.multiple_of(half * width, 128), width)

    tensors = ((aq_hbm, aq), (ak_hbm, ak), (av_hbm, av), (mk_own, mk))

    def x_copies(t, sender):
        src, dst = tensors[t]
        return [
            remote(
                src if t == 3 else src.at[:, pl.ds(cc * 768, 768)], dst.at[sender, z, y], x_send.at[t, cc],
                x_recv.at[t, sender], device(gm, z, y, cc),
            )
            for cc in (0, 1)
        ]

    def x_step(t):
        return x_copies(t, core)

    def x_wait(t):
        for cc in (0, 1):
            x_copies(t, cc)[0].wait_recv()

    def gather(t, stage):
        x = tensors[t][1]
        rows = x.shape[3] // 2
        low, high = pl.ds(0, rows), pl.ds(rows, rows)
        first, last = pl.ds(0, 2), pl.ds(2, 2)
        plan = (
            (x.at[0, z, y], to_yp),
            (x.at[0, z, y], to_ym),
            (x.at[1, z, y], to_zp),
            (x.at[1, z, y], to_zm),
        ), (
            (x.at[0, z, ym, low], to_yp),
            (x.at[0, z, yp, high], to_ym),
            (x.at[1, zm, y, low], to_zp),
            (x.at[1, zp, y, high], to_zm),
        ), (
            (x.at[0, z], to_zp),
            (x.at[0, z], to_zm),
            (x.at[1, :, y], to_yp),
            (x.at[1, :, y], to_ym),
        ), (
            (x.at[0, zm, first], to_zp),
            (x.at[0, zp, last], to_zm),
            (x.at[1, first, ym], to_yp),
            (x.at[1, last, yp], to_ym),
        )
        return [
            remote(ref, ref, g_send.at[t, stage * 4 + i], g_recv.at[t, stage * 4 + i], dev)
            for i, (ref, dev) in enumerate(plan[stage])
        ]

    def start(copies):
        for copy in copies:
            copy.start()

    def arrive(copies):
        for copy in copies:
            copy.wait_recv()

    def sent(copies):
        for copy in copies:
            copy.wait_send()

    video = ((vk_hbm, vk), (vv_hbm, vv), (vq_hbm, vq))
    own_rows = pl.ds(pl.multiple_of(core * 512, 512), 512)
    other_rows = pl.ds(pl.multiple_of((1 - core) * 512, 512), 512)

    def swap(i):
        src, dst = video[i]
        return (
            remote(src.at[:, columns(1 - core, 768)], dst.at[own_rows], v_send.at[i], v_recv.at[i], other),
            pltpu.make_async_copy(src.at[:, columns(core, 768)], dst.at[own_rows], v_local.at[i]),
        )

    def swap_start(i):
        away, here = swap(i)
        away.start()
        here.start()

    def swap_wait(i):
        away, here = swap(i)
        away.wait_recv()
        here.wait()

    def swap_marks():
        return remote(ve.at[own_rows], ve.at[own_rows], v_send.at[3], v_recv.at[3], other)

    start(x_step(0))
    swap_start(0)
    swap_start(1)

    numbers = (audio_clip[...] - gm * CLIPS).astype(F32)
    numbers = jnp.concatenate([numbers, numbers], axis=1)
    mk_own[...] = jnp.broadcast_to(numbers, (32, HD)).astype(BF)
    start(x_step(3))
    clips = lax.broadcasted_iota(jnp.int32, (HD, HD), 0)
    for i in range(4):
        same = video_clip[i : i + 1, :] - g * CLIPS == clips
        at = pl.multiple_of(core * 512 + i * HD, HD)
        ve[pl.ds(at, HD), :] = jnp.where(same, 0.0, FAR).T.astype(BF)
    swap_marks().start()

    x_wait(3)
    start(gather(3, 0))
    x_wait(0)
    start(gather(0, 0))
    start(x_step(1))
    arrive(gather(3, 0))
    start(gather(3, 1))
    arrive(gather(0, 0))
    start(gather(0, 1))
    arrive(gather(3, 1))
    start(gather(3, 2))
    arrive(gather(0, 1))
    start(gather(0, 2))
    x_wait(1)
    start(gather(1, 0))
    start(x_step(2))
    swap_start(2)

    swap_wait(1)

    def turn(h, carry):
        cols = pl.ds(pl.multiple_of(h * HD, HD), HD)
        vt[h, pl.ds(0, HD), :] = vv[:, cols].T
        vt[h, pl.ds(HD, 16), :] = jnp.ones((16, 1024), BF)
        return carry

    lax.fori_loop(0, 6, turn, 0)
    x_wait(2)
    start(gather(2, 0))
    arrive(gather(3, 2))
    start(gather(3, 3))
    arrive(gather(1, 0))
    start(gather(1, 1))
    arrive(gather(2, 0))
    start(gather(2, 1))
    arrive(gather(0, 2))
    start(gather(0, 3))
    arrive(gather(1, 1))
    start(gather(1, 2))
    arrive(gather(2, 1))
    start(gather(2, 2))
    arrive(gather(3, 3))

    lanes = lax.broadcasted_iota(jnp.int32, (HD, HD), 0).astype(F32)

    def expand(i, carry):
        bz, by = i // 4, lax.rem(i, 4)
        for cc in (0, 1):
            numbers = mk[cc, bz, by, pl.ds(0, 16), :].astype(F32)[0:1]
            am[cc, bz, by] = jnp.where(numbers == lanes, 1.0, 0.0).T[0:64].astype(BF)
        return carry

    lax.fori_loop(0, 16, expand, 0)
    swap_wait(0)
    swap_marks().wait_recv()
    arrive(gather(0, 3))

    first = jnp.where(core == 0, clip_smem[0], clip_smem[511] - 1) - g * CLIPS

    def block(i):
        return jnp.bitwise_and(first + i, 15)

    def pieces(ref, i, cols):
        b, a = block(i - 1), block(i)
        return [ref[1, b // 4, jnp.bitwise_and(b, 3), :, cols], ref[0, a // 4, jnp.bitwise_and(a, 3), :, cols]]

    marks = pl.ds(0, HD)

    def packed(top, total):
        high = total.astype(BF).astype(F32)
        gap = jnp.zeros((1, HD), F32)
        return jnp.concatenate([top, gap, total - high, gap, high, jnp.zeros((5, HD), F32)], axis=0)

    def pipeline(units, sizes, scores_of, finish, events):
        def both(u_scores, u_out, buf_scores, buf_out, top):
            q, k_of = scores_of(u_scores)
            if u_out is not None:
                top = jnp.max(top, axis=0, keepdims=True) * SCALE
                top, v_of, store = finish(u_out, top)
            high, total = None, None
            for c in range(sizes):
                rows = pl.ds(c * 256, 256)
                scores = jnp.dot(k_of(c), q, preferred_element_type=F32)
                buf_scores[rows, :] = scores
                best = jnp.max(scores.reshape(32, 8, 256), axis=0)
                high = best if high is None else jnp.maximum(high, best)
                if u_out is not None:
                    weights = jnp.exp2(buf_out[rows, :] * SCALE - top).astype(BF)
                    out = jnp.dot(v_of(c), weights, preferred_element_type=F32)
                    total = out if total is None else total + out
            if u_out is not None:
                store(total, top)
            return high

        def body(i, top):
            u = 2 * i
            top = both(u + 1, u, buf_b, buf_a, top)
            top = both(jnp.minimum(u + 2, units - 1), u + 1, buf_a, buf_b, top)
            for at, event in events:
                pl.when(i == at)(event)
            return top

        lax.fori_loop(0, units // 2, body, both(0, None, buf_a, None, None))

    def audio_scores(u):
        h, tile = u // 5, lax.rem(u, 5)
        cols = pl.ds(pl.multiple_of(h * HD, HD), HD)
        mark = jnp.concatenate(pieces(am, 2 * tile, marks) + pieces(am, 2 * tile + 1, marks), axis=0)
        q = jnp.concatenate(pieces(aq, 2 * tile, cols) + pieces(aq, 2 * tile + 1, cols), axis=0)

        def k_of(c):
            rows = pl.ds(c * 256, 256)
            return jnp.concatenate([vk[rows, cols], ve[rows, :]], axis=1)

        return jnp.concatenate([q, mark], axis=1).T, k_of

    def audio_finish(u, top):
        h, tile = u // 5, lax.rem(u, 5)
        top = jnp.maximum(top, LOW).astype(BF).astype(F32)

        def v_of(c):
            return vt[h, :, pl.ds(c * 256, 256)]

        def store(out, top):
            where = pl.ds(pl.multiple_of(lax.rem(h, 3) * HD, HD), HD)
            for b in range(2):
                window[h // 3, 2 * tile + b, where, :] = out[:HD, b * HD : (b + 1) * HD].astype(BF)
                tops[h, 2 * tile + b] = jnp.broadcast_to(top[:, b * HD : (b + 1) * HD], (8, HD))
                sums[h, 2 * tile + b] = jnp.broadcast_to(out[HD : HD + 1, b * HD : (b + 1) * HD], (8, HD))

        return top, v_of, store

    empty = jnp.where(lax.broadcasted_iota(jnp.int32, (16, HD), 0) < 3, LOW, 0.0)

    def place(half, b):
        at = jnp.bitwise_and(b - first, 15)
        inside = (at < BLOCKS).astype(F32)
        at = jnp.minimum(at, BLOCKS - 1)
        bz, by = b // 4, lax.rem(b, 4)
        body = window[half, at, :, :].astype(F32)
        part[half, bz, by, pl.ds(0, STAT), :] = (body * inside).astype(BF)
        top = jnp.concatenate([tops[half * 3 + hh, at][0:1] for hh in range(3)], axis=0)
        total = jnp.concatenate([sums[half * 3 + hh, at][0:1] for hh in range(3)], axis=0)
        stats = packed(top, total)
        part[half, bz, by, pl.ds(STAT, 16), :] = (stats * inside + empty * (1.0 - inside)).astype(BF)

    def place_all(half):
        def body(b, carry):
            place(half, b)
            return carry

        lax.fori_loop(0, 16, body, 0)

    def slab(half, where, lo):
        if half == 0:
            return part.at[0, where, pl.ds(lo, 2)]
        return part.at[1, pl.ds(lo, 2), where]

    axes = ((z, zp, zm, z2, to_zp, to_zm), (y, yp, ym, y2, to_yp, to_ym))
    turn_by = 1 + 2 * core

    def cross(at, two):
        p, m = lax.rem(at + turn_by, 4), lax.rem(at + 4 - turn_by, 4)
        return at, p, m, two

    crosses = (cross(y, y2), cross(z, z2))

    def reduce1(half):
        _, p, m, two, to_p, to_m = axes[half]
        plan = (
            (slab(half, two, 0), to_p), (slab(half, two, 2), to_m),
            (slab(half, p, 2), to_p), (slab(half, m, 0), to_m),
            (slab(half, p, 0), to_p), (slab(half, m, 2), to_m),
        )
        return [
            remote(ref, got1.at[half, i], r_send.at[half, i], r_recv.at[half, i], dev)
            for i, (ref, dev) in enumerate(plan)
        ]

    def one(half, u):
        if half == 0:
            return part.at[0, z, u]
        return part.at[1, u, y]

    def reduce2(half):
        _, p, m, two = crosses[half]
        to_p, to_m = (device(g, z, u, core) if half == 0 else device(g, u, y, core) for u in (p, m))
        return [
            remote(one(half, u), got2.at[half, i], r_send.at[half, 6 + i], r_recv.at[half, 6 + i], dev)
            for i, (u, dev) in enumerate(((two, to_p), (m, to_m), (p, to_p)))
        ]

    def merged(refs):
        stats = [ref[pl.ds(STAT, 16), :].astype(F32) for ref in refs]
        tops = [x[0:3] for x in stats]
        top = tops[0]
        for x in tops[1:]:
            top = jnp.maximum(top, x)
        factors = [jnp.exp2(x - top) for x in tops]
        total = sum((x[8:11] + x[4:7]) * f for x, f in zip(stats, factors))
        outs = [
            sum(ref[pl.ds(hh * HD, HD), :].astype(F32) * f[hh : hh + 1] for ref, f in zip(refs, factors))
            for hh in range(3)
        ]
        return outs, top, total

    def merge_into(target, sources):
        outs, top, total = merged([target] + sources)
        for hh in range(3):
            target[pl.ds(hh * HD, HD), :] = outs[hh].astype(BF)
        target[pl.ds(STAT, 16), :] = packed(top, total).astype(BF)

    def merge_slab(half, where, lo, slots):
        def body(i, carry):
            target = part.at[0, where, lo + i] if half == 0 else part.at[1, lo + i, where]
            merge_into(target, [got1.at[half, slot, i] for slot in slots])
            return carry

        lax.fori_loop(0, 2, body, 0)

    def reduce_start(half):
        start(reduce1(half)[:4])

    def reduce_pass(half):
        _, p, m, *_ = axes[half]
        copies = reduce1(half)
        copies[0].wait_recv()
        merge_slab(half, p, 0, (0,))
        copies[4].start()
        copies[1].wait_recv()
        merge_slab(half, m, 2, (1,))
        copies[5].start()

    def reduce_cross(half):
        own = axes[half][0]
        arrive(reduce1(half)[2:])
        merge_slab(half, own, 0, (3, 4))
        merge_slab(half, own, 2, (2, 5))
        start(reduce2(half)[:2])

    def reduce_cross_pass(half):
        copies = reduce2(half)
        copies[0].wait_recv()
        merge_into(one(half, crosses[half][1]), [got2.at[half, 0]])
        copies[2].start()

    def reduce_end(half):
        own = crosses[half][0]
        arrive(reduce2(half)[1:])
        outs, _, total = merged([one(half, own)] + [got2.at[half, i] for i in (1, 2)])
        scale = 1.0 / total
        for hh in range(3):
            done = (outs[hh] * scale[hh : hh + 1]).T
            ao[:, pl.ds((half * 3 + hh) * HD, HD)] = done.astype(BF)

    def results(half):
        mine = pl.ds(pl.multiple_of(core * 768 + half * 384, 128), 384)
        cols = pl.ds(half * 384, 384)
        return [
            remote(
                ao.at[rows, cols], aout_hbm.at[:, mine], o_send.at[half, i], o_recv.at[half, core], dev
            )
            for i, (rows, dev) in enumerate(((pl.ds(64, 64), result_low), (pl.ds(0, 64), result_high)))
        ]

    def event_first():
        place_all(0)
        reduce_start(0)

    def event_k():
        arrive(gather(1, 2))
        start(gather(1, 3))

    def event_v():
        arrive(gather(2, 2))
        start(gather(2, 3))

    pipeline(30, 4, audio_scores, audio_finish, ((7, event_first), (9, event_k), (12, event_v)))
    place_all(1)
    reduce_start(1)
    reduce_pass(0)
    swap_wait(2)
    arrive(gather(1, 3))
    arrive(gather(2, 3))

    def turn_window(h, carry):
        cols = pl.ds(pl.multiple_of(h * HD, HD), HD)
        for i in range(BLOCKS):
            wt[h, pl.ds(0, HD), pl.ds(i * HD, HD)] = jnp.concatenate(pieces(av, i, cols), axis=0).T
        wt[h, pl.ds(HD, 16), :] = jnp.ones((16, BLOCKS * HD), BF)
        return carry

    lax.fori_loop(0, 6, turn_window, 0)

    def video_scores(u):
        h, tile = u // 4, lax.rem(u, 4)
        cols = pl.ds(pl.multiple_of(h * HD, HD), HD)
        here = pl.ds(pl.multiple_of(tile * 256, 256), 256)

        def k_of(c):
            k = pieces(ak, 2 * c, cols) + pieces(ak, 2 * c + 1, cols)
            mark = pieces(am, 2 * c, marks) + pieces(am, 2 * c + 1, marks)
            return jnp.concatenate([jnp.concatenate(k, axis=0), jnp.concatenate(mark, axis=0)], axis=1)

        return jnp.concatenate([vq[here, cols], ve[here, :]], axis=1).T, k_of

    def video_finish(u, top):
        h, tile = u // 4, lax.rem(u, 4)
        cols = pl.ds(pl.multiple_of(h * HD, HD), HD)
        here = pl.ds(pl.multiple_of(tile * 256, 256), 256)

        def v_of(c):
            return wt[h, :, pl.ds(c * 256, 256)]

        def store(out, top):
            done = out[:HD] * (1.0 / out[HD : HD + 1])
            vo[here, cols] = done.T.astype(BF)

        return top, v_of, store

    def video_copies(i):
        cols = pl.ds(i * 256, 256)
        mine = pl.ds(pl.multiple_of(core * 768 + i * 256, 128), 256)
        return (
            remote(vo.at[other_rows, cols], vout_hbm.at[:, mine], w_send.at[i], w_recv.at[i], other),
            pltpu.make_async_copy(vo.at[own_rows, cols], vout_hbm.at[:, mine], w_local.at[i]),
        )

    def event_pass():
        reduce_pass(1)

    def event_cross0():
        reduce_cross(0)

    def event_cross1():
        reduce_cross_pass(0)
        reduce_cross(1)
        start(video_copies(0))

    def event_end0():
        reduce_end(0)
        start(results(0))
        reduce_cross_pass(1)

    def event_end1():
        reduce_end(1)
        start(results(1))
        start(video_copies(1))

    pipeline(
        24, 5, video_scores, video_finish,
        ((0, event_pass), (2, event_cross0), (4, event_cross1), (6, event_end0), (8, event_end1)),
    )
    start(video_copies(2))

    for t in range(4):
        sent(x_step(t))
        for stage in range(4):
            sent(gather(t, stage))
    for i in range(3):
        swap(i)[0].wait_send()
    swap_marks().wait_send()
    for half in range(2):
        sent(reduce1(half))
        sent(reduce2(half))
        sent(results(half))
        for cc in (0, 1):
            mine = pl.ds(cc * 768 + half * 384, 384)
            remote(
                ao.at[pl.ds(0, 64), pl.ds(half * 384, 384)], aout_hbm.at[:, mine], o_send.at[half, 0],
                o_recv.at[half, cc], result_low,
            ).wait_recv()
    for i in range(3):
        away, here = video_copies(i)
        here.wait()
        away.wait()


def on_device(video_q, video_k, video_v, audio_q, audio_k, audio_v, video_clip, audio_clip):
    anywhere = pl.BlockSpec(memory_space=pl.ANY)
    dma = pltpu.SemaphoreType.DMA
    return pl.pallas_call(
        kernel,
        out_shape=(
            jax.ShapeDtypeStruct(video_q.shape, BF),
            jax.ShapeDtypeStruct(audio_k.shape, BF),
        ),
        in_specs=[
            pl.BlockSpec(memory_space=pltpu.SMEM),
            pl.BlockSpec(memory_space=pltpu.VMEM),
            pl.BlockSpec(memory_space=pltpu.VMEM),
        ]
        + [anywhere] * 6,
        out_specs=(anywhere, anywhere),
        scratch_shapes=[
            pltpu.VMEM((1024, 768), BF),
            pltpu.VMEM((1024, 768), BF),
            pltpu.VMEM((1024, 768), BF),
            pltpu.VMEM((1024, HD), BF),
            pltpu.VMEM((2, 4, 4, 64, 768), BF),
            pltpu.VMEM((2, 4, 4, 64, 768), BF),
            pltpu.VMEM((2, 4, 4, 64, 768), BF),
            pltpu.VMEM((2, 4, 4, 32, HD), BF),
            pltpu.VMEM((2, 4, 4, 64, HD), BF),
            pltpu.VMEM((32, HD), BF),
            pltpu.VMEM((6, HD + 16, 1024), BF),
            pltpu.VMEM((6, HD + 16, BLOCKS * HD), BF),
            pltpu.VMEM((BLOCKS * HD, 256), F32),
            pltpu.VMEM((BLOCKS * HD, 256), F32),
            pltpu.VMEM((6, BLOCKS, 8, HD), F32),
            pltpu.VMEM((6, BLOCKS, 8, HD), F32),
            pltpu.VMEM((2, BLOCKS, STAT, HD), BF),
            pltpu.VMEM((2, 4, 4, ROWS, HD), BF),
            pltpu.VMEM((2, 6, 2, ROWS, HD), BF),
            pltpu.VMEM((2, 3, ROWS, HD), BF),
            pltpu.VMEM((1024, 768), BF),
            pltpu.VMEM((HD, 768), BF),
            dma((4, 2)),
            dma((4, 2)),
            dma((4, 16)),
            dma((4, 16)),
            dma((4,)),
            dma((4,)),
            dma((3,)),
            dma((2, 9)),
            dma((2, 9)),
            dma((2, 2)),
            dma((2, 2)),
            dma((3,)),
            dma((3,)),
            dma((3,)),
        ],
        compiler_params=pltpu.CompilerParams(
            collective_id=0, has_side_effects=True, vmem_limit_bytes=56 * 1024 * 1024
        ),
    )(
        video_clip, video_clip.reshape(4, HD), audio_clip.reshape(1, 64), video_q, video_k, video_v, audio_q, audio_k,
        audio_v,
    )


def solution(mesh):
    spread = P(("grp", "seq"), None)
    return jax.shard_map(
        on_device,
        mesh=mesh,
        in_specs=(spread,) * 6 + (P(("grp", "seq")),) * 2,
        out_specs=(spread, spread),
        check_vma=False,
    )
```

```python
import math

import jax
import jax.numpy as jnp
from jax import lax
from jax.experimental import pallas as pl
from jax.experimental.pallas import tpu as pltpu
from jax.sharding import PartitionSpec as P

MESH = pl.DeviceIdType.MESH
BF = jnp.bfloat16
F32 = jnp.float32
HD = 128
CLIPS = 9
SCALE = math.log2(math.e) / math.sqrt(HD)
FAR = -1048576.0
LOW = -32768.0
BLOCKS = 10
STAT = 3 * HD
ROWS = STAT + 16


ORDER = (
    "1Q", "2Q", "3Q", "vqs", "xKs", "xVs", "1K", "1V", "4Q", "ex", "2K", "vt", "2V", "3K",
    "A", 2, "3V", 8, "4K", 12, "p0", 13, "r1_0",
    "B", "p1", "r1_1",
    "X", 3, "4V", 5, "r2_0", "r2_1",
    "T", "tw", "ca_0", "ca_1",
    "Y", 1, "cb_0", "cb_1", "w0", 2, "o_0", 3, "o_1", "w1", 5, "w2",
)


def kernel(
    clip_smem, video_clip, audio_clip, vq_hbm, vk_hbm, vv_hbm, aq_hbm, ak_hbm, av_hbm,
    vout_hbm, aout_hbm,
    vq, vk, vv, ve, aq, ak, av, mk, am, mk_own, vt, buf_c, buf_d, buf_a, buf_b, wb, tops, sums, window, part, got1, got2, vo, ao,
    x_send, x_recv, g_send, g_recv, v_send, v_recv, v_local, r_send, r_recv, o_send, o_recv, w_send, w_recv, w_local,
):
    g = lax.axis_index("grp")
    s = lax.axis_index("seq")
    core = lax.rem(s, 2)
    chip = s // 2
    z, y = chip // 4, lax.rem(chip, 4)
    zp, zm, z2 = lax.rem(z + 1, 4), lax.rem(z + 3, 4), lax.rem(z + 2, 4)
    yp, ym, y2 = lax.rem(y + 1, 4), lax.rem(y + 3, 4), lax.rem(y + 2, 4)
    gp, gm = lax.rem(g + 1, 4), lax.rem(g + 3, 4)

    def device(grp, zz, yy, cc):
        return (grp, (zz * 4 + yy) * 2 + cc)

    other = device(g, z, y, 1 - core)
    to_yp, to_ym = (device(g, z, b, core) for b in (yp, ym))
    to_zp, to_zm = (device(g, b, y, core) for b in (zp, zm))
    before = lax.rem(chip + 15, 16)
    after = lax.rem(chip + 1, 16)
    result_low = (gp, chip * 2)
    result_high = (gp, before * 2 + 1)

    barrier = pltpu.get_barrier_semaphore()

    def greet(dev):
        pl.semaphore_signal(barrier, inc=1, device_id=dev, device_id_type=MESH)

    for dev in (other, to_yp, to_ym, to_zp, to_zm):
        greet(dev)
    for cc in (0, 1):
        greet(device(gm, z, y, cc))
        greet(device(gp, z, y, cc))
    greet(result_high)

    @pl.when(core == 1)
    def _():
        greet((gm, after * 2))
        greet((gm, after * 2 + 1))

    pl.semaphore_wait(barrier, 10 + 2 * core)

    def remote(src, dst, ssem, rsem, dev):
        return pltpu.make_async_remote_copy(
            src_ref=src, dst_ref=dst, send_sem=ssem, recv_sem=rsem, device_id=dev, device_id_type=MESH
        )

    def columns(half, width):
        return pl.ds(pl.multiple_of(half * width, 128), width)

    tensors = ((aq_hbm, aq), (ak_hbm, ak), (av_hbm, av), (mk_own, mk))

    def x_copies(t, sender):
        src, dst = tensors[t]
        return [
            remote(
                src if t == 3 else src.at[:, pl.ds(cc * 768, 768)], dst.at[sender, z, y], x_send.at[t, cc],
                x_recv.at[t, sender], device(gm, z, y, cc),
            )
            for cc in (0, 1)
        ]

    def x_step(t):
        return x_copies(t, core)

    here_already = set()

    def x_wait(t):
        if t in here_already:
            return
        here_already.add(t)
        for cc in (0, 1):
            x_copies(t, cc)[0].wait_recv()

    def gather(t, stage):
        x = tensors[t][1]
        rows = x.shape[3] // 2
        low, high = pl.ds(0, rows), pl.ds(rows, rows)
        first, last = pl.ds(0, 2), pl.ds(2, 2)
        plan = (
            (x.at[0, z, y], to_yp),
            (x.at[0, z, y], to_ym),
            (x.at[1, z, y], to_zp),
            (x.at[1, z, y], to_zm),
        ), (
            (x.at[0, z, ym, low], to_yp),
            (x.at[0, z, yp, high], to_ym),
            (x.at[1, zm, y, low], to_zp),
            (x.at[1, zp, y, high], to_zm),
        ), (
            (x.at[0, z], to_zp),
            (x.at[0, z], to_zm),
            (x.at[1, :, y], to_yp),
            (x.at[1, :, y], to_ym),
        ), (
            (x.at[0, zm, first], to_zp),
            (x.at[0, zp, last], to_zm),
            (x.at[1, first, ym], to_yp),
            (x.at[1, last, yp], to_ym),
        )
        return [
            remote(ref, ref, g_send.at[t, stage * 4 + i], g_recv.at[t, stage * 4 + i], dev)
            for i, (ref, dev) in enumerate(plan[stage])
        ]

    def start(copies):
        for copy in copies:
            copy.start()

    def arrive(copies):
        for copy in copies:
            copy.wait_recv()

    def sent(copies):
        for copy in copies:
            copy.wait_send()

    video = ((vk_hbm, vk), (vv_hbm, vv), (vq_hbm, vq))
    own_rows = pl.ds(pl.multiple_of(core * 512, 512), 512)
    other_rows = pl.ds(pl.multiple_of((1 - core) * 512, 512), 512)

    def swap(i):
        src, dst = video[i]
        return (
            remote(src.at[:, columns(1 - core, 768)], dst.at[own_rows], v_send.at[i], v_recv.at[i], other),
            pltpu.make_async_copy(src.at[:, columns(core, 768)], dst.at[own_rows], v_local.at[i]),
        )

    def swap_start(i):
        away, here = swap(i)
        away.start()
        here.start()

    def swap_wait(i):
        away, here = swap(i)
        away.wait_recv()
        here.wait()

    def swap_marks():
        return remote(ve.at[own_rows], ve.at[own_rows], v_send.at[3], v_recv.at[3], other)

    start(x_step(0))
    swap_start(0)
    swap_start(1)

    numbers = (audio_clip[...] - gm * CLIPS).astype(F32)
    numbers = jnp.concatenate([numbers, numbers], axis=1)
    mk_own[...] = jnp.broadcast_to(numbers, (32, HD)).astype(BF)
    start(x_step(3))
    clips = lax.broadcasted_iota(jnp.int32, (HD, HD), 0)
    for i in range(4):
        same = video_clip[i : i + 1, :] - g * CLIPS == clips
        at = pl.multiple_of(core * 512 + i * HD, HD)
        ve[pl.ds(at, HD), :] = jnp.where(same, 0.0, FAR).T.astype(BF)
    swap_marks().start()

    def turn(h, carry):
        cols = pl.ds(pl.multiple_of(h * HD, HD), HD)
        vt[h, pl.ds(0, HD), :] = vv[:, cols].T
        vt[h, pl.ds(HD, 16), :] = jnp.ones((16, 1024), BF)
        return carry

    lanes = clips.astype(F32)

    def expand(i, carry):
        bz, by = i // 4, lax.rem(i, 4)
        for cc in (0, 1):
            numbers = mk[cc, bz, by, pl.ds(0, 16), :].astype(F32)[0:1]
            am[cc, bz, by] = jnp.where(numbers == lanes, 1.0, 0.0).T[0:64].astype(BF)
        return carry

    first = jnp.where(core == 0, clip_smem[0], clip_smem[511] - 1) - g * CLIPS

    def block(i):
        return jnp.bitwise_and(first + i, 15)

    def pieces(ref, i, cols):
        b, a = block(i - 1), block(i)
        return [ref[1, b // 4, jnp.bitwise_and(b, 3), :, cols], ref[0, a // 4, jnp.bitwise_and(a, 3), :, cols]]

    marks = pl.ds(0, HD)

    def packed(top, total):
        high = total.astype(BF).astype(F32)
        gap = jnp.zeros((1, HD), F32)
        return jnp.concatenate([top, gap, total - high, gap, high, jnp.zeros((5, HD), F32)], axis=0)

    def run_events(i, events):
        for at in sorted({at for at, _ in events}):

            @pl.when(i == at)
            def _():
                for where, event in events:
                    if where == at:
                        event()

    def pipeline(units, sizes, scores_of, finish, events):
        def both(u_scores, u_out, buf_scores, buf_out, top):
            q, k_of = scores_of(u_scores)
            store = None
            if u_out is not None:
                top = jnp.max(top, axis=0, keepdims=True) * SCALE
                top, use, store = finish(u_out, top)
            high, total = None, None
            for c in range(sizes):
                rows = pl.ds(c * 256, 256)
                scores = lax.dot_general(k_of(c), q, (((1,), (1,)), ((), ())), preferred_element_type=F32)
                buf_scores[rows, :] = scores
                best = jnp.max(scores.reshape(32, 8, 256), axis=0)
                high = best if high is None else jnp.maximum(high, best)
                if u_out is not None:
                    weights = jnp.exp2(buf_out[rows, :] * SCALE - top).astype(BF)
                    out = use(c, weights)
                    if store is not None:
                        total = out if total is None else total + out
            if store is not None:
                store(total, top)
            return high

        def body(i, top):
            u = 2 * i
            top = both(u + 1, u, buf_d, buf_c, top)
            top = both(jnp.minimum(u + 2, units - 1), u + 1, buf_c, buf_d, top)
            run_events(i, events)
            return top

        lax.fori_loop(0, units // 2, body, both(0, None, buf_c, None, None))

    def audio_scores(u):
        h, tile = u // 5, lax.rem(u, 5)
        cols = pl.ds(pl.multiple_of(h * HD, HD), HD)
        mark = jnp.concatenate(pieces(am, 2 * tile, marks) + pieces(am, 2 * tile + 1, marks), axis=0)
        q = jnp.concatenate(pieces(aq, 2 * tile, cols) + pieces(aq, 2 * tile + 1, cols), axis=0)

        def k_of(c):
            rows = pl.ds(c * 256, 256)
            return jnp.concatenate([vk[rows, cols], ve[rows, :]], axis=1)

        return jnp.concatenate([q, mark], axis=1), k_of

    def audio_finish(u, top):
        h, tile = u // 5, lax.rem(u, 5)
        top = jnp.maximum(top, LOW).astype(BF).astype(F32)

        def use(c, weights):
            return jnp.dot(vt[h, :, pl.ds(c * 256, 256)], weights, preferred_element_type=F32)

        def store(out, top):
            where = pl.ds(pl.multiple_of(lax.rem(h, 3) * HD, HD), HD)
            for b in range(2):
                window[h // 3, 2 * tile + b, where, :] = out[:HD, b * HD : (b + 1) * HD].astype(BF)
                tops[h, 2 * tile + b] = jnp.broadcast_to(top[:, b * HD : (b + 1) * HD], (8, HD))
                sums[h, 2 * tile + b] = jnp.broadcast_to(out[HD : HD + 1, b * HD : (b + 1) * HD], (8, HD))

        return top, use, store

    empty = jnp.where(lax.broadcasted_iota(jnp.int32, (16, HD), 0) < 3, LOW, 0.0)

    def place_block(half, b):
        at = jnp.bitwise_and(b - first, 15)
        inside = (at < BLOCKS).astype(F32)
        at = jnp.minimum(at, BLOCKS - 1)
        bz, by = b // 4, lax.rem(b, 4)
        body = window[half, at, :, :].astype(F32)
        part[half, bz, by, pl.ds(0, STAT), :] = (body * inside).astype(BF)
        top = jnp.concatenate([tops[half * 3 + hh, at][0:1] for hh in range(3)], axis=0)
        total = jnp.concatenate([sums[half * 3 + hh, at][0:1] for hh in range(3)], axis=0)
        stats = packed(top, total)
        part[half, bz, by, pl.ds(STAT, 16), :] = (stats * inside + empty * (1.0 - inside)).astype(BF)

    def place_all(half):
        def body(b, carry):
            place_block(half, b)
            return carry

        lax.fori_loop(0, 16, body, 0)

    def slab(half, where, lo):
        if half == 0:
            return part.at[0, where, pl.ds(lo, 2)]
        return part.at[1, pl.ds(lo, 2), where]

    axes = ((z, zp, zm, z2, to_zp, to_zm), (y, yp, ym, y2, to_yp, to_ym))
    turn_by = 1 + 2 * core

    def cross(at, two):
        p, m = lax.rem(at + turn_by, 4), lax.rem(at + 4 - turn_by, 4)
        return at, p, m, two

    crosses = (cross(y, y2), cross(z, z2))

    def reduce1(half):
        _, p, m, two, to_p, to_m = axes[half]
        plan = (
            (slab(half, two, 0), to_p), (slab(half, two, 2), to_m),
            (slab(half, p, 2), to_p), (slab(half, m, 0), to_m),
            (slab(half, p, 0), to_p), (slab(half, m, 2), to_m),
        )
        return [
            remote(ref, got1.at[half, i], r_send.at[half, i], r_recv.at[half, i], dev)
            for i, (ref, dev) in enumerate(plan)
        ]

    def one(half, u):
        if half == 0:
            return part.at[0, z, u]
        return part.at[1, u, y]

    def reduce2(half):
        _, p, m, two = crosses[half]
        to_p, to_m = (device(g, z, u, core) if half == 0 else device(g, u, y, core) for u in (p, m))
        return [
            remote(one(half, u), got2.at[half, i], r_send.at[half, 6 + i], r_recv.at[half, 6 + i], dev)
            for i, (u, dev) in enumerate(((two, to_p), (m, to_m), (p, to_p)))
        ]

    def merged(refs):
        stats = [ref[pl.ds(STAT, 16), :].astype(F32) for ref in refs]
        tops = [x[0:3] for x in stats]
        top = tops[0]
        for x in tops[1:]:
            top = jnp.maximum(top, x)
        factors = [jnp.exp2(x - top) for x in tops]
        total = sum((x[8:11] + x[4:7]) * f for x, f in zip(stats, factors))
        outs = [
            sum(ref[pl.ds(hh * HD, HD), :].astype(F32) * f[hh : hh + 1] for ref, f in zip(refs, factors))
            for hh in range(3)
        ]
        return outs, top, total

    def merge_into(target, sources):
        outs, top, total = merged([target] + sources)
        for hh in range(3):
            target[pl.ds(hh * HD, HD), :] = outs[hh].astype(BF)
        target[pl.ds(STAT, 16), :] = packed(top, total).astype(BF)

    def merge_slab(half, where, lo, slots):
        def body(i, carry):
            target = part.at[0, where, lo + i] if half == 0 else part.at[1, lo + i, where]
            merge_into(target, [got1.at[half, slot, i] for slot in slots])
            return carry

        lax.fori_loop(0, 2, body, 0)

    def reduce_start(half):
        start(reduce1(half)[:4])

    def reduce_pass(half):
        _, p, m, *_ = axes[half]
        copies = reduce1(half)
        copies[0].wait_recv()
        merge_slab(half, p, 0, (0,))
        copies[4].start()
        copies[1].wait_recv()
        merge_slab(half, m, 2, (1,))
        copies[5].start()

    def reduce_cross(half):
        own = axes[half][0]
        arrive(reduce1(half)[2:])
        merge_slab(half, own, 0, (3, 4))
        merge_slab(half, own, 2, (2, 5))
        start(reduce2(half)[:2])

    def reduce_cross_pass(half):
        copies = reduce2(half)
        copies[0].wait_recv()
        merge_into(one(half, crosses[half][1]), [got2.at[half, 0]])
        copies[2].start()

    def reduce_end(half):
        own = crosses[half][0]
        arrive(reduce2(half)[1:])
        outs, _, total = merged([one(half, own)] + [got2.at[half, i] for i in (1, 2)])
        scale = 1.0 / total
        for hh in range(3):
            done = (outs[hh] * scale[hh : hh + 1]).T
            ao[:, pl.ds((half * 3 + hh) * HD, HD)] = done.astype(BF)

    def results(half):
        mine = pl.ds(pl.multiple_of(core * 768 + half * 384, 128), 384)
        cols = pl.ds(half * 384, 384)
        return [
            remote(
                ao.at[rows, cols], aout_hbm.at[:, mine], o_send.at[half, i], o_recv.at[half, core], dev
            )
            for i, (rows, dev) in enumerate(((pl.ds(64, 64), result_low), (pl.ds(0, 64), result_high)))
        ]

    def rows_of(ref, i, cols):
        return jnp.concatenate(pieces(ref, 2 * i, cols) + pieces(ref, 2 * i + 1, cols), axis=0)

    def video_unit(u):
        cols = pl.ds(pl.multiple_of(u // 2 * HD, HD), HD)
        return cols, pl.ds(pl.multiple_of(lax.rem(u, 2) * 512, 512), 512)

    def video_both(u_scores, u_out, buf_scores, buf_out):
        cols, here = video_unit(u_scores)
        q = jnp.concatenate([vq[here, cols], ve[here, :]], axis=1)
        row = 0
        for c in range(5):
            k = jnp.concatenate([rows_of(ak, c, cols), rows_of(am, c, marks)], axis=1)
            buf_scores[:, c * 256 : (c + 1) * 256] = lax.dot_general(
                q, k, (((1,), (1,)), ((), ())), preferred_element_type=F32
            )
            if u_out is not None:
                for _ in range(7 if c < 2 else 6):
                    scores = buf_out[row : row + 16, :]
                    top = jnp.max(scores, axis=1, keepdims=True) * SCALE
                    wb[u_out, row : row + 16, :] = jnp.exp2(scores * SCALE - top).astype(BF)
                    row += 16

    def video_weights(events):
        def body(i, carry):
            u = 2 * i
            video_both(u + 1, u, buf_b, buf_a)
            video_both(jnp.minimum(u + 2, 11), u + 1, buf_a, buf_b)
            run_events(i, events)
            return carry

        video_both(0, None, buf_a, None)
        lax.fori_loop(0, 6, body, 0)

    def video_values(events):
        def body(i, carry):
            cols, _ = video_unit(2 * i)
            v = jnp.concatenate([rows_of(av, c, cols) for c in range(5)], axis=0)
            v = jnp.concatenate([v, jnp.ones((BLOCKS * HD, HD), BF)], axis=1)
            for j in range(2):
                out = jnp.dot(wb[2 * i + j], v, preferred_element_type=F32)
                vo[pl.ds(j * 512, 512), cols] = (out[:, :HD] / out[:, HD:]).astype(BF)
            run_events(i, events)
            return carry

        lax.fori_loop(0, 6, body, 0)

    def video_copies(i):
        cols = pl.ds(i * 256, 256)
        mine = pl.ds(pl.multiple_of(core * 768 + i * 256, 128), 256)
        return (
            remote(vo.at[other_rows, cols], vout_hbm.at[:, mine], w_send.at[i], w_recv.at[i], other),
            pltpu.make_async_copy(vo.at[own_rows, cols], vout_hbm.at[:, mine], w_local.at[i]),
        )

    def take(t, stage):
        for tensor in (3, 0) if t == 0 else (t,):
            if stage == 0:
                x_wait(tensor)
            else:
                arrive(gather(tensor, stage - 1))
            start(gather(tensor, stage))

    def x_next(t):
        x_wait(t - 1)
        start(x_step(t))

    def turn_values():
        swap_wait(1)
        lax.fori_loop(0, 6, turn, 0)

    def make_marks():
        arrive(gather(3, 3))
        lax.fori_loop(0, 16, expand, 0)

    def ready_audio():
        swap_wait(0)
        swap_marks().wait_recv()
        arrive(gather(0, 3))

    def turn_window_all():
        arrive(gather(2, 3))

    def ready_video():
        swap_wait(2)
        arrive(gather(1, 3))

    def finish_half(half):
        reduce_end(half)
        start(results(half))

    steps = {
        "xKs": lambda: x_next(1), "xVs": lambda: x_next(2), "vqs": lambda: swap_start(2),
        "vt": turn_values, "ex": make_marks, "tw": turn_window_all,
        "w0": lambda: start(video_copies(0)), "w1": lambda: start(video_copies(1)), "w2": lambda: start(video_copies(2)),
    }
    for t, name in enumerate("QKV"):
        for stage in range(4):
            steps[f"{stage + 1}{name}"] = lambda t=t, stage=stage: take(t, stage)
    for half in range(2):
        steps[f"p{half}"] = lambda half=half: place_all(half)
        steps[f"r1_{half}"] = lambda half=half: reduce_start(half)
        steps[f"r2_{half}"] = lambda half=half: reduce_pass(half)
        steps[f"ca_{half}"] = lambda half=half: reduce_cross(half)
        steps[f"cb_{half}"] = lambda half=half: reduce_cross_pass(half)
        steps[f"o_{half}"] = lambda half=half: finish_half(half)

    parts = {"": [], "A": [], "B": [], "X": [], "T": [], "Y": []}
    part_now, at = "", None
    for name in ORDER:
        if isinstance(name, int):
            at = name
        elif name in parts:
            part_now, at = name, None
        else:
            parts[part_now].append((at, steps[name]))

    def run(name):
        for _, step in parts[name]:
            step()

    run("")
    ready_audio()
    pipeline(30, 4, audio_scores, audio_finish, parts["A"])
    run("B")
    ready_video()
    video_weights(parts["X"])
    run("T")
    video_values(parts["Y"])

    for t in range(4):
        sent(x_step(t))
        for stage in range(4):
            sent(gather(t, stage))
    for i in range(3):
        swap(i)[0].wait_send()
    swap_marks().wait_send()
    for half in range(2):
        sent(reduce1(half))
        sent(reduce2(half))
        sent(results(half))
        for cc in (0, 1):
            mine = pl.ds(cc * 768 + half * 384, 384)
            remote(
                ao.at[pl.ds(0, 64), pl.ds(half * 384, 384)], aout_hbm.at[:, mine], o_send.at[half, 0],
                o_recv.at[half, cc], result_low,
            ).wait_recv()
    for i in range(3):
        away, here = video_copies(i)
        here.wait()
        away.wait()


def on_device(video_q, video_k, video_v, audio_q, audio_k, audio_v, video_clip, audio_clip):
    anywhere = pl.BlockSpec(memory_space=pl.ANY)
    dma = pltpu.SemaphoreType.DMA
    return pl.pallas_call(
        kernel,
        out_shape=(
            jax.ShapeDtypeStruct(video_q.shape, BF),
            jax.ShapeDtypeStruct(audio_k.shape, BF),
        ),
        in_specs=[
            pl.BlockSpec(memory_space=pltpu.SMEM),
            pl.BlockSpec(memory_space=pltpu.VMEM),
            pl.BlockSpec(memory_space=pltpu.VMEM),
        ]
        + [anywhere] * 6,
        out_specs=(anywhere, anywhere),
        scratch_shapes=[
            pltpu.VMEM((1024, 768), BF),
            pltpu.VMEM((1024, 768), BF),
            pltpu.VMEM((1024, 768), BF),
            pltpu.VMEM((1024, HD), BF),
            pltpu.VMEM((2, 4, 4, 64, 768), BF),
            pltpu.VMEM((2, 4, 4, 64, 768), BF),
            pltpu.VMEM((2, 4, 4, 64, 768), BF),
            pltpu.VMEM((2, 4, 4, 32, HD), BF),
            pltpu.VMEM((2, 4, 4, 64, HD), BF),
            pltpu.VMEM((32, HD), BF),
            pltpu.VMEM((6, HD + 16, 1024), BF),
            pltpu.VMEM((1024, 256), F32),
            pltpu.VMEM((1024, 256), F32),
            pltpu.VMEM((512, BLOCKS * HD), F32),
            pltpu.VMEM((512, BLOCKS * HD), F32),
            pltpu.VMEM((12, 512, BLOCKS * HD), BF),
            pltpu.VMEM((6, BLOCKS, 8, HD), F32),
            pltpu.VMEM((6, BLOCKS, 8, HD), F32),
            pltpu.VMEM((2, BLOCKS, STAT, HD), BF),
            pltpu.VMEM((2, 4, 4, ROWS, HD), BF),
            pltpu.VMEM((2, 6, 2, ROWS, HD), BF),
            pltpu.VMEM((2, 3, ROWS, HD), BF),
            pltpu.VMEM((1024, 768), BF),
            pltpu.VMEM((HD, 768), BF),
            dma((4, 2)),
            dma((4, 2)),
            dma((4, 16)),
            dma((4, 16)),
            dma((4,)),
            dma((4,)),
            dma((3,)),
            dma((2, 9)),
            dma((2, 9)),
            dma((2, 2)),
            dma((2, 2)),
            dma((3,)),
            dma((3,)),
            dma((3,)),
        ],
        compiler_params=pltpu.CompilerParams(
            collective_id=0, has_side_effects=True, vmem_limit_bytes=56 * 1024 * 1024
        ),
    )(
        video_clip, video_clip.reshape(4, HD), audio_clip.reshape(1, 64), video_q, video_k, video_v, audio_q, audio_k,
        audio_v,
    )


def solution(mesh):
    spread = P(("grp", "seq"), None)
    return jax.shard_map(
        on_device,
        mesh=mesh,
        in_specs=(spread,) * 6 + (P(("grp", "seq")),) * 2,
        out_specs=(spread, spread),
        check_vma=False,
    )
```

```python
import math

import jax
import jax.numpy as jnp
from jax import lax
from jax.experimental import pallas as pl
from jax.experimental.pallas import tpu as pltpu
from jax.sharding import PartitionSpec as P

MESH = pl.DeviceIdType.MESH
BF = jnp.bfloat16
F32 = jnp.float32
HD = 128
CLIPS = 9
SCALE = math.log2(math.e) / math.sqrt(HD)
FAR = -1048576.0
LOW = -32768.0
BLOCKS = 10
STAT = 3 * HD
ROWS = STAT + 16


ORDER = (
    "1Q", "xKs", "2Q", "xVs", "1K", "3Q", "1V", "vt", "2K", "4Q", "2V", "ex", "3K", "vqs", "A", 1, "3V", 7,
    "p0", "4K", 11, "r1_0", "B", "p1", "r1_1", "X", 1, "4V", 3, "r2_0", "r2_1", 5, "ca_0", "T", "ca_1", "tw",
    "Y", 0, "cb_0", 1, "cb_1", 3, "o_0", 4, "w1", "o_1", "w0", 5, "w2",
)


def kernel(
    clip_smem, video_clip, audio_clip, vq_hbm, vk_hbm, vv_hbm, aq_hbm, ak_hbm, av_hbm,
    vout_hbm, aout_hbm,
    vq, vk, vv, ve, aq, ak, av, mk, am, mk_own, vt, buf_c, buf_d, buf_a, buf_b, wb, tops, sums, window, part, got1, got2, vo, ao,
    x_send, x_recv, g_send, g_recv, v_send, v_recv, v_local, r_send, r_recv, o_send, o_recv, w_send, w_recv, w_local,
):
    g = lax.axis_index("grp")
    s = lax.axis_index("seq")
    core = lax.rem(s, 2)
    chip = s // 2
    z, y = chip // 4, lax.rem(chip, 4)
    zp, zm, z2 = lax.rem(z + 1, 4), lax.rem(z + 3, 4), lax.rem(z + 2, 4)
    yp, ym, y2 = lax.rem(y + 1, 4), lax.rem(y + 3, 4), lax.rem(y + 2, 4)
    gp, gm = lax.rem(g + 1, 4), lax.rem(g + 3, 4)

    def device(grp, zz, yy, cc):
        return (grp, (zz * 4 + yy) * 2 + cc)

    other = device(g, z, y, 1 - core)
    to_yp, to_ym = (device(g, z, b, core) for b in (yp, ym))
    to_zp, to_zm = (device(g, b, y, core) for b in (zp, zm))
    before = lax.rem(chip + 15, 16)
    after = lax.rem(chip + 1, 16)
    result_low = (gp, chip * 2)
    result_high = (gp, before * 2 + 1)

    barrier = pltpu.get_barrier_semaphore()

    def greet(dev):
        pl.semaphore_signal(barrier, inc=1, device_id=dev, device_id_type=MESH)

    for dev in (other, to_yp, to_ym, to_zp, to_zm):
        greet(dev)
    for cc in (0, 1):
        greet(device(gm, z, y, cc))
        greet(device(gp, z, y, cc))
    greet(result_high)

    @pl.when(core == 1)
    def _():
        greet((gm, after * 2))
        greet((gm, after * 2 + 1))

    pl.semaphore_wait(barrier, 10 + 2 * core)

    def remote(src, dst, ssem, rsem, dev):
        return pltpu.make_async_remote_copy(
            src_ref=src, dst_ref=dst, send_sem=ssem, recv_sem=rsem, device_id=dev, device_id_type=MESH
        )

    def columns(half, width):
        return pl.ds(pl.multiple_of(half * width, 128), width)

    tensors = ((aq_hbm, aq), (ak_hbm, ak), (av_hbm, av), (mk_own, mk))

    def x_copies(t, sender):
        src, dst = tensors[t]
        return [
            remote(
                src if t == 3 else src.at[:, pl.ds(cc * 768, 768)], dst.at[sender, z, y], x_send.at[t, cc],
                x_recv.at[t, sender], device(gm, z, y, cc),
            )
            for cc in (0, 1)
        ]

    def x_step(t):
        return x_copies(t, core)

    here_already = set()

    def x_wait(t):
        if t in here_already:
            return
        here_already.add(t)
        for cc in (0, 1):
            x_copies(t, cc)[0].wait_recv()

    def gather(t, stage):
        x = tensors[t][1]
        rows = x.shape[3] // 2
        low, high = pl.ds(0, rows), pl.ds(rows, rows)
        first, last = pl.ds(0, 2), pl.ds(2, 2)
        plan = (
            (x.at[0, z, y], to_yp),
            (x.at[0, z, y], to_ym),
            (x.at[1, z, y], to_zp),
            (x.at[1, z, y], to_zm),
        ), (
            (x.at[0, z, ym, low], to_yp),
            (x.at[0, z, yp, high], to_ym),
            (x.at[1, zm, y, low], to_zp),
            (x.at[1, zp, y, high], to_zm),
        ), (
            (x.at[0, z], to_zp),
            (x.at[0, z], to_zm),
            (x.at[1, :, y], to_yp),
            (x.at[1, :, y], to_ym),
        ), (
            (x.at[0, zm, first], to_zp),
            (x.at[0, zp, last], to_zm),
            (x.at[1, first, ym], to_yp),
            (x.at[1, last, yp], to_ym),
        )
        return [
            remote(ref, ref, g_send.at[t, stage * 4 + i], g_recv.at[t, stage * 4 + i], dev)
            for i, (ref, dev) in enumerate(plan[stage])
        ]

    def start(copies):
        for copy in copies:
            copy.start()

    def arrive(copies):
        for copy in copies:
            copy.wait_recv()

    def sent(copies):
        for copy in copies:
            copy.wait_send()

    video = ((vk_hbm, vk), (vv_hbm, vv), (vq_hbm, vq))
    own_rows = pl.ds(pl.multiple_of(core * 512, 512), 512)
    other_rows = pl.ds(pl.multiple_of((1 - core) * 512, 512), 512)

    def swap(i):
        src, dst = video[i]
        return (
            remote(src.at[:, columns(1 - core, 768)], dst.at[own_rows], v_send.at[i], v_recv.at[i], other),
            pltpu.make_async_copy(src.at[:, columns(core, 768)], dst.at[own_rows], v_local.at[i]),
        )

    def swap_start(i):
        away, here = swap(i)
        away.start()
        here.start()

    def swap_wait(i):
        away, here = swap(i)
        away.wait_recv()
        here.wait()

    def swap_marks():
        return remote(ve.at[own_rows], ve.at[own_rows], v_send.at[3], v_recv.at[3], other)

    start(x_step(0))
    swap_start(0)
    swap_start(1)

    numbers = (audio_clip[...] - gm * CLIPS).astype(F32)
    numbers = jnp.concatenate([numbers, numbers], axis=1)
    mk_own[...] = jnp.broadcast_to(numbers, (32, HD)).astype(BF)
    start(x_step(3))
    clips = lax.broadcasted_iota(jnp.int32, (HD, HD), 0)
    for i in range(4):
        same = video_clip[i : i + 1, :] - g * CLIPS == clips
        at = pl.multiple_of(core * 512 + i * HD, HD)
        ve[pl.ds(at, HD), :] = jnp.where(same, 0.0, FAR).T.astype(BF)
    swap_marks().start()

    def turn(h, carry):
        cols = pl.ds(pl.multiple_of(h * HD, HD), HD)
        vt[h, pl.ds(0, HD), :] = vv[:, cols].T
        vt[h, pl.ds(HD, 16), :] = jnp.ones((16, 1024), BF)
        return carry

    lanes = clips.astype(F32)

    def expand(i, carry):
        bz, by = i // 4, lax.rem(i, 4)
        for cc in (0, 1):
            numbers = mk[cc, bz, by, pl.ds(0, 16), :].astype(F32)[0:1]
            am[cc, bz, by] = jnp.where(numbers == lanes, 1.0, 0.0).T[0:64].astype(BF)
        return carry

    first = jnp.where(core == 0, clip_smem[0], clip_smem[511] - 1) - g * CLIPS

    def block(i):
        return jnp.bitwise_and(first + i, 15)

    def pieces(ref, i, cols):
        b, a = block(i - 1), block(i)
        return [ref[1, b // 4, jnp.bitwise_and(b, 3), :, cols], ref[0, a // 4, jnp.bitwise_and(a, 3), :, cols]]

    marks = pl.ds(0, HD)

    def packed(top, total):
        high = total.astype(BF).astype(F32)
        gap = jnp.zeros((1, HD), F32)
        return jnp.concatenate([top, gap, total - high, gap, high, jnp.zeros((5, HD), F32)], axis=0)

    def run_events(i, events):
        for at in sorted({at for at, _ in events}):

            @pl.when(i == at)
            def _():
                for where, event in events:
                    if where == at:
                        event()

    def pipeline(units, sizes, scores_of, finish, events):
        def both(u_scores, u_out, buf_scores, buf_out, top):
            q, k_of = scores_of(u_scores)
            store = None
            if u_out is not None:
                top = jnp.max(top, axis=0, keepdims=True) * SCALE
                top, use, store = finish(u_out, top)
            high, total = None, None
            for c in range(sizes):
                rows = pl.ds(c * 256, 256)
                scores = lax.dot_general(k_of(c), q, (((1,), (1,)), ((), ())), preferred_element_type=F32)
                buf_scores[rows, :] = scores
                best = jnp.max(scores.reshape(32, 8, 256), axis=0)
                high = best if high is None else jnp.maximum(high, best)
                if u_out is not None:
                    weights = jnp.exp2(buf_out[rows, :] * SCALE - top).astype(BF)
                    out = use(c, weights)
                    if store is not None:
                        total = out if total is None else total + out
            if store is not None:
                store(total, top)
            return high

        def body(i, top):
            u = 2 * i
            top = both(u + 1, u, buf_d, buf_c, top)
            top = both(jnp.minimum(u + 2, units - 1), u + 1, buf_c, buf_d, top)
            run_events(i, events)
            return top

        lax.fori_loop(0, units // 2, body, both(0, None, buf_c, None, None))

    def audio_scores(u):
        h, tile = u // 5, lax.rem(u, 5)
        cols = pl.ds(pl.multiple_of(h * HD, HD), HD)
        mark = jnp.concatenate(pieces(am, 2 * tile, marks) + pieces(am, 2 * tile + 1, marks), axis=0)
        q = jnp.concatenate(pieces(aq, 2 * tile, cols) + pieces(aq, 2 * tile + 1, cols), axis=0)

        def k_of(c):
            rows = pl.ds(c * 256, 256)
            return jnp.concatenate([vk[rows, cols], ve[rows, :]], axis=1)

        return jnp.concatenate([q, mark], axis=1), k_of

    def audio_finish(u, top):
        h, tile = u // 5, lax.rem(u, 5)
        top = jnp.maximum(top, LOW).astype(BF).astype(F32)

        def use(c, weights):
            return jnp.dot(vt[h, :, pl.ds(c * 256, 256)], weights, preferred_element_type=F32)

        def store(out, top):
            where = pl.ds(pl.multiple_of(lax.rem(h, 3) * HD, HD), HD)
            for b in range(2):
                window[h // 3, 2 * tile + b, where, :] = out[:HD, b * HD : (b + 1) * HD].astype(BF)
                tops[h, 2 * tile + b] = jnp.broadcast_to(top[:, b * HD : (b + 1) * HD], (8, HD))
                sums[h, 2 * tile + b] = jnp.broadcast_to(out[HD : HD + 1, b * HD : (b + 1) * HD], (8, HD))

        return top, use, store

    empty = jnp.where(lax.broadcasted_iota(jnp.int32, (16, HD), 0) < 3, LOW, 0.0)

    def place_block(half, b):
        at = jnp.bitwise_and(b - first, 15)
        inside = (at < BLOCKS).astype(F32)
        at = jnp.minimum(at, BLOCKS - 1)
        bz, by = b // 4, lax.rem(b, 4)
        body = window[half, at, :, :].astype(F32)
        part[half, bz, by, pl.ds(0, STAT), :] = (body * inside).astype(BF)
        top = jnp.concatenate([tops[half * 3 + hh, at][0:1] for hh in range(3)], axis=0)
        total = jnp.concatenate([sums[half * 3 + hh, at][0:1] for hh in range(3)], axis=0)
        stats = packed(top, total)
        part[half, bz, by, pl.ds(STAT, 16), :] = (stats * inside + empty * (1.0 - inside)).astype(BF)

    def place_all(half):
        def body(b, carry):
            place_block(half, b)
            return carry

        lax.fori_loop(0, 16, body, 0)

    def slab(half, where, lo):
        if half == 0:
            return part.at[0, where, pl.ds(lo, 2)]
        return part.at[1, pl.ds(lo, 2), where]

    axes = ((z, zp, zm, z2, to_zp, to_zm), (y, yp, ym, y2, to_yp, to_ym))
    turn_by = 1 + 2 * core

    def cross(at, two):
        p, m = lax.rem(at + turn_by, 4), lax.rem(at + 4 - turn_by, 4)
        return at, p, m, two

    crosses = (cross(y, y2), cross(z, z2))

    def reduce1(half):
        _, p, m, two, to_p, to_m = axes[half]
        plan = (
            (slab(half, two, 0), to_p), (slab(half, two, 2), to_m),
            (slab(half, p, 2), to_p), (slab(half, m, 0), to_m),
            (slab(half, p, 0), to_p), (slab(half, m, 2), to_m),
        )
        return [
            remote(ref, got1.at[half, i], r_send.at[half, i], r_recv.at[half, i], dev)
            for i, (ref, dev) in enumerate(plan)
        ]

    def one(half, u):
        if half == 0:
            return part.at[0, z, u]
        return part.at[1, u, y]

    def reduce2(half):
        _, p, m, two = crosses[half]
        to_p, to_m = (device(g, z, u, core) if half == 0 else device(g, u, y, core) for u in (p, m))
        return [
            remote(one(half, u), got2.at[half, i], r_send.at[half, 6 + i], r_recv.at[half, 6 + i], dev)
            for i, (u, dev) in enumerate(((two, to_p), (m, to_m), (p, to_p)))
        ]

    def merged(refs):
        stats = [ref[pl.ds(STAT, 16), :].astype(F32) for ref in refs]
        tops = [x[0:3] for x in stats]
        top = tops[0]
        for x in tops[1:]:
            top = jnp.maximum(top, x)
        factors = [jnp.exp2(x - top) for x in tops]
        total = sum((x[8:11] + x[4:7]) * f for x, f in zip(stats, factors))
        outs = [
            sum(ref[pl.ds(hh * HD, HD), :].astype(F32) * f[hh : hh + 1] for ref, f in zip(refs, factors))
            for hh in range(3)
        ]
        return outs, top, total

    def merge_into(target, sources):
        outs, top, total = merged([target] + sources)
        for hh in range(3):
            target[pl.ds(hh * HD, HD), :] = outs[hh].astype(BF)
        target[pl.ds(STAT, 16), :] = packed(top, total).astype(BF)

    def merge_slab(half, where, lo, slots):
        def body(i, carry):
            target = part.at[0, where, lo + i] if half == 0 else part.at[1, lo + i, where]
            merge_into(target, [got1.at[half, slot, i] for slot in slots])
            return carry

        lax.fori_loop(0, 2, body, 0)

    def reduce_start(half):
        start(reduce1(half)[:4])

    def reduce_pass(half):
        _, p, m, *_ = axes[half]
        copies = reduce1(half)
        copies[0].wait_recv()
        merge_slab(half, p, 0, (0,))
        copies[4].start()
        copies[1].wait_recv()
        merge_slab(half, m, 2, (1,))
        copies[5].start()

    def reduce_cross(half):
        own = axes[half][0]
        arrive(reduce1(half)[2:])
        merge_slab(half, own, 0, (3, 4))
        merge_slab(half, own, 2, (2, 5))
        start(reduce2(half)[:2])

    def reduce_cross_pass(half):
        copies = reduce2(half)
        copies[0].wait_recv()
        merge_into(one(half, crosses[half][1]), [got2.at[half, 0]])
        copies[2].start()

    def reduce_end(half):
        own = crosses[half][0]
        arrive(reduce2(half)[1:])
        outs, _, total = merged([one(half, own)] + [got2.at[half, i] for i in (1, 2)])
        scale = 1.0 / total
        for hh in range(3):
            done = (outs[hh] * scale[hh : hh + 1]).T
            ao[:, pl.ds((half * 3 + hh) * HD, HD)] = done.astype(BF)

    def results(half):
        mine = pl.ds(pl.multiple_of(core * 768 + half * 384, 128), 384)
        cols = pl.ds(half * 384, 384)
        return [
            remote(
                ao.at[rows, cols], aout_hbm.at[:, mine], o_send.at[half, i], o_recv.at[half, core], dev
            )
            for i, (rows, dev) in enumerate(((pl.ds(64, 64), result_low), (pl.ds(0, 64), result_high)))
        ]

    def rows_of(ref, i, cols):
        return jnp.concatenate(pieces(ref, 2 * i, cols) + pieces(ref, 2 * i + 1, cols), axis=0)

    def video_unit(u):
        cols = pl.ds(pl.multiple_of(u // 2 * HD, HD), HD)
        return cols, pl.ds(pl.multiple_of(lax.rem(u, 2) * 512, 512), 512)

    def video_both(u_scores, u_out, buf_scores, buf_out):
        cols, here = video_unit(u_scores)
        q = jnp.concatenate([vq[here, cols], ve[here, :]], axis=1)
        row = 0
        for c in range(5):
            k = jnp.concatenate([rows_of(ak, c, cols), rows_of(am, c, marks)], axis=1)
            buf_scores[:, c * 256 : (c + 1) * 256] = lax.dot_general(
                q, k, (((1,), (1,)), ((), ())), preferred_element_type=F32
            )
            if u_out is not None:
                for _ in range(7 if c < 2 else 6):
                    scores = buf_out[row : row + 16, :]
                    top = jnp.max(scores, axis=1, keepdims=True) * SCALE
                    wb[u_out, row : row + 16, :] = jnp.exp2(scores * SCALE - top).astype(BF)
                    row += 16

    def video_weights(events):
        def body(i, carry):
            u = 2 * i
            video_both(u + 1, u, buf_b, buf_a)
            video_both(jnp.minimum(u + 2, 11), u + 1, buf_a, buf_b)
            run_events(i, events)
            return carry

        video_both(0, None, buf_a, None)
        lax.fori_loop(0, 6, body, 0)

    def video_values(events):
        def body(i, carry):
            cols, _ = video_unit(2 * i)
            v = jnp.concatenate([rows_of(av, c, cols) for c in range(5)], axis=0)
            v = jnp.concatenate([v, jnp.ones((BLOCKS * HD, HD), BF)], axis=1)
            for j in range(2):
                out = jnp.dot(wb[2 * i + j], v, preferred_element_type=F32)
                vo[pl.ds(j * 512, 512), cols] = (out[:, :HD] / out[:, HD:]).astype(BF)
            run_events(i, events)
            return carry

        lax.fori_loop(0, 6, body, 0)

    def video_copies(i):
        cols = pl.ds(i * 256, 256)
        mine = pl.ds(pl.multiple_of(core * 768 + i * 256, 128), 256)
        return (
            remote(vo.at[other_rows, cols], vout_hbm.at[:, mine], w_send.at[i], w_recv.at[i], other),
            pltpu.make_async_copy(vo.at[own_rows, cols], vout_hbm.at[:, mine], w_local.at[i]),
        )

    def take(t, stage):
        for tensor in (3, 0) if t == 0 else (t,):
            if stage == 0:
                x_wait(tensor)
            else:
                arrive(gather(tensor, stage - 1))
            start(gather(tensor, stage))

    def x_next(t):
        x_wait(t - 1)
        start(x_step(t))

    def turn_values():
        swap_wait(1)
        lax.fori_loop(0, 6, turn, 0)

    def make_marks():
        arrive(gather(3, 3))
        lax.fori_loop(0, 16, expand, 0)

    def ready_audio():
        swap_wait(0)
        swap_marks().wait_recv()
        arrive(gather(0, 3))

    def turn_window_all():
        arrive(gather(2, 3))

    def ready_video():
        swap_wait(2)
        arrive(gather(1, 3))

    def finish_half(half):
        reduce_end(half)
        start(results(half))

    steps = {
        "xKs": lambda: x_next(1), "xVs": lambda: x_next(2), "vqs": lambda: swap_start(2),
        "vt": turn_values, "ex": make_marks, "tw": turn_window_all,
        "w0": lambda: start(video_copies(0)), "w1": lambda: start(video_copies(1)), "w2": lambda: start(video_copies(2)),
    }
    for t, name in enumerate("QKV"):
        for stage in range(4):
            steps[f"{stage + 1}{name}"] = lambda t=t, stage=stage: take(t, stage)
    for half in range(2):
        steps[f"p{half}"] = lambda half=half: place_all(half)
        steps[f"r1_{half}"] = lambda half=half: reduce_start(half)
        steps[f"r2_{half}"] = lambda half=half: reduce_pass(half)
        steps[f"ca_{half}"] = lambda half=half: reduce_cross(half)
        steps[f"cb_{half}"] = lambda half=half: reduce_cross_pass(half)
        steps[f"o_{half}"] = lambda half=half: finish_half(half)

    parts = {"": [], "A": [], "B": [], "X": [], "T": [], "Y": []}
    part_now, at = "", None
    for name in ORDER:
        if isinstance(name, int):
            at = name
        elif name in parts:
            part_now, at = name, None
        else:
            parts[part_now].append((at, steps[name]))

    def run(name):
        for _, step in parts[name]:
            step()

    run("")
    ready_audio()
    pipeline(30, 4, audio_scores, audio_finish, parts["A"])
    run("B")
    ready_video()
    video_weights(parts["X"])
    run("T")
    video_values(parts["Y"])

    for t in range(4):
        sent(x_step(t))
        for stage in range(4):
            sent(gather(t, stage))
    for i in range(3):
        swap(i)[0].wait_send()
    swap_marks().wait_send()
    for half in range(2):
        sent(reduce1(half))
        sent(reduce2(half))
        sent(results(half))
        for cc in (0, 1):
            mine = pl.ds(cc * 768 + half * 384, 384)
            remote(
                ao.at[pl.ds(0, 64), pl.ds(half * 384, 384)], aout_hbm.at[:, mine], o_send.at[half, 0],
                o_recv.at[half, cc], result_low,
            ).wait_recv()
    for i in range(3):
        away, here = video_copies(i)
        here.wait()
        away.wait()


def on_device(video_q, video_k, video_v, audio_q, audio_k, audio_v, video_clip, audio_clip):
    anywhere = pl.BlockSpec(memory_space=pl.ANY)
    dma = pltpu.SemaphoreType.DMA
    return pl.pallas_call(
        kernel,
        out_shape=(
            jax.ShapeDtypeStruct(video_q.shape, BF),
            jax.ShapeDtypeStruct(audio_k.shape, BF),
        ),
        in_specs=[
            pl.BlockSpec(memory_space=pltpu.SMEM),
            pl.BlockSpec(memory_space=pltpu.VMEM),
            pl.BlockSpec(memory_space=pltpu.VMEM),
        ]
        + [anywhere] * 6,
        out_specs=(anywhere, anywhere),
        scratch_shapes=[
            pltpu.VMEM((1024, 768), BF),
            pltpu.VMEM((1024, 768), BF),
            pltpu.VMEM((1024, 768), BF),
            pltpu.VMEM((1024, HD), BF),
            pltpu.VMEM((2, 4, 4, 64, 768), BF),
            pltpu.VMEM((2, 4, 4, 64, 768), BF),
            pltpu.VMEM((2, 4, 4, 64, 768), BF),
            pltpu.VMEM((2, 4, 4, 32, HD), BF),
            pltpu.VMEM((2, 4, 4, 64, HD), BF),
            pltpu.VMEM((32, HD), BF),
            pltpu.VMEM((6, HD + 16, 1024), BF),
            pltpu.VMEM((1024, 256), F32),
            pltpu.VMEM((1024, 256), F32),
            pltpu.VMEM((512, BLOCKS * HD), F32),
            pltpu.VMEM((512, BLOCKS * HD), F32),
            pltpu.VMEM((12, 512, BLOCKS * HD), BF),
            pltpu.VMEM((6, BLOCKS, 8, HD), F32),
            pltpu.VMEM((6, BLOCKS, 8, HD), F32),
            pltpu.VMEM((2, BLOCKS, STAT, HD), BF),
            pltpu.VMEM((2, 4, 4, ROWS, HD), BF),
            pltpu.VMEM((2, 6, 2, ROWS, HD), BF),
            pltpu.VMEM((2, 3, ROWS, HD), BF),
            pltpu.VMEM((1024, 768), BF),
            pltpu.VMEM((HD, 768), BF),
            dma((4, 2)),
            dma((4, 2)),
            dma((4, 16)),
            dma((4, 16)),
            dma((4,)),
            dma((4,)),
            dma((3,)),
            dma((2, 9)),
            dma((2, 9)),
            dma((2, 2)),
            dma((2, 2)),
            dma((3,)),
            dma((3,)),
            dma((3,)),
        ],
        compiler_params=pltpu.CompilerParams(
            collective_id=0, has_side_effects=True, vmem_limit_bytes=56 * 1024 * 1024
        ),
    )(
        video_clip, video_clip.reshape(4, HD), audio_clip.reshape(1, 64), video_q, video_k, video_v, audio_q, audio_k,
        audio_v,
    )


def solution(mesh):
    spread = P(("grp", "seq"), None)
    return jax.shard_map(
        on_device,
        mesh=mesh,
        in_specs=(spread,) * 6 + (P(("grp", "seq")),) * 2,
        out_specs=(spread, spread),
        check_vma=False,
    )
```

```python
import math

import jax
import jax.numpy as jnp
from jax import lax
from jax.experimental import pallas as pl
from jax.experimental.pallas import tpu as pltpu
from jax.sharding import PartitionSpec as P

MESH = pl.DeviceIdType.MESH
BF = jnp.bfloat16
F32 = jnp.float32
HD = 128
CLIPS = 9
SCALE = math.log2(math.e) / math.sqrt(HD)
FAR = -1048576.0
LOW = -32768.0
BLOCKS = 10
STAT = 3 * HD
ROWS = STAT + 16


ORDER = (
    "1Q", "xKs", "2Q", "xVs", "1K", "3Q", "1V", "vt", "2K", "4Q", "2V", "ex", "3K", "vqs",
    "A", 0, "3V", 5, "p0", "4K", 8, "r1_0",
    "B", "p1", "r1_1",
    "X", 1, "4V", 3, "r2_0", "r2_1", 5, "ca_0",
    "T", "ca_1", "tw",
    "Y", 0, "cb_0", 1, "cb_1", 3, "o_0", 4, "w1", "o_1", "w0", 5, "w2",
)


def kernel(
    clip_smem, video_clip, audio_clip, vq_hbm, vk_hbm, vv_hbm, aq_hbm, ak_hbm, av_hbm,
    vout_hbm, aout_hbm,
    vq, vk, vv, ve, aq, ak, av, mk, am, mk_own, buf_c, buf_d, wt_c, wt_d, high_c, high_d, buf_a, buf_b, wb, tops, sums, window, part, got1, got2, vo, ao,
    x_send, x_recv, g_send, g_recv, v_send, v_recv, v_local, r_send, r_recv, o_send, o_recv, w_send, w_recv, w_local,
):
    g = lax.axis_index("grp")
    s = lax.axis_index("seq")
    core = lax.rem(s, 2)
    chip = s // 2
    z, y = chip // 4, lax.rem(chip, 4)
    zp, zm, z2 = lax.rem(z + 1, 4), lax.rem(z + 3, 4), lax.rem(z + 2, 4)
    yp, ym, y2 = lax.rem(y + 1, 4), lax.rem(y + 3, 4), lax.rem(y + 2, 4)
    gp, gm = lax.rem(g + 1, 4), lax.rem(g + 3, 4)

    def device(grp, zz, yy, cc):
        return (grp, (zz * 4 + yy) * 2 + cc)

    other = device(g, z, y, 1 - core)
    to_yp, to_ym = (device(g, z, b, core) for b in (yp, ym))
    to_zp, to_zm = (device(g, b, y, core) for b in (zp, zm))
    before = lax.rem(chip + 15, 16)
    after = lax.rem(chip + 1, 16)
    result_low = (gp, chip * 2)
    result_high = (gp, before * 2 + 1)

    barrier = pltpu.get_barrier_semaphore()

    def greet(dev):
        pl.semaphore_signal(barrier, inc=1, device_id=dev, device_id_type=MESH)

    for dev in (other, to_yp, to_ym, to_zp, to_zm):
        greet(dev)
    for cc in (0, 1):
        greet(device(gm, z, y, cc))
        greet(device(gp, z, y, cc))
    greet(result_high)

    @pl.when(core == 1)
    def _():
        greet((gm, after * 2))
        greet((gm, after * 2 + 1))

    pl.semaphore_wait(barrier, 10 + 2 * core)

    def remote(src, dst, ssem, rsem, dev):
        return pltpu.make_async_remote_copy(
            src_ref=src, dst_ref=dst, send_sem=ssem, recv_sem=rsem, device_id=dev, device_id_type=MESH
        )

    def columns(half, width):
        return pl.ds(pl.multiple_of(half * width, 128), width)

    tensors = ((aq_hbm, aq), (ak_hbm, ak), (av_hbm, av), (mk_own, mk))

    def x_copies(t, sender):
        src, dst = tensors[t]
        return [
            remote(
                src if t == 3 else src.at[:, pl.ds(cc * 768, 768)], dst.at[sender, z, y], x_send.at[t, cc],
                x_recv.at[t, sender], device(gm, z, y, cc),
            )
            for cc in (0, 1)
        ]

    def x_step(t):
        return x_copies(t, core)

    here_already = set()

    def x_wait(t):
        if t in here_already:
            return
        here_already.add(t)
        for cc in (0, 1):
            x_copies(t, cc)[0].wait_recv()

    def gather(t, stage):
        x = tensors[t][1]
        rows = x.shape[3] // 2
        low, high = pl.ds(0, rows), pl.ds(rows, rows)
        first, last = pl.ds(0, 2), pl.ds(2, 2)
        plan = (
            (x.at[0, z, y], to_yp),
            (x.at[0, z, y], to_ym),
            (x.at[1, z, y], to_zp),
            (x.at[1, z, y], to_zm),
        ), (
            (x.at[0, z, ym, low], to_yp),
            (x.at[0, z, yp, high], to_ym),
            (x.at[1, zm, y, low], to_zp),
            (x.at[1, zp, y, high], to_zm),
        ), (
            (x.at[0, z], to_zp),
            (x.at[0, z], to_zm),
            (x.at[1, :, y], to_yp),
            (x.at[1, :, y], to_ym),
        ), (
            (x.at[0, zm, first], to_zp),
            (x.at[0, zp, last], to_zm),
            (x.at[1, first, ym], to_yp),
            (x.at[1, last, yp], to_ym),
        )
        return [
            remote(ref, ref, g_send.at[t, stage * 4 + i], g_recv.at[t, stage * 4 + i], dev)
            for i, (ref, dev) in enumerate(plan[stage])
        ]

    def start(copies):
        for copy in copies:
            copy.start()

    def arrive(copies):
        for copy in copies:
            copy.wait_recv()

    def sent(copies):
        for copy in copies:
            copy.wait_send()

    video = ((vk_hbm, vk), (vv_hbm, vv), (vq_hbm, vq))
    own_rows = pl.ds(pl.multiple_of(core * 512, 512), 512)
    other_rows = pl.ds(pl.multiple_of((1 - core) * 512, 512), 512)

    def swap(i):
        src, dst = video[i]
        return (
            remote(src.at[:, columns(1 - core, 768)], dst.at[own_rows], v_send.at[i], v_recv.at[i], other),
            pltpu.make_async_copy(src.at[:, columns(core, 768)], dst.at[own_rows], v_local.at[i]),
        )

    def swap_start(i):
        away, here = swap(i)
        away.start()
        here.start()

    def swap_wait(i):
        away, here = swap(i)
        away.wait_recv()
        here.wait()

    def swap_marks():
        return remote(ve.at[own_rows], ve.at[own_rows], v_send.at[3], v_recv.at[3], other)

    start(x_step(0))
    swap_start(0)
    swap_start(1)

    numbers = (audio_clip[...] - gm * CLIPS).astype(F32)
    numbers = jnp.concatenate([numbers, numbers], axis=1)
    mk_own[...] = jnp.broadcast_to(numbers, (32, HD)).astype(BF)
    start(x_step(3))
    clips = lax.broadcasted_iota(jnp.int32, (HD, HD), 0)
    for i in range(4):
        same = video_clip[i : i + 1, :] - g * CLIPS == clips
        at = pl.multiple_of(core * 512 + i * HD, HD)
        ve[pl.ds(at, HD), :] = jnp.where(same, 0.0, FAR).T.astype(BF)
    swap_marks().start()

    lanes = clips.astype(F32)

    def expand(i, carry):
        bz, by = i // 4, lax.rem(i, 4)
        for cc in (0, 1):
            numbers = mk[cc, bz, by, pl.ds(0, 16), :].astype(F32)[0:1]
            am[cc, bz, by] = jnp.where(numbers == lanes, 1.0, 0.0).T[0:64].astype(BF)
        return carry

    first = jnp.where(core == 0, clip_smem[0], clip_smem[511] - 1) - g * CLIPS

    def block(i):
        return jnp.bitwise_and(first + i, 15)

    def pieces(ref, i, cols):
        b, a = block(i - 1), block(i)
        return [ref[1, b // 4, jnp.bitwise_and(b, 3), :, cols], ref[0, a // 4, jnp.bitwise_and(a, 3), :, cols]]

    marks = pl.ds(0, HD)

    def packed(top, total):
        high = total.astype(BF).astype(F32)
        gap = jnp.zeros((1, HD), F32)
        return jnp.concatenate([top, gap, total - high, gap, high, jnp.zeros((5, HD), F32)], axis=0)

    def run_events(i, events):
        for at in sorted({at for at, _ in events}):

            @pl.when(i == at)
            def _():
                for where, event in events:
                    if where == at:
                        event()

    lane = lax.broadcasted_iota(jnp.int32, (HD, HD), 1)

    def audio_step(unit_scores, unit_weights, unit_values):
        if unit_scores is not None:
            u, buf = unit_scores
            cols = pl.ds(pl.multiple_of(u // 2 * HD, HD), HD)
            blocks = [5 * lax.rem(u, 2) + i for i in range(5)]
            q = jnp.concatenate([piece for i in blocks for piece in pieces(aq, i, cols)], axis=0)
            mark = jnp.concatenate([piece for i in blocks for piece in pieces(am, i, marks)], axis=0)
            q = jnp.concatenate([q, mark], axis=1)
        if unit_values is not None:
            h, tile, weights, high = unit_values[0] // 2, lax.rem(unit_values[0], 2), unit_values[1], unit_values[2]
            v = jnp.concatenate([vv[:, pl.ds(pl.multiple_of(h * HD, HD), HD)], jnp.ones((1024, HD), BF)], axis=1)
            out = jnp.dot(weights[...], v, preferred_element_type=F32)
        row = 0
        for c in range(4):
            if unit_scores is not None:
                rows = pl.ds(c * 256, 256)
                k = jnp.concatenate([vk[rows, cols], ve[rows, :]], axis=1)
                buf[:, c * 256 : (c + 1) * 256] = lax.dot_general(
                    q, k, (((1,), (1,)), ((), ())), preferred_element_type=F32
                )
            if unit_weights is not None:
                scores_w, weights_w, high_w = unit_weights
                for _ in range(10):
                    scores = scores_w[row : row + 16, :]
                    top = jnp.maximum(jnp.max(scores, axis=1, keepdims=True) * SCALE, LOW).astype(BF).astype(F32)
                    weights_w[row : row + 16, :] = jnp.exp2(scores * SCALE - top).astype(BF)
                    high_w[row : row + 16, :] = jnp.broadcast_to(top, (16, HD))
                    row += 16
        if unit_values is not None:
            where = pl.ds(pl.multiple_of(lax.rem(h, 3) * HD, HD), HD)
            for b in range(5):
                rows = slice(b * HD, (b + 1) * HD)
                window[h // 3, 5 * tile + b, where, :] = out[rows, :HD].T.astype(BF)
                stats = jnp.where(lane < 8, high[rows, :], out[rows, HD:]).T
                tops[h, 5 * tile + b] = stats[0:8]
                sums[h, 5 * tile + b] = stats[8:16]

    def audio(events):
        even, odd = (buf_c, wt_c, high_c), (buf_d, wt_d, high_d)

        def body(i, carry):
            u = 2 * i
            audio_step((u + 2, buf_c), odd, (u, wt_c, high_c))
            run_events(u, events)
            audio_step((u + 3, buf_d), even, (u + 1, wt_d, high_d))
            run_events(u + 1, events)
            return carry

        audio_step((0, buf_c), None, None)
        audio_step((1, buf_d), even, None)
        lax.fori_loop(0, 5, body, 0)
        audio_step(None, odd, (10, wt_c, high_c))
        audio_step(None, None, (11, wt_d, high_d))

    def run_events(i, events):
        for at in sorted({at for at, _ in events}):

            @pl.when(i == at)
            def _():
                for where, event in events:
                    if where == at:
                        event()

    empty = jnp.where(lax.broadcasted_iota(jnp.int32, (16, HD), 0) < 3, LOW, 0.0)

    def place_block(half, b):
        at = jnp.bitwise_and(b - first, 15)
        inside = (at < BLOCKS).astype(F32)
        at = jnp.minimum(at, BLOCKS - 1)
        bz, by = b // 4, lax.rem(b, 4)
        body = window[half, at, :, :].astype(F32)
        part[half, bz, by, pl.ds(0, STAT), :] = (body * inside).astype(BF)
        top = jnp.concatenate([tops[half * 3 + hh, at][0:1] for hh in range(3)], axis=0)
        total = jnp.concatenate([sums[half * 3 + hh, at][0:1] for hh in range(3)], axis=0)
        stats = packed(top, total)
        part[half, bz, by, pl.ds(STAT, 16), :] = (stats * inside + empty * (1.0 - inside)).astype(BF)

    def place_all(half):
        def body(b, carry):
            place_block(half, b)
            return carry

        lax.fori_loop(0, 16, body, 0)

    def slab(half, where, lo):
        if half == 0:
            return part.at[0, where, pl.ds(lo, 2)]
        return part.at[1, pl.ds(lo, 2), where]

    axes = ((z, zp, zm, z2, to_zp, to_zm), (y, yp, ym, y2, to_yp, to_ym))
    turn_by = 1 + 2 * core

    def cross(at, two):
        p, m = lax.rem(at + turn_by, 4), lax.rem(at + 4 - turn_by, 4)
        return at, p, m, two

    crosses = (cross(y, y2), cross(z, z2))

    def reduce1(half):
        _, p, m, two, to_p, to_m = axes[half]
        plan = (
            (slab(half, two, 0), to_p), (slab(half, two, 2), to_m),
            (slab(half, p, 2), to_p), (slab(half, m, 0), to_m),
            (slab(half, p, 0), to_p), (slab(half, m, 2), to_m),
        )
        return [
            remote(ref, got1.at[half, i], r_send.at[half, i], r_recv.at[half, i], dev)
            for i, (ref, dev) in enumerate(plan)
        ]

    def one(half, u):
        if half == 0:
            return part.at[0, z, u]
        return part.at[1, u, y]

    def reduce2(half):
        _, p, m, two = crosses[half]
        to_p, to_m = (device(g, z, u, core) if half == 0 else device(g, u, y, core) for u in (p, m))
        return [
            remote(one(half, u), got2.at[half, i], r_send.at[half, 6 + i], r_recv.at[half, 6 + i], dev)
            for i, (u, dev) in enumerate(((two, to_p), (m, to_m), (p, to_p)))
        ]

    def merged(refs):
        stats = [ref[pl.ds(STAT, 16), :].astype(F32) for ref in refs]
        tops = [x[0:3] for x in stats]
        top = tops[0]
        for x in tops[1:]:
            top = jnp.maximum(top, x)
        factors = [jnp.exp2(x - top) for x in tops]
        total = sum((x[8:11] + x[4:7]) * f for x, f in zip(stats, factors))
        outs = [
            sum(ref[pl.ds(hh * HD, HD), :].astype(F32) * f[hh : hh + 1] for ref, f in zip(refs, factors))
            for hh in range(3)
        ]
        return outs, top, total

    def merge_into(target, sources):
        outs, top, total = merged([target] + sources)
        for hh in range(3):
            target[pl.ds(hh * HD, HD), :] = outs[hh].astype(BF)
        target[pl.ds(STAT, 16), :] = packed(top, total).astype(BF)

    def merge_slab(half, where, lo, slots):
        def body(i, carry):
            target = part.at[0, where, lo + i] if half == 0 else part.at[1, lo + i, where]
            merge_into(target, [got1.at[half, slot, i] for slot in slots])
            return carry

        lax.fori_loop(0, 2, body, 0)

    def reduce_start(half):
        start(reduce1(half)[:4])

    def reduce_pass(half):
        _, p, m, *_ = axes[half]
        copies = reduce1(half)
        copies[0].wait_recv()
        merge_slab(half, p, 0, (0,))
        copies[4].start()
        copies[1].wait_recv()
        merge_slab(half, m, 2, (1,))
        copies[5].start()

    def reduce_cross(half):
        own = axes[half][0]
        arrive(reduce1(half)[2:])
        merge_slab(half, own, 0, (3, 4))
        merge_slab(half, own, 2, (2, 5))
        start(reduce2(half)[:2])

    def reduce_cross_pass(half):
        copies = reduce2(half)
        copies[0].wait_recv()
        merge_into(one(half, crosses[half][1]), [got2.at[half, 0]])
        copies[2].start()

    def reduce_end(half):
        own = crosses[half][0]
        arrive(reduce2(half)[1:])
        outs, _, total = merged([one(half, own)] + [got2.at[half, i] for i in (1, 2)])
        scale = 1.0 / total
        for hh in range(3):
            done = (outs[hh] * scale[hh : hh + 1]).T
            ao[:, pl.ds((half * 3 + hh) * HD, HD)] = done.astype(BF)

    def results(half):
        mine = pl.ds(pl.multiple_of(core * 768 + half * 384, 128), 384)
        cols = pl.ds(half * 384, 384)
        return [
            remote(
                ao.at[rows, cols], aout_hbm.at[:, mine], o_send.at[half, i], o_recv.at[half, core], dev
            )
            for i, (rows, dev) in enumerate(((pl.ds(64, 64), result_low), (pl.ds(0, 64), result_high)))
        ]

    def rows_of(ref, i, cols):
        return jnp.concatenate(pieces(ref, 2 * i, cols) + pieces(ref, 2 * i + 1, cols), axis=0)

    def video_unit(u):
        cols = pl.ds(pl.multiple_of(u // 2 * HD, HD), HD)
        return cols, pl.ds(pl.multiple_of(lax.rem(u, 2) * 512, 512), 512)

    def video_both(u_scores, u_out, buf_scores, buf_out):
        cols, here = video_unit(u_scores)
        q = jnp.concatenate([vq[here, cols], ve[here, :]], axis=1)
        row = 0
        for c in range(5):
            k = jnp.concatenate([rows_of(ak, c, cols), rows_of(am, c, marks)], axis=1)
            buf_scores[:, c * 256 : (c + 1) * 256] = lax.dot_general(
                q, k, (((1,), (1,)), ((), ())), preferred_element_type=F32
            )
            if u_out is not None:
                for _ in range(7 if c < 2 else 6):
                    scores = buf_out[row : row + 16, :]
                    top = jnp.max(scores, axis=1, keepdims=True) * SCALE
                    wb[u_out, row : row + 16, :] = jnp.exp2(scores * SCALE - top).astype(BF)
                    row += 16

    def video_weights(events):
        def body(i, carry):
            u = 2 * i
            video_both(u + 1, u, buf_b, buf_a)
            video_both(jnp.minimum(u + 2, 11), u + 1, buf_a, buf_b)
            run_events(i, events)
            return carry

        video_both(0, None, buf_a, None)
        lax.fori_loop(0, 6, body, 0)

    def video_values(events):
        def body(i, carry):
            cols, _ = video_unit(2 * i)
            v = jnp.concatenate([rows_of(av, c, cols) for c in range(5)], axis=0)
            v = jnp.concatenate([v, jnp.ones((BLOCKS * HD, HD), BF)], axis=1)
            for j in range(2):
                out = jnp.dot(wb[2 * i + j], v, preferred_element_type=F32)
                vo[pl.ds(j * 512, 512), cols] = (out[:, :HD] / out[:, HD:]).astype(BF)
            run_events(i, events)
            return carry

        lax.fori_loop(0, 6, body, 0)

    def video_copies(i):
        cols = pl.ds(i * 256, 256)
        mine = pl.ds(pl.multiple_of(core * 768 + i * 256, 128), 256)
        return (
            remote(vo.at[other_rows, cols], vout_hbm.at[:, mine], w_send.at[i], w_recv.at[i], other),
            pltpu.make_async_copy(vo.at[own_rows, cols], vout_hbm.at[:, mine], w_local.at[i]),
        )

    def take(t, stage):
        for tensor in (3, 0) if t == 0 else (t,):
            if stage == 0:
                x_wait(tensor)
            else:
                arrive(gather(tensor, stage - 1))
            start(gather(tensor, stage))

    def x_next(t):
        x_wait(t - 1)
        start(x_step(t))

    def turn_values():
        swap_wait(1)

    def make_marks():
        arrive(gather(3, 3))
        lax.fori_loop(0, 16, expand, 0)

    def ready_audio():
        swap_wait(0)
        swap_marks().wait_recv()
        arrive(gather(0, 3))

    def turn_window_all():
        arrive(gather(2, 3))

    def ready_video():
        swap_wait(2)
        arrive(gather(1, 3))

    def finish_half(half):
        reduce_end(half)
        start(results(half))

    steps = {
        "xKs": lambda: x_next(1), "xVs": lambda: x_next(2), "vqs": lambda: swap_start(2),
        "vt": turn_values, "ex": make_marks, "tw": turn_window_all,
        "w0": lambda: start(video_copies(0)), "w1": lambda: start(video_copies(1)), "w2": lambda: start(video_copies(2)),
    }
    for t, name in enumerate("QKV"):
        for stage in range(4):
            steps[f"{stage + 1}{name}"] = lambda t=t, stage=stage: take(t, stage)
    for half in range(2):
        steps[f"p{half}"] = lambda half=half: place_all(half)
        steps[f"r1_{half}"] = lambda half=half: reduce_start(half)
        steps[f"r2_{half}"] = lambda half=half: reduce_pass(half)
        steps[f"ca_{half}"] = lambda half=half: reduce_cross(half)
        steps[f"cb_{half}"] = lambda half=half: reduce_cross_pass(half)
        steps[f"o_{half}"] = lambda half=half: finish_half(half)

    parts = {"": [], "A": [], "B": [], "X": [], "T": [], "Y": []}
    part_now, at = "", None
    for name in ORDER:
        if isinstance(name, int):
            at = name
        elif name in parts:
            part_now, at = name, None
        else:
            parts[part_now].append((at, steps[name]))

    def run(name):
        for _, step in parts[name]:
            step()

    run("")
    ready_audio()
    audio(parts["A"])
    run("B")
    ready_video()
    video_weights(parts["X"])
    run("T")
    video_values(parts["Y"])

    for t in range(4):
        sent(x_step(t))
        for stage in range(4):
            sent(gather(t, stage))
    for i in range(3):
        swap(i)[0].wait_send()
    swap_marks().wait_send()
    for half in range(2):
        sent(reduce1(half))
        sent(reduce2(half))
        sent(results(half))
        for cc in (0, 1):
            mine = pl.ds(cc * 768 + half * 384, 384)
            remote(
                ao.at[pl.ds(0, 64), pl.ds(half * 384, 384)], aout_hbm.at[:, mine], o_send.at[half, 0],
                o_recv.at[half, cc], result_low,
            ).wait_recv()
    for i in range(3):
        away, here = video_copies(i)
        here.wait()
        away.wait()


def on_device(video_q, video_k, video_v, audio_q, audio_k, audio_v, video_clip, audio_clip):
    anywhere = pl.BlockSpec(memory_space=pl.ANY)
    dma = pltpu.SemaphoreType.DMA
    return pl.pallas_call(
        kernel,
        out_shape=(
            jax.ShapeDtypeStruct(video_q.shape, BF),
            jax.ShapeDtypeStruct(audio_k.shape, BF),
        ),
        in_specs=[
            pl.BlockSpec(memory_space=pltpu.SMEM),
            pl.BlockSpec(memory_space=pltpu.VMEM),
            pl.BlockSpec(memory_space=pltpu.VMEM),
        ]
        + [anywhere] * 6,
        out_specs=(anywhere, anywhere),
        scratch_shapes=[
            pltpu.VMEM((1024, 768), BF),
            pltpu.VMEM((1024, 768), BF),
            pltpu.VMEM((1024, 768), BF),
            pltpu.VMEM((1024, HD), BF),
            pltpu.VMEM((2, 4, 4, 64, 768), BF),
            pltpu.VMEM((2, 4, 4, 64, 768), BF),
            pltpu.VMEM((2, 4, 4, 64, 768), BF),
            pltpu.VMEM((2, 4, 4, 32, HD), BF),
            pltpu.VMEM((2, 4, 4, 64, HD), BF),
            pltpu.VMEM((32, HD), BF),
            pltpu.VMEM((640, 1024), F32),
            pltpu.VMEM((640, 1024), F32),
            pltpu.VMEM((640, 1024), BF),
            pltpu.VMEM((640, 1024), BF),
            pltpu.VMEM((640, HD), F32),
            pltpu.VMEM((640, HD), F32),
            pltpu.VMEM((512, BLOCKS * HD), F32),
            pltpu.VMEM((512, BLOCKS * HD), F32),
            pltpu.VMEM((12, 512, BLOCKS * HD), BF),
            pltpu.VMEM((6, BLOCKS, 8, HD), F32),
            pltpu.VMEM((6, BLOCKS, 8, HD), F32),
            pltpu.VMEM((2, BLOCKS, STAT, HD), BF),
            pltpu.VMEM((2, 4, 4, ROWS, HD), BF),
            pltpu.VMEM((2, 6, 2, ROWS, HD), BF),
            pltpu.VMEM((2, 3, ROWS, HD), BF),
            pltpu.VMEM((1024, 768), BF),
            pltpu.VMEM((HD, 768), BF),
            dma((4, 2)),
            dma((4, 2)),
            dma((4, 16)),
            dma((4, 16)),
            dma((4,)),
            dma((4,)),
            dma((3,)),
            dma((2, 9)),
            dma((2, 9)),
            dma((2, 2)),
            dma((2, 2)),
            dma((3,)),
            dma((3,)),
            dma((3,)),
        ],
        compiler_params=pltpu.CompilerParams(
            collective_id=0, has_side_effects=True, vmem_limit_bytes=60 * 1024 * 1024
        ),
    )(
        video_clip, video_clip.reshape(4, HD), audio_clip.reshape(1, 64), video_q, video_k, video_v, audio_q, audio_k,
        audio_v,
    )


def solution(mesh):
    spread = P(("grp", "seq"), None)
    return jax.shard_map(
        on_device,
        mesh=mesh,
        in_specs=(spread,) * 6 + (P(("grp", "seq")),) * 2,
        out_specs=(spread, spread),
        check_vma=False,
    )
```

```python
import functools
import math

import jax
import jax.numpy as jnp
from jax import lax
from jax.experimental import pallas as pl
from jax.experimental.pallas import tpu as pltpu
from jax.sharding import PartitionSpec as P

MESH = pl.DeviceIdType.MESH
BF = jnp.bfloat16
F32 = jnp.float32
HD = 128
CLIPS = 9
SCALE = math.log2(math.e) / math.sqrt(HD)
FAR = -1048576.0
LOW = -32768.0
BLOCKS = 10
STAT = 3 * HD
ROWS = STAT + 16


ORDER = (
    "1Q0", "sQ1", "2Q0", "sK0", "1Q1", "3Q0", "2Q1", "sK1", "1K0", "3Q1", "4Q0", "sV0", "1K1", "1V0", "2K0",
    "sV1", "4Q1", "ex", "A", -2, "2K1", -1, "1V1", "2V0", "3K0", "vqs", 2, "2V1", "3K1", "rQ1", 3, "3V0", 5,
    "4K0", 6, "p0", 8, "4K1", "r1_0", "B", "p1", "r1_1", "X", -1, "rK1", 3, "3V1", "r2_0", "4V0", 6, "r2_1",
    10, "ca_0", "4V1", "tw0", "T", "ca_1", "Y", 1, "cb_0", 2, "w0", "cb_1", "tw1", 3, "o_0", "w1", 4, "o_1",
    5, "w2",
)


def kernel(
    clip_smem, video_clip, audio_clip, vq_hbm, vk_hbm, vv_hbm, aq_hbm, ak_hbm, av_hbm,
    vout_hbm, aout_hbm,
    vq, vk, vv, ve, aq0, aq1, ak0, ak1, av0, av1, mk, am, mk_own, buf_c, buf_d, wt_c, wt_d, high_c, high_d, buf_a, buf_b, wb, tops, sums, window, part, got1, got2, vo, ao,
    x_send, x_recv, g_send, g_recv, v_send, v_recv, v_local, r_send, r_recv, o_send, o_recv, w_send, w_recv, w_local,
):
    g = lax.axis_index("grp")
    s = lax.axis_index("seq")
    core = lax.rem(s, 2)
    chip = s // 2
    z, y = chip // 4, lax.rem(chip, 4)
    zp, zm, z2 = lax.rem(z + 1, 4), lax.rem(z + 3, 4), lax.rem(z + 2, 4)
    yp, ym, y2 = lax.rem(y + 1, 4), lax.rem(y + 3, 4), lax.rem(y + 2, 4)
    gp, gm = lax.rem(g + 1, 4), lax.rem(g + 3, 4)

    def device(grp, zz, yy, cc):
        return (grp, (zz * 4 + yy) * 2 + cc)

    other = device(g, z, y, 1 - core)
    to_yp, to_ym = (device(g, z, b, core) for b in (yp, ym))
    to_zp, to_zm = (device(g, b, y, core) for b in (zp, zm))
    before = lax.rem(chip + 15, 16)
    after = lax.rem(chip + 1, 16)
    result_low = (gp, chip * 2)
    result_high = (gp, before * 2 + 1)

    barrier = pltpu.get_barrier_semaphore()

    def greet(dev):
        pl.semaphore_signal(barrier, inc=1, device_id=dev, device_id_type=MESH)

    for dev in (other, to_yp, to_ym, to_zp, to_zm):
        greet(dev)
    for cc in (0, 1):
        greet(device(gm, z, y, cc))
        greet(device(gp, z, y, cc))
    greet(result_high)

    @pl.when(core == 1)
    def _():
        greet((gm, after * 2))
        greet((gm, after * 2 + 1))

    pl.semaphore_wait(barrier, 10 + 2 * core)

    def remote(src, dst, ssem, rsem, dev):
        return pltpu.make_async_remote_copy(
            src_ref=src, dst_ref=dst, send_sem=ssem, recv_sem=rsem, device_id=dev, device_id_type=MESH
        )

    def columns(half, width):
        return pl.ds(pl.multiple_of(half * width, 128), width)

    aq, ak, av = (aq0, aq1), (ak0, ak1), (av0, av1)
    tensors = [(src, dst[half], half) for src, dst in ((aq_hbm, aq), (ak_hbm, ak), (av_hbm, av)) for half in (0, 1)]
    tensors.append((mk_own, mk, None))

    def x_copies(t, sender):
        src, dst, half = tensors[t]
        return [
            remote(
                src if half is None else src.at[:, pl.ds(cc * 768 + half * 384, 384)], dst.at[sender, z, y], x_send.at[t, cc],
                x_recv.at[t, sender], device(gm, z, y, cc),
            )
            for cc in (0, 1)
        ]

    def x_step(t):
        return x_copies(t, core)

    here_already = set()

    def x_wait(t):
        if t in here_already:
            return
        here_already.add(t)
        for cc in (0, 1):
            x_copies(t, cc)[0].wait_recv()

    def gather(t, stage):
        x = tensors[t][1]
        rows = 16 if t == 6 else 32
        low, high = pl.ds(0, rows), pl.ds(rows, rows)
        first, last = pl.ds(0, 2), pl.ds(2, 2)
        plan = (
            (x.at[0, z, y], to_yp),
            (x.at[0, z, y], to_ym),
            (x.at[1, z, y], to_zp),
            (x.at[1, z, y], to_zm),
        ), (
            (x.at[0, z, ym, low], to_yp),
            (x.at[0, z, yp, high], to_ym),
            (x.at[1, zm, y, low], to_zp),
            (x.at[1, zp, y, high], to_zm),
        ), (
            (x.at[0, z], to_zp),
            (x.at[0, z], to_zm),
            (x.at[1, :, y], to_yp),
            (x.at[1, :, y], to_ym),
        ), (
            (x.at[0, zm, first], to_zp),
            (x.at[0, zp, last], to_zm),
            (x.at[1, first, ym], to_yp),
            (x.at[1, last, yp], to_ym),
        )
        return [
            remote(ref, ref, g_send.at[t, stage * 4 + i], g_recv.at[t, stage * 4 + i], dev)
            for i, (ref, dev) in enumerate(plan[stage])
        ]

    def start(copies):
        for copy in copies:
            copy.start()

    def arrive(copies):
        for copy in copies:
            copy.wait_recv()

    def sent(copies):
        for copy in copies:
            copy.wait_send()

    video = ((vk_hbm, vk), (vv_hbm, vv), (vq_hbm, vq))
    own_rows = pl.ds(pl.multiple_of(core * 512, 512), 512)
    other_rows = pl.ds(pl.multiple_of((1 - core) * 512, 512), 512)

    def swap(i):
        src, dst = video[i]
        return (
            remote(src.at[:, columns(1 - core, 768)], dst.at[own_rows], v_send.at[i], v_recv.at[i], other),
            pltpu.make_async_copy(src.at[:, columns(core, 768)], dst.at[own_rows], v_local.at[i]),
        )

    def swap_start(i):
        away, here = swap(i)
        away.start()
        here.start()

    def swap_wait(i):
        away, here = swap(i)
        away.wait_recv()
        here.wait()

    def swap_marks():
        return remote(ve.at[own_rows], ve.at[own_rows], v_send.at[3], v_recv.at[3], other)

    start(x_step(0))
    swap_start(0)
    swap_start(1)

    numbers = (audio_clip[...] - gm * CLIPS).astype(F32)
    numbers = jnp.concatenate([numbers, numbers], axis=1)
    mk_own[...] = jnp.broadcast_to(numbers, (32, HD)).astype(BF)
    start(x_step(6))
    clips = lax.broadcasted_iota(jnp.int32, (HD, HD), 0)
    for i in range(4):
        same = video_clip[i : i + 1, :] - g * CLIPS == clips
        at = pl.multiple_of(core * 512 + i * HD, HD)
        ve[pl.ds(at, HD), :] = jnp.where(same, 0.0, FAR).T.astype(BF)
    swap_marks().start()

    lanes = clips.astype(F32)

    def expand(i, carry):
        bz, by = i // 4, lax.rem(i, 4)
        for cc in (0, 1):
            numbers = mk[cc, bz, by, pl.ds(0, 16), :].astype(F32)[0:1]
            am[cc, bz, by] = jnp.where(numbers == lanes, 1.0, 0.0).T[0:64].astype(BF)
        return carry

    first = jnp.where(core == 0, clip_smem[0], clip_smem[511] - 1) - g * CLIPS

    def block(i):
        return jnp.bitwise_and(first + i, 15)

    def pieces(ref, i, h):
        b, a = block(i - 1), block(i)
        where = (1, b // 4, jnp.bitwise_and(b, 3)), (0, a // 4, jnp.bitwise_and(a, 3))
        if h is None:
            return [ref[at] for at in where]
        cols = pl.ds(pl.multiple_of(lax.rem(h, 3) * HD, HD), HD)
        return [ref[(*at, slice(None), cols)] for at in where]

    def packed(top, total):
        high = total.astype(BF).astype(F32)
        gap = jnp.zeros((1, HD), F32)
        return jnp.concatenate([top, gap, total - high, gap, high, jnp.zeros((5, HD), F32)], axis=0)

    lane = lax.broadcasted_iota(jnp.int32, (HD, HD), 1)

    def audio_step(unit_scores, unit_weights, unit_values):
        if unit_scores is not None:
            u, buf, ref = unit_scores
            cols = pl.ds(pl.multiple_of(u // 2 * HD, HD), HD)
            blocks = [5 * lax.rem(u, 2) + i for i in range(5)]
            q = jnp.concatenate([piece for i in blocks for piece in pieces(ref, i, u // 2)], axis=0)
            mark = jnp.concatenate([piece for i in blocks for piece in pieces(am, i, None)], axis=0)
            q = jnp.concatenate([q, mark], axis=1)
        if unit_values is not None:
            h, tile, weights, high = unit_values[0] // 2, lax.rem(unit_values[0], 2), unit_values[1], unit_values[2]
            v = jnp.concatenate([vv[:, pl.ds(pl.multiple_of(h * HD, HD), HD)], jnp.ones((1024, HD), BF)], axis=1)
            out = jnp.dot(weights[...], v, preferred_element_type=F32)
        row = 0
        for c in range(4):
            if unit_scores is not None:
                rows = pl.ds(c * 256, 256)
                k = jnp.concatenate([vk[rows, cols], ve[rows, :]], axis=1)
                buf[:, c * 256 : (c + 1) * 256] = lax.dot_general(
                    q, k, (((1,), (1,)), ((), ())), preferred_element_type=F32
                )
            if unit_weights is not None:
                scores_w, weights_w, high_w = unit_weights
                for _ in range(10):
                    scores = scores_w[row : row + 16, :]
                    top = jnp.maximum(jnp.max(scores, axis=1, keepdims=True) * SCALE, LOW).astype(BF).astype(F32)
                    weights_w[row : row + 16, :] = jnp.exp2(scores * SCALE - top).astype(BF)
                    high_w[row : row + 16, :] = jnp.broadcast_to(top, (16, HD))
                    row += 16
        if unit_values is not None:
            where = pl.ds(pl.multiple_of(lax.rem(h, 3) * HD, HD), HD)
            for b in range(5):
                rows = slice(b * HD, (b + 1) * HD)
                window[h // 3, 5 * tile + b, where, :] = out[rows, :HD].T.astype(BF)
                stats = jnp.where(lane < 8, high[rows, :], out[rows, HD:]).T
                tops[h, 5 * tile + b] = stats[0:8]
                sums[h, 5 * tile + b] = stats[8:16]

    def audio(events):
        even, odd = (buf_c, wt_c, high_c), (buf_d, wt_d, high_d)

        def body(ref, lo, hi, i, carry):
            u = 2 * i
            audio_step((u + 2, buf_c, ref), odd, (u, wt_c, high_c))
            run_events(u, events, range(lo, hi, 2))
            audio_step((u + 3, buf_d, ref), even, (u + 1, wt_d, high_d))
            run_events(u + 1, events, range(lo + 1, hi, 2))
            return carry

        audio_step((0, buf_c, aq[0]), None, None)
        run_now(-2, events)
        audio_step((1, buf_d, aq[0]), even, None)
        run_now(-1, events)
        lax.fori_loop(0, 2, functools.partial(body, aq[0], 0, 4), 0)
        lax.fori_loop(2, 5, functools.partial(body, aq[1], 4, 10), 0)
        audio_step(None, odd, (10, wt_c, high_c))
        audio_step(None, None, (11, wt_d, high_d))

    def run_now(at, events):
        for where, event in events:
            if where == at:
                event()

    def run_events(i, events, steps_here):
        for at in sorted({at for at, _ in events if at in steps_here}):

            @pl.when(i == at)
            def _():
                run_now(at, events)

    empty = jnp.where(lax.broadcasted_iota(jnp.int32, (16, HD), 0) < 3, LOW, 0.0)

    def place_block(half, b):
        at = jnp.bitwise_and(b - first, 15)
        inside = (at < BLOCKS).astype(F32)
        at = jnp.minimum(at, BLOCKS - 1)
        bz, by = b // 4, lax.rem(b, 4)
        body = window[half, at, :, :].astype(F32)
        part[half, bz, by, pl.ds(0, STAT), :] = (body * inside).astype(BF)
        top = jnp.concatenate([tops[half * 3 + hh, at][0:1] for hh in range(3)], axis=0)
        total = jnp.concatenate([sums[half * 3 + hh, at][0:1] for hh in range(3)], axis=0)
        stats = packed(top, total)
        part[half, bz, by, pl.ds(STAT, 16), :] = (stats * inside + empty * (1.0 - inside)).astype(BF)

    def place_all(half):
        def body(b, carry):
            place_block(half, b)
            return carry

        lax.fori_loop(0, 16, body, 0)

    def slab(half, where, lo):
        if half == 0:
            return part.at[0, where, pl.ds(lo, 2)]
        return part.at[1, pl.ds(lo, 2), where]

    axes = ((z, zp, zm, z2, to_zp, to_zm), (y, yp, ym, y2, to_yp, to_ym))
    turn_by = 1 + 2 * core

    def cross(at, two):
        p, m = lax.rem(at + turn_by, 4), lax.rem(at + 4 - turn_by, 4)
        return at, p, m, two

    crosses = (cross(y, y2), cross(z, z2))

    def reduce1(half):
        _, p, m, two, to_p, to_m = axes[half]
        plan = (
            (slab(half, two, 0), to_p), (slab(half, two, 2), to_m),
            (slab(half, p, 2), to_p), (slab(half, m, 0), to_m),
            (slab(half, p, 0), to_p), (slab(half, m, 2), to_m),
        )
        return [
            remote(ref, got1.at[half, i], r_send.at[half, i], r_recv.at[half, i], dev)
            for i, (ref, dev) in enumerate(plan)
        ]

    def one(half, u):
        if half == 0:
            return part.at[0, z, u]
        return part.at[1, u, y]

    def reduce2(half):
        _, p, m, two = crosses[half]
        to_p, to_m = (device(g, z, u, core) if half == 0 else device(g, u, y, core) for u in (p, m))
        return [
            remote(one(half, u), got2.at[half, i], r_send.at[half, 6 + i], r_recv.at[half, 6 + i], dev)
            for i, (u, dev) in enumerate(((two, to_p), (m, to_m), (p, to_p)))
        ]

    def merged(refs):
        stats = [ref[pl.ds(STAT, 16), :].astype(F32) for ref in refs]
        tops = [x[0:3] for x in stats]
        top = tops[0]
        for x in tops[1:]:
            top = jnp.maximum(top, x)
        factors = [jnp.exp2(x - top) for x in tops]
        total = sum((x[8:11] + x[4:7]) * f for x, f in zip(stats, factors))
        outs = [
            sum(ref[pl.ds(hh * HD, HD), :].astype(F32) * f[hh : hh + 1] for ref, f in zip(refs, factors))
            for hh in range(3)
        ]
        return outs, top, total

    def merge_into(target, sources):
        outs, top, total = merged([target] + sources)
        for hh in range(3):
            target[pl.ds(hh * HD, HD), :] = outs[hh].astype(BF)
        target[pl.ds(STAT, 16), :] = packed(top, total).astype(BF)

    def merge_slab(half, where, lo, slots):
        def body(i, carry):
            target = part.at[0, where, lo + i] if half == 0 else part.at[1, lo + i, where]
            merge_into(target, [got1.at[half, slot, i] for slot in slots])
            return carry

        lax.fori_loop(0, 2, body, 0)

    def reduce_start(half):
        start(reduce1(half)[:4])

    def reduce_pass(half):
        _, p, m, *_ = axes[half]
        copies = reduce1(half)
        copies[0].wait_recv()
        merge_slab(half, p, 0, (0,))
        copies[4].start()
        copies[1].wait_recv()
        merge_slab(half, m, 2, (1,))
        copies[5].start()

    def reduce_cross(half):
        own = axes[half][0]
        arrive(reduce1(half)[2:])
        merge_slab(half, own, 0, (3, 4))
        merge_slab(half, own, 2, (2, 5))
        start(reduce2(half)[:2])

    def reduce_cross_pass(half):
        copies = reduce2(half)
        copies[0].wait_recv()
        merge_into(one(half, crosses[half][1]), [got2.at[half, 0]])
        copies[2].start()

    def reduce_end(half):
        own = crosses[half][0]
        arrive(reduce2(half)[1:])
        outs, _, total = merged([one(half, own)] + [got2.at[half, i] for i in (1, 2)])
        scale = 1.0 / total
        for hh in range(3):
            done = (outs[hh] * scale[hh : hh + 1]).T
            ao[:, pl.ds((half * 3 + hh) * HD, HD)] = done.astype(BF)

    def results(half):
        mine = pl.ds(pl.multiple_of(core * 768 + half * 384, 128), 384)
        cols = pl.ds(half * 384, 384)
        return [
            remote(
                ao.at[rows, cols], aout_hbm.at[:, mine], o_send.at[half, i], o_recv.at[half, core], dev
            )
            for i, (rows, dev) in enumerate(((pl.ds(64, 64), result_low), (pl.ds(0, 64), result_high)))
        ]

    def rows_of(ref, i, h):
        return jnp.concatenate(pieces(ref, 2 * i, h) + pieces(ref, 2 * i + 1, h), axis=0)

    def video_unit(u):
        cols = pl.ds(pl.multiple_of(u // 2 * HD, HD), HD)
        return cols, pl.ds(pl.multiple_of(lax.rem(u, 2) * 512, 512), 512)

    def video_both(u_scores, ref, u_out, buf_scores, buf_out):
        cols, here = video_unit(u_scores)
        q = jnp.concatenate([vq[here, cols], ve[here, :]], axis=1)
        row = 0
        for c in range(5):
            k = jnp.concatenate([rows_of(ref, c, u_scores // 2), rows_of(am, c, None)], axis=1)
            buf_scores[:, c * 256 : (c + 1) * 256] = lax.dot_general(
                q, k, (((1,), (1,)), ((), ())), preferred_element_type=F32
            )
            if u_out is not None:
                for _ in range(7 if c < 2 else 6):
                    scores = buf_out[row : row + 16, :]
                    top = jnp.max(scores, axis=1, keepdims=True) * SCALE
                    wb[u_out, row : row + 16, :] = jnp.exp2(scores * SCALE - top).astype(BF)
                    row += 16

    def video_weights(events):
        def body(refs, lo, hi, i, carry):
            u = 2 * i
            video_both(u + 1, refs[0], u, buf_b, buf_a)
            run_events(u, events, range(lo, hi, 2))
            video_both(jnp.minimum(u + 2, 11), refs[1], u + 1, buf_a, buf_b)
            run_events(u + 1, events, range(lo + 1, hi, 2))
            return carry

        video_both(0, ak[0], None, buf_a, None)
        run_now(-1, events)
        lax.fori_loop(0, 2, functools.partial(body, (ak[0], ak[0]), 0, 4), 0)
        lax.fori_loop(2, 3, functools.partial(body, (ak[0], ak[1]), 4, 6), 0)
        lax.fori_loop(3, 6, functools.partial(body, (ak[1], ak[1]), 6, 12), 0)

    def video_values(events):
        def body(ref, lo, hi, i, carry):
            cols, _ = video_unit(2 * i)
            v = jnp.concatenate([rows_of(ref, c, i) for c in range(5)], axis=0)
            v = jnp.concatenate([v, jnp.ones((BLOCKS * HD, HD), BF)], axis=1)
            for j in range(2):
                out = jnp.dot(wb[2 * i + j], v, preferred_element_type=F32)
                vo[pl.ds(j * 512, 512), cols] = (out[:, :HD] / out[:, HD:]).astype(BF)
            run_events(i, events, range(lo, hi))
            return carry

        lax.fori_loop(0, 3, functools.partial(body, av[0], 0, 3), 0)
        lax.fori_loop(3, 6, functools.partial(body, av[1], 3, 6), 0)

    def video_copies(i):
        cols = pl.ds(i * 256, 256)
        mine = pl.ds(pl.multiple_of(core * 768 + i * 256, 128), 256)
        return (
            remote(vo.at[other_rows, cols], vout_hbm.at[:, mine], w_send.at[i], w_recv.at[i], other),
            pltpu.make_async_copy(vo.at[own_rows, cols], vout_hbm.at[:, mine], w_local.at[i]),
        )

    def take(t, stage):
        for tensor in (6, 0) if t == 0 else (t,):
            if stage == 0:
                x_wait(tensor)
            else:
                arrive(gather(tensor, stage - 1))
            start(gather(tensor, stage))

    def x_next(t):
        x_wait(t - 1)
        start(x_step(t))

    def make_marks():
        arrive(gather(6, 3))
        lax.fori_loop(0, 16, expand, 0)

    def ready_audio():
        swap_wait(0)
        swap_wait(1)
        swap_marks().wait_recv()
        arrive(gather(0, 3))

    def ready_video():
        swap_wait(2)
        arrive(gather(2, 3))

    def finish_half(half):
        reduce_end(half)
        start(results(half))

    steps = {
        "vqs": lambda: swap_start(2), "ex": make_marks, "rQ1": lambda: arrive(gather(1, 3)), "rK1": lambda: arrive(gather(3, 3)),
        "tw0": lambda: arrive(gather(4, 3)), "tw1": lambda: arrive(gather(5, 3)),
        "w0": lambda: start(video_copies(0)), "w1": lambda: start(video_copies(1)), "w2": lambda: start(video_copies(2)),
    }
    for t, name in enumerate(("Q0", "Q1", "K0", "K1", "V0", "V1")):
        steps[f"s{name}"] = lambda t=t: x_next(t)
        for stage in range(4):
            steps[f"{stage + 1}{name}"] = lambda t=t, stage=stage: take(t, stage)
    for half in range(2):
        steps[f"p{half}"] = lambda half=half: place_all(half)
        steps[f"r1_{half}"] = lambda half=half: reduce_start(half)
        steps[f"r2_{half}"] = lambda half=half: reduce_pass(half)
        steps[f"ca_{half}"] = lambda half=half: reduce_cross(half)
        steps[f"cb_{half}"] = lambda half=half: reduce_cross_pass(half)
        steps[f"o_{half}"] = lambda half=half: finish_half(half)

    parts = {"": [], "A": [], "B": [], "X": [], "T": [], "Y": []}
    part_now, at = "", None
    for name in ORDER:
        if isinstance(name, int):
            at = name
        elif name in parts:
            part_now, at = name, None
        else:
            parts[part_now].append((at, steps[name]))

    def run(name):
        for _, step in parts[name]:
            step()

    run("")
    ready_audio()
    audio(parts["A"])
    run("B")
    ready_video()
    video_weights(parts["X"])
    run("T")
    video_values(parts["Y"])

    for t in range(7):
        sent(x_step(t))
        for stage in range(4):
            sent(gather(t, stage))
    for i in range(3):
        swap(i)[0].wait_send()
    swap_marks().wait_send()
    for half in range(2):
        sent(reduce1(half))
        sent(reduce2(half))
        sent(results(half))
        for cc in (0, 1):
            mine = pl.ds(cc * 768 + half * 384, 384)
            remote(
                ao.at[pl.ds(0, 64), pl.ds(half * 384, 384)], aout_hbm.at[:, mine], o_send.at[half, 0],
                o_recv.at[half, cc], result_low,
            ).wait_recv()
    for i in range(3):
        away, here = video_copies(i)
        here.wait()
        away.wait()


def on_device(video_q, video_k, video_v, audio_q, audio_k, audio_v, video_clip, audio_clip):
    anywhere = pl.BlockSpec(memory_space=pl.ANY)
    dma = pltpu.SemaphoreType.DMA
    return pl.pallas_call(
        kernel,
        out_shape=(
            jax.ShapeDtypeStruct(video_q.shape, BF),
            jax.ShapeDtypeStruct(audio_k.shape, BF),
        ),
        in_specs=[
            pl.BlockSpec(memory_space=pltpu.SMEM),
            pl.BlockSpec(memory_space=pltpu.VMEM),
            pl.BlockSpec(memory_space=pltpu.VMEM),
        ]
        + [anywhere] * 6,
        out_specs=(anywhere, anywhere),
        scratch_shapes=[
            pltpu.VMEM((1024, 768), BF),
            pltpu.VMEM((1024, 768), BF),
            pltpu.VMEM((1024, 768), BF),
            pltpu.VMEM((1024, HD), BF),
            pltpu.VMEM((2, 4, 4, 64, 384), BF),
            pltpu.VMEM((2, 4, 4, 64, 384), BF),
            pltpu.VMEM((2, 4, 4, 64, 384), BF),
            pltpu.VMEM((2, 4, 4, 64, 384), BF),
            pltpu.VMEM((2, 4, 4, 64, 384), BF),
            pltpu.VMEM((2, 4, 4, 64, 384), BF),
            pltpu.VMEM((2, 4, 4, 32, HD), BF),
            pltpu.VMEM((2, 4, 4, 64, HD), BF),
            pltpu.VMEM((32, HD), BF),
            pltpu.VMEM((640, 1024), F32),
            pltpu.VMEM((640, 1024), F32),
            pltpu.VMEM((640, 1024), BF),
            pltpu.VMEM((640, 1024), BF),
            pltpu.VMEM((640, HD), F32),
            pltpu.VMEM((640, HD), F32),
            pltpu.VMEM((512, BLOCKS * HD), F32),
            pltpu.VMEM((512, BLOCKS * HD), F32),
            pltpu.VMEM((12, 512, BLOCKS * HD), BF),
            pltpu.VMEM((6, BLOCKS, 8, HD), F32),
            pltpu.VMEM((6, BLOCKS, 8, HD), F32),
            pltpu.VMEM((2, BLOCKS, STAT, HD), BF),
            pltpu.VMEM((2, 4, 4, ROWS, HD), BF),
            pltpu.VMEM((2, 6, 2, ROWS, HD), BF),
            pltpu.VMEM((2, 3, ROWS, HD), BF),
            pltpu.VMEM((1024, 768), BF),
            pltpu.VMEM((HD, 768), BF),
            dma((7, 2)),
            dma((7, 2)),
            dma((7, 16)),
            dma((7, 16)),
            dma((4,)),
            dma((4,)),
            dma((3,)),
            dma((2, 9)),
            dma((2, 9)),
            dma((2, 2)),
            dma((2, 2)),
            dma((3,)),
            dma((3,)),
            dma((3,)),
        ],
        compiler_params=pltpu.CompilerParams(
            collective_id=0, has_side_effects=True, vmem_limit_bytes=60 * 1024 * 1024
        ),
    )(
        video_clip, video_clip.reshape(4, HD), audio_clip.reshape(1, 64), video_q, video_k, video_v, audio_q, audio_k,
        audio_v,
    )


def solution(mesh):
    spread = P(("grp", "seq"), None)
    return jax.shard_map(
        on_device,
        mesh=mesh,
        in_specs=(spread,) * 6 + (P(("grp", "seq")),) * 2,
        out_specs=(spread, spread),
        check_vma=False,
    )
```

```python
import functools
import math

import jax
import jax.numpy as jnp
from jax import lax
from jax.experimental import pallas as pl
from jax.experimental.pallas import tpu as pltpu
from jax.sharding import PartitionSpec as P

MESH = pl.DeviceIdType.MESH
BF = jnp.bfloat16
F32 = jnp.float32
HD = 128
CLIPS = 9
SCALE = math.log2(math.e) / math.sqrt(HD)
FAR = -1048576.0
LOW = -32768.0
BLOCKS = 10
STAT = 3 * HD
ROWS = STAT + 16


ORDER = (
    "1Q0", "sQ1", "fV", "2Q0", "1Q1", "sK0", "3Q0", "sK1", "2Q1", "1K0", "3Q1", "1K1", "4Q0", "sV0", "2K0",
    "4Q1", "vqs", "2K1", "ex", "A", -2, "3K0", -1, "rQ1", 1, "3K1", 5, "4K0", 6, "3V0", "p0", "4K1", 7,
    "sV1", "r1_0", "B", "p1", "r1_1", "X", 3, "3V1", 4, "rK1", 5, "r2_0", "r2_1", 10, "4V0", "ca_0", "ca_1",
    "T", "4V1", "tw0", "Y", 1, "w0", "cb_0", 2, "cb_1", "tw1", 3, "w1", "o_0", 5, "w2", "o_1",
)


def kernel(
    clip_smem, video_clip, audio_clip, vq_hbm, vk_hbm, vv_hbm, aq_hbm, ak_hbm, av_hbm,
    vout_hbm, aout_hbm,
    vq, vk, vv, ve, aq0, aq1, ak0, ak1, av0, av1, v_row, mk, am, mk_own, buf_c, buf_d, wt_c, wt_d, high_c, high_d, buf_a, buf_b, wb, tops, sums, window, part, got1, got2, vo, ao,
    x_send, x_recv, p_send, p_recv, p_local, g_send, g_recv, v_send, v_recv, v_local, r_send, r_recv, o_send, o_recv, w_send, w_recv, w_local,
):
    g = lax.axis_index("grp")
    s = lax.axis_index("seq")
    core = lax.rem(s, 2)
    chip = s // 2
    z, y = chip // 4, lax.rem(chip, 4)
    zp, zm, z2 = lax.rem(z + 1, 4), lax.rem(z + 3, 4), lax.rem(z + 2, 4)
    yp, ym, y2 = lax.rem(y + 1, 4), lax.rem(y + 3, 4), lax.rem(y + 2, 4)
    gp, gm = lax.rem(g + 1, 4), lax.rem(g + 3, 4)

    def device(grp, zz, yy, cc):
        return (grp, (zz * 4 + yy) * 2 + cc)

    other = device(g, z, y, 1 - core)
    to_yp, to_ym = (device(g, z, b, core) for b in (yp, ym))
    to_zp, to_zm = (device(g, b, y, core) for b in (zp, zm))
    before = lax.rem(chip + 15, 16)
    after = lax.rem(chip + 1, 16)
    result_low = (gp, chip * 2)
    result_high = (gp, before * 2 + 1)

    barrier = pltpu.get_barrier_semaphore()

    def greet(dev):
        pl.semaphore_signal(barrier, inc=1, device_id=dev, device_id_type=MESH)

    for dev in (other, to_yp, to_ym, to_zp, to_zm):
        greet(dev)
    for cc in (0, 1):
        greet(device(gm, z, y, cc))
        greet(device(gp, z, y, cc))
    greet(result_high)

    @pl.when(core == 1)
    def _():
        greet((gm, after * 2))
        greet((gm, after * 2 + 1))

    pl.semaphore_wait(barrier, 10 + 2 * core)

    def remote(src, dst, ssem, rsem, dev):
        return pltpu.make_async_remote_copy(
            src_ref=src, dst_ref=dst, send_sem=ssem, recv_sem=rsem, device_id=dev, device_id_type=MESH
        )

    def columns(half, width):
        return pl.ds(pl.multiple_of(half * width, 128), width)

    aq, ak, av = (aq0, aq1), (ak0, ak1), (av0, av1)
    tensors = [(src, dst[half], half) for src, dst in ((aq_hbm, aq), (ak_hbm, ak), (av_hbm, av)) for half in (0, 1)]
    tensors.append((mk_own, mk, None))

    def along(on_y, on_z):
        return on_y * (1 - core) + on_z * core

    u, up, um = along(y, z), along(yp, zp), along(ym, zm)
    to_up = device(g, along(z, zp), along(yp, y), core)
    to_um = device(g, along(z, zm), along(ym, y), core)
    def ring(stage):
        src, row = av_hbm, v_row
        low, high = row.at[um, pl.ds(0, 32)], row.at[up, pl.ds(32, 32)]
        plan = ((src, row.at[u], to_up), (src, row.at[u], to_um)) if stage == 0 else ((low, low, to_up), (high, high, to_um))
        return [
            remote(a, b, p_send.at[2 * stage + n], p_recv.at[2 * stage + n], dev) for n, (a, b, dev) in enumerate(plan)
        ]

    def ring_own():
        return pltpu.make_async_copy(av_hbm, v_row.at[u], p_local)

    def x_copies(t, sender):
        src, dst, half = tensors[t]
        copies = []
        for cc in (0, 1):
            if half is None:
                a, b = src, dst.at[sender, z, y]
            elif t < 4:
                a, b = src.at[:, pl.ds(cc * 768 + half * 384, 384)], dst.at[sender, z, y]
            else:
                a = v_row.at[:, :, pl.ds(cc * 768 + half * 384, 384)]
                b = dst.at[0, z] if sender == 0 else dst.at[1, :, y]
            copies.append(remote(a, b, x_send.at[t, cc], x_recv.at[t, sender], device(gm, z, y, cc)))
        return copies

    def x_start(t):
        if t < 4 or t == 6:
            start(x_copies(t, core))
            return
        for cc in (0, 1):

            @pl.when(core == cc)
            def _():
                start(x_copies(t, cc))

    here_already = set()

    def x_wait(t):
        if t in here_already:
            return
        here_already.add(t)
        for cc in (0, 1):
            x_copies(t, cc)[0].wait_recv()

    def gather(t, stage):
        x = tensors[t][1]
        rows = 16 if t == 6 else 32
        low, high = pl.ds(0, rows), pl.ds(rows, rows)
        first, last = pl.ds(0, 2), pl.ds(2, 2)
        plan = (
            (x.at[0, z, y], to_yp),
            (x.at[0, z, y], to_ym),
            (x.at[1, z, y], to_zp),
            (x.at[1, z, y], to_zm),
        ), (
            (x.at[0, z, ym, low], to_yp),
            (x.at[0, z, yp, high], to_ym),
            (x.at[1, zm, y, low], to_zp),
            (x.at[1, zp, y, high], to_zm),
        ), (
            (x.at[0, z], to_zp),
            (x.at[0, z], to_zm),
            (x.at[1, :, y], to_yp),
            (x.at[1, :, y], to_ym),
        ), (
            (x.at[0, zm, first], to_zp),
            (x.at[0, zp, last], to_zm),
            (x.at[1, first, ym], to_yp),
            (x.at[1, last, yp], to_ym),
        )
        return [
            remote(ref, ref, g_send.at[t, stage * 4 + i], g_recv.at[t, stage * 4 + i], dev)
            for i, (ref, dev) in enumerate(plan[stage])
        ]

    def start(copies):
        for copy in copies:
            copy.start()

    def arrive(copies):
        for copy in copies:
            copy.wait_recv()

    def sent(copies):
        for copy in copies:
            copy.wait_send()

    video = ((vk_hbm, vk), (vv_hbm, vv), (vq_hbm, vq))
    own_rows = pl.ds(pl.multiple_of(core * 512, 512), 512)
    other_rows = pl.ds(pl.multiple_of((1 - core) * 512, 512), 512)

    def swap(i):
        src, dst = video[i]
        return (
            remote(src.at[:, columns(1 - core, 768)], dst.at[own_rows], v_send.at[i], v_recv.at[i], other),
            pltpu.make_async_copy(src.at[:, columns(core, 768)], dst.at[own_rows], v_local.at[i]),
        )

    def swap_start(i):
        away, here = swap(i)
        away.start()
        here.start()

    def swap_wait(i):
        away, here = swap(i)
        away.wait_recv()
        here.wait()

    def swap_marks():
        return remote(ve.at[own_rows], ve.at[own_rows], v_send.at[3], v_recv.at[3], other)

    x_start(0)
    start(ring(0))
    ring_own().start()
    swap_start(0)
    swap_start(1)

    numbers = (audio_clip[...] - gm * CLIPS).astype(F32)
    numbers = jnp.concatenate([numbers, numbers], axis=1)
    mk_own[...] = jnp.broadcast_to(numbers, (32, HD)).astype(BF)
    x_start(6)
    clips = lax.broadcasted_iota(jnp.int32, (HD, HD), 0)
    for i in range(4):
        same = video_clip[i : i + 1, :] - g * CLIPS == clips
        at = pl.multiple_of(core * 512 + i * HD, HD)
        ve[pl.ds(at, HD), :] = jnp.where(same, 0.0, FAR).T.astype(BF)
    swap_marks().start()

    lanes = clips.astype(F32)

    def expand(i, carry):
        bz, by = i // 4, lax.rem(i, 4)
        for cc in (0, 1):
            numbers = mk[cc, bz, by, pl.ds(0, 16), :].astype(F32)[0:1]
            am[cc, bz, by] = jnp.where(numbers == lanes, 1.0, 0.0).T[0:64].astype(BF)
        return carry

    first = jnp.where(core == 0, clip_smem[0], clip_smem[511] - 1) - g * CLIPS

    def block(i):
        return jnp.bitwise_and(first + i, 15)

    def pieces(ref, i, h):
        b, a = block(i - 1), block(i)
        where = (1, b // 4, jnp.bitwise_and(b, 3)), (0, a // 4, jnp.bitwise_and(a, 3))
        if h is None:
            return [ref[at] for at in where]
        cols = pl.ds(pl.multiple_of(lax.rem(h, 3) * HD, HD), HD)
        return [ref[(*at, slice(None), cols)] for at in where]

    def packed(top, total):
        high = total.astype(BF).astype(F32)
        gap = jnp.zeros((1, HD), F32)
        return jnp.concatenate([top, gap, total - high, gap, high, jnp.zeros((5, HD), F32)], axis=0)

    lane = lax.broadcasted_iota(jnp.int32, (HD, HD), 1)

    def audio_step(unit_scores, unit_weights, unit_values):
        if unit_scores is not None:
            u, buf, ref = unit_scores
            cols = pl.ds(pl.multiple_of(u // 2 * HD, HD), HD)
            blocks = [5 * lax.rem(u, 2) + i for i in range(5)]
            q = jnp.concatenate([piece for i in blocks for piece in pieces(ref, i, u // 2)], axis=0)
            mark = jnp.concatenate([piece for i in blocks for piece in pieces(am, i, None)], axis=0)
            q = jnp.concatenate([q, mark], axis=1)
        if unit_values is not None:
            h, tile, weights, high = unit_values[0] // 2, lax.rem(unit_values[0], 2), unit_values[1], unit_values[2]
            v = jnp.concatenate([vv[:, pl.ds(pl.multiple_of(h * HD, HD), HD)], jnp.ones((1024, HD), BF)], axis=1)
            out = jnp.dot(weights[...], v, preferred_element_type=F32)
        row = 0
        for c in range(4):
            if unit_scores is not None:
                rows = pl.ds(c * 256, 256)
                k = jnp.concatenate([vk[rows, cols], ve[rows, :]], axis=1)
                buf[:, c * 256 : (c + 1) * 256] = lax.dot_general(
                    q, k, (((1,), (1,)), ((), ())), preferred_element_type=F32
                )
            if unit_weights is not None:
                scores_w, weights_w, high_w = unit_weights
                for _ in range(10):
                    scores = scores_w[row : row + 16, :]
                    top = jnp.maximum(jnp.max(scores, axis=1, keepdims=True) * SCALE, LOW).astype(BF).astype(F32)
                    weights_w[row : row + 16, :] = jnp.exp2(scores * SCALE - top).astype(BF)
                    high_w[row : row + 16, :] = jnp.broadcast_to(top, (16, HD))
                    row += 16
        if unit_values is not None:
            where = pl.ds(pl.multiple_of(lax.rem(h, 3) * HD, HD), HD)
            for b in range(5):
                rows = slice(b * HD, (b + 1) * HD)
                window[h // 3, 5 * tile + b, where, :] = out[rows, :HD].T.astype(BF)
                stats = jnp.where(lane < 8, high[rows, :], out[rows, HD:]).T
                tops[h, 5 * tile + b] = stats[0:8]
                sums[h, 5 * tile + b] = stats[8:16]

    def audio(events):
        even, odd = (buf_c, wt_c, high_c), (buf_d, wt_d, high_d)

        def body(ref, lo, hi, i, carry):
            u = 2 * i
            audio_step((u + 2, buf_c, ref), odd, (u, wt_c, high_c))
            run_events(u, events, range(lo, hi, 2))
            audio_step((u + 3, buf_d, ref), even, (u + 1, wt_d, high_d))
            run_events(u + 1, events, range(lo + 1, hi, 2))
            return carry

        audio_step((0, buf_c, aq[0]), None, None)
        run_now(-2, events)
        audio_step((1, buf_d, aq[0]), even, None)
        run_now(-1, events)
        lax.fori_loop(0, 2, functools.partial(body, aq[0], 0, 4), 0)
        lax.fori_loop(2, 5, functools.partial(body, aq[1], 4, 10), 0)
        audio_step(None, odd, (10, wt_c, high_c))
        audio_step(None, None, (11, wt_d, high_d))

    def run_now(at, events):
        for where, event in events:
            if where == at:
                event()

    def run_events(i, events, steps_here):
        for at in sorted({at for at, _ in events if at in steps_here}):

            @pl.when(i == at)
            def _():
                run_now(at, events)

    empty = jnp.where(lax.broadcasted_iota(jnp.int32, (16, HD), 0) < 3, LOW, 0.0)

    def place_block(half, b):
        at = jnp.bitwise_and(b - first, 15)
        inside = (at < BLOCKS).astype(F32)
        at = jnp.minimum(at, BLOCKS - 1)
        bz, by = b // 4, lax.rem(b, 4)
        body = window[half, at, :, :].astype(F32)
        part[half, bz, by, pl.ds(0, STAT), :] = (body * inside).astype(BF)
        top = jnp.concatenate([tops[half * 3 + hh, at][0:1] for hh in range(3)], axis=0)
        total = jnp.concatenate([sums[half * 3 + hh, at][0:1] for hh in range(3)], axis=0)
        stats = packed(top, total)
        part[half, bz, by, pl.ds(STAT, 16), :] = (stats * inside + empty * (1.0 - inside)).astype(BF)

    def place_all(half):
        def body(b, carry):
            place_block(half, b)
            return carry

        lax.fori_loop(0, 16, body, 0)

    def slab(half, where, lo):
        if half == 0:
            return part.at[0, where, pl.ds(lo, 2)]
        return part.at[1, pl.ds(lo, 2), where]

    axes = ((z, zp, zm, z2, to_zp, to_zm), (y, yp, ym, y2, to_yp, to_ym))
    turn_by = 1 + 2 * core

    def cross(at, two):
        p, m = lax.rem(at + turn_by, 4), lax.rem(at + 4 - turn_by, 4)
        return at, p, m, two

    crosses = (cross(y, y2), cross(z, z2))

    def reduce1(half):
        _, p, m, two, to_p, to_m = axes[half]
        plan = (
            (slab(half, two, 0), to_p), (slab(half, two, 2), to_m),
            (slab(half, p, 2), to_p), (slab(half, m, 0), to_m),
            (slab(half, p, 0), to_p), (slab(half, m, 2), to_m),
        )
        return [
            remote(ref, got1.at[half, i], r_send.at[half, i], r_recv.at[half, i], dev)
            for i, (ref, dev) in enumerate(plan)
        ]

    def one(half, u):
        if half == 0:
            return part.at[0, z, u]
        return part.at[1, u, y]

    def reduce2(half):
        _, p, m, two = crosses[half]
        to_p, to_m = (device(g, z, u, core) if half == 0 else device(g, u, y, core) for u in (p, m))
        return [
            remote(one(half, u), got2.at[half, i], r_send.at[half, 6 + i], r_recv.at[half, 6 + i], dev)
            for i, (u, dev) in enumerate(((two, to_p), (m, to_m), (p, to_p)))
        ]

    def merged(refs):
        stats = [ref[pl.ds(STAT, 16), :].astype(F32) for ref in refs]
        tops = [x[0:3] for x in stats]
        top = tops[0]
        for x in tops[1:]:
            top = jnp.maximum(top, x)
        factors = [jnp.exp2(x - top) for x in tops]
        total = sum((x[8:11] + x[4:7]) * f for x, f in zip(stats, factors))
        outs = [
            sum(ref[pl.ds(hh * HD, HD), :].astype(F32) * f[hh : hh + 1] for ref, f in zip(refs, factors))
            for hh in range(3)
        ]
        return outs, top, total

    def merge_into(target, sources):
        outs, top, total = merged([target] + sources)
        for hh in range(3):
            target[pl.ds(hh * HD, HD), :] = outs[hh].astype(BF)
        target[pl.ds(STAT, 16), :] = packed(top, total).astype(BF)

    def merge_slab(half, where, lo, slots):
        def body(i, carry):
            target = part.at[0, where, lo + i] if half == 0 else part.at[1, lo + i, where]
            merge_into(target, [got1.at[half, slot, i] for slot in slots])
            return carry

        lax.fori_loop(0, 2, body, 0)

    def reduce_start(half):
        start(reduce1(half)[:4])

    def reduce_pass(half):
        _, p, m, *_ = axes[half]
        copies = reduce1(half)
        copies[0].wait_recv()
        merge_slab(half, p, 0, (0,))
        copies[4].start()
        copies[1].wait_recv()
        merge_slab(half, m, 2, (1,))
        copies[5].start()

    def reduce_cross(half):
        own = axes[half][0]
        arrive(reduce1(half)[2:])
        merge_slab(half, own, 0, (3, 4))
        merge_slab(half, own, 2, (2, 5))
        start(reduce2(half)[:2])

    def reduce_cross_pass(half):
        copies = reduce2(half)
        copies[0].wait_recv()
        merge_into(one(half, crosses[half][1]), [got2.at[half, 0]])
        copies[2].start()

    def reduce_end(half):
        own = crosses[half][0]
        arrive(reduce2(half)[1:])
        outs, _, total = merged([one(half, own)] + [got2.at[half, i] for i in (1, 2)])
        scale = 1.0 / total
        for hh in range(3):
            done = (outs[hh] * scale[hh : hh + 1]).T
            ao[:, pl.ds((half * 3 + hh) * HD, HD)] = done.astype(BF)

    def results(half):
        mine = pl.ds(pl.multiple_of(core * 768 + half * 384, 128), 384)
        cols = pl.ds(half * 384, 384)
        return [
            remote(
                ao.at[rows, cols], aout_hbm.at[:, mine], o_send.at[half, i], o_recv.at[half, core], dev
            )
            for i, (rows, dev) in enumerate(((pl.ds(64, 64), result_low), (pl.ds(0, 64), result_high)))
        ]

    def rows_of(ref, i, h):
        return jnp.concatenate(pieces(ref, 2 * i, h) + pieces(ref, 2 * i + 1, h), axis=0)

    def video_unit(u):
        cols = pl.ds(pl.multiple_of(u // 2 * HD, HD), HD)
        return cols, pl.ds(pl.multiple_of(lax.rem(u, 2) * 512, 512), 512)

    def video_both(u_scores, ref, u_out, buf_scores, buf_out):
        cols, here = video_unit(u_scores)
        q = jnp.concatenate([vq[here, cols], ve[here, :]], axis=1)
        row = 0
        for c in range(5):
            k = jnp.concatenate([rows_of(ref, c, u_scores // 2), rows_of(am, c, None)], axis=1)
            buf_scores[:, c * 256 : (c + 1) * 256] = lax.dot_general(
                q, k, (((1,), (1,)), ((), ())), preferred_element_type=F32
            )
            if u_out is not None:
                for _ in range(7 if c < 2 else 6):
                    scores = buf_out[row : row + 16, :]
                    top = jnp.max(scores, axis=1, keepdims=True) * SCALE
                    wb[u_out, row : row + 16, :] = jnp.exp2(scores * SCALE - top).astype(BF)
                    row += 16

    def video_weights(events):
        def body(refs, lo, hi, i, carry):
            u = 2 * i
            video_both(u + 1, refs[0], u, buf_b, buf_a)
            run_events(u, events, range(lo, hi, 2))
            video_both(jnp.minimum(u + 2, 11), refs[1], u + 1, buf_a, buf_b)
            run_events(u + 1, events, range(lo + 1, hi, 2))
            return carry

        video_both(0, ak[0], None, buf_a, None)
        run_now(-1, events)
        lax.fori_loop(0, 2, functools.partial(body, (ak[0], ak[0]), 0, 4), 0)
        lax.fori_loop(2, 3, functools.partial(body, (ak[0], ak[1]), 4, 6), 0)
        lax.fori_loop(3, 6, functools.partial(body, (ak[1], ak[1]), 6, 12), 0)

    def video_values(events):
        def body(ref, lo, hi, i, carry):
            cols, _ = video_unit(2 * i)
            v = jnp.concatenate([rows_of(ref, c, i) for c in range(5)], axis=0)
            v = jnp.concatenate([v, jnp.ones((BLOCKS * HD, HD), BF)], axis=1)
            for j in range(2):
                out = jnp.dot(wb[2 * i + j], v, preferred_element_type=F32)
                vo[pl.ds(j * 512, 512), cols] = (out[:, :HD] / out[:, HD:]).astype(BF)
            run_events(i, events, range(lo, hi))
            return carry

        lax.fori_loop(0, 3, functools.partial(body, av[0], 0, 3), 0)
        lax.fori_loop(3, 6, functools.partial(body, av[1], 3, 6), 0)

    def video_copies(i):
        cols = pl.ds(i * 256, 256)
        mine = pl.ds(pl.multiple_of(core * 768 + i * 256, 128), 256)
        return (
            remote(vo.at[other_rows, cols], vout_hbm.at[:, mine], w_send.at[i], w_recv.at[i], other),
            pltpu.make_async_copy(vo.at[own_rows, cols], vout_hbm.at[:, mine], w_local.at[i]),
        )

    def take(t, stage):
        for tensor in (6, 0) if t == 0 else (t,):
            if stage == 0 or stage == 2 and 4 <= t < 6:
                x_wait(tensor)
            else:
                arrive(gather(tensor, stage - 1))
            start(gather(tensor, stage))

    def x_next(t):
        x_wait(t - 1)
        if t == 4:
            arrive(ring(1))
            ring_own().wait()
        x_start(t)

    def ring_next():
        arrive(ring(0))
        start(ring(1))

    def make_marks():
        arrive(gather(6, 3))
        lax.fori_loop(0, 16, expand, 0)

    def ready_audio():
        swap_wait(0)
        swap_wait(1)
        swap_marks().wait_recv()
        arrive(gather(0, 3))

    def ready_video():
        swap_wait(2)
        arrive(gather(2, 3))

    def finish_half(half):
        reduce_end(half)
        start(results(half))

    steps = {
        "fV": ring_next, "vqs": lambda: swap_start(2), "ex": make_marks, "rQ1": lambda: arrive(gather(1, 3)), "rK1": lambda: arrive(gather(3, 3)),
        "tw0": lambda: arrive(gather(4, 3)), "tw1": lambda: arrive(gather(5, 3)),
        "w0": lambda: start(video_copies(0)), "w1": lambda: start(video_copies(1)), "w2": lambda: start(video_copies(2)),
    }
    for t, name in enumerate(("Q0", "Q1", "K0", "K1", "V0", "V1")):
        steps[f"s{name}"] = lambda t=t: x_next(t)
        for stage in range(4):
            steps[f"{stage + 1}{name}"] = lambda t=t, stage=stage: take(t, stage)
    for half in range(2):
        steps[f"p{half}"] = lambda half=half: place_all(half)
        steps[f"r1_{half}"] = lambda half=half: reduce_start(half)
        steps[f"r2_{half}"] = lambda half=half: reduce_pass(half)
        steps[f"ca_{half}"] = lambda half=half: reduce_cross(half)
        steps[f"cb_{half}"] = lambda half=half: reduce_cross_pass(half)
        steps[f"o_{half}"] = lambda half=half: finish_half(half)

    parts = {"": [], "A": [], "B": [], "X": [], "T": [], "Y": []}
    part_now, at = "", None
    for name in ORDER:
        if isinstance(name, int):
            at = name
        elif name in parts:
            part_now, at = name, None
        else:
            parts[part_now].append((at, steps[name]))

    def run(name):
        for _, step in parts[name]:
            step()

    run("")
    ready_audio()
    audio(parts["A"])
    run("B")
    ready_video()
    video_weights(parts["X"])
    run("T")
    video_values(parts["Y"])

    for t in range(7):
        sent(x_copies(t, 0))
        for stage in (2, 3) if 4 <= t < 6 else range(4):
            sent(gather(t, stage))
    sent(ring(0))
    sent(ring(1))
    for i in range(3):
        swap(i)[0].wait_send()
    swap_marks().wait_send()
    for half in range(2):
        sent(reduce1(half))
        sent(reduce2(half))
        sent(results(half))
        for cc in (0, 1):
            mine = pl.ds(cc * 768 + half * 384, 384)
            remote(
                ao.at[pl.ds(0, 64), pl.ds(half * 384, 384)], aout_hbm.at[:, mine], o_send.at[half, 0],
                o_recv.at[half, cc], result_low,
            ).wait_recv()
    for i in range(3):
        away, here = video_copies(i)
        here.wait()
        away.wait()


def hand_over(video_from, audio_from, video_to, audio_to):
    video_to[...] = video_from[...]
    audio_to[...] = audio_from[...]


def on_device(video_q, video_k, video_v, audio_q, audio_k, audio_v, video_clip, audio_clip):
    anywhere = pl.BlockSpec(memory_space=pl.ANY)
    dma = pltpu.SemaphoreType.DMA
    results = (jax.ShapeDtypeStruct(video_q.shape, BF), jax.ShapeDtypeStruct(audio_k.shape, BF))
    made = pl.pallas_call(
        kernel,
        out_shape=results,
        in_specs=[
            pl.BlockSpec(memory_space=pltpu.SMEM),
            pl.BlockSpec(memory_space=pltpu.VMEM),
            pl.BlockSpec(memory_space=pltpu.VMEM),
        ]
        + [anywhere] * 6,
        out_specs=(anywhere, anywhere),
        scratch_shapes=[
            pltpu.VMEM((1024, 768), BF),
            pltpu.VMEM((1024, 768), BF),
            pltpu.VMEM((1024, 768), BF),
            pltpu.VMEM((1024, HD), BF),
            pltpu.VMEM((2, 4, 4, 64, 384), BF),
            pltpu.VMEM((2, 4, 4, 64, 384), BF),
            pltpu.VMEM((2, 4, 4, 64, 384), BF),
            pltpu.VMEM((2, 4, 4, 64, 384), BF),
            pltpu.VMEM((2, 4, 4, 64, 384), BF),
            pltpu.VMEM((2, 4, 4, 64, 384), BF),
            pltpu.VMEM((4, 64, 1536), BF),
            pltpu.VMEM((2, 4, 4, 32, HD), BF),
            pltpu.VMEM((2, 4, 4, 64, HD), BF),
            pltpu.VMEM((32, HD), BF),
            pltpu.VMEM((640, 1024), F32),
            pltpu.VMEM((640, 1024), F32),
            pltpu.VMEM((640, 1024), BF),
            pltpu.VMEM((640, 1024), BF),
            pltpu.VMEM((640, HD), F32),
            pltpu.VMEM((640, HD), F32),
            pltpu.VMEM((512, BLOCKS * HD), F32),
            pltpu.VMEM((512, BLOCKS * HD), F32),
            pltpu.VMEM((12, 512, BLOCKS * HD), BF),
            pltpu.VMEM((6, BLOCKS, 8, HD), F32),
            pltpu.VMEM((6, BLOCKS, 8, HD), F32),
            pltpu.VMEM((2, BLOCKS, STAT, HD), BF),
            pltpu.VMEM((2, 4, 4, ROWS, HD), BF),
            pltpu.VMEM((2, 6, 2, ROWS, HD), BF),
            pltpu.VMEM((2, 3, ROWS, HD), BF),
            pltpu.VMEM((1024, 768), BF),
            pltpu.VMEM((HD, 768), BF),
            dma((7, 2)),
            dma((7, 2)),
            dma((4,)),
            dma((4,)),
            dma,
            dma((7, 16)),
            dma((7, 16)),
            dma((4,)),
            dma((4,)),
            dma((3,)),
            dma((2, 9)),
            dma((2, 9)),
            dma((2, 2)),
            dma((2, 2)),
            dma((3,)),
            dma((3,)),
            dma((3,)),
        ],
        compiler_params=pltpu.CompilerParams(
            collective_id=0, has_side_effects=True, vmem_limit_bytes=60 * 1024 * 1024
        ),
    )(
        video_clip, video_clip.reshape(4, HD), audio_clip.reshape(1, 64), video_q, video_k, video_v, audio_q, audio_k,
        audio_v,
    )
    return pl.pallas_call(
        hand_over,
        out_shape=results,
        grid=(4,),
        in_specs=[pl.BlockSpec((128, 1536), lambda i: (i, 0)), pl.BlockSpec((16, 1536), lambda i: (i, 0))],
        out_specs=(pl.BlockSpec((128, 1536), lambda i: (i, 0)), pl.BlockSpec((16, 1536), lambda i: (i, 0))),
    )(*made)


def solution(mesh):
    spread = P(("grp", "seq"), None)
    return jax.shard_map(
        on_device,
        mesh=mesh,
        in_specs=(spread,) * 6 + (P(("grp", "seq")),) * 2,
        out_specs=(spread, spread),
        check_vma=False,
    )
```

```python
import functools
import math

import jax
import jax.numpy as jnp
from jax import lax
from jax.experimental import pallas as pl
from jax.experimental.pallas import tpu as pltpu
from jax.sharding import PartitionSpec as P

MESH = pl.DeviceIdType.MESH
BF = jnp.bfloat16
F32 = jnp.float32
HD = 128
CLIPS = 9
SCALE = math.log2(math.e) / math.sqrt(HD)
FAR = -1048576.0
LOW = -32768.0
BLOCKS = 10
STAT = 3 * HD
ROWS = STAT + 16


ORDER = (
    "1Q0", "sQ1", "fV", "2Q0", "1Q1", "sK0", "3Q0", "sK1", "2Q1", "1K0", "3Q1", "1K1", "4Q0", "sV0", "2K0",
    "4Q1", "vqs", "2K1", "ex", "A", -2, "3K0", -1, "rQ1", 1, "3K1", 5, "4K0", 6, "3V0", "p0", "4K1", 7,
    "sV1", "r1_0", "B", "p1", "r1_1", "X", 3, "3V1", 4, "rK1", 5, "r2_0", "r2_1", 10, "4V0", "ca_0", "ca_1",
    "T", "4V1", "tw0", "Y", 1, "w0", "cb_0", 2, "cb_1", "tw1", 3, "w1", "o_0", 5, "w2", "o_1",
)


def kernel(
    clip_smem, video_clip, audio_clip, vq_hbm, vk_hbm, vv_hbm, aq_hbm, ak_hbm, av_hbm,
    vout_hbm, aout_hbm,
    vq, vk, vv, ve, aq0, aq1, ak0, ak1, av0, av1, v_row, mk, am, mk_own, buf_c, buf_d, wt_c, wt_d, high_c, high_d, buf_a, buf_b, wb, tops, sums, window, part, got1, got2, vo, ao,
    x_send, x_recv, p_send, p_recv, p_local, g_send, g_recv, v_send, v_recv, v_local, r_send, r_recv, o_send, o_recv, w_send, w_recv, w_local,
):
    g = lax.axis_index("grp")
    s = lax.axis_index("seq")
    core = lax.rem(s, 2)
    chip = s // 2
    z, y = chip // 4, lax.rem(chip, 4)
    zp, zm, z2 = lax.rem(z + 1, 4), lax.rem(z + 3, 4), lax.rem(z + 2, 4)
    yp, ym, y2 = lax.rem(y + 1, 4), lax.rem(y + 3, 4), lax.rem(y + 2, 4)
    gp, gm = lax.rem(g + 1, 4), lax.rem(g + 3, 4)

    def device(grp, zz, yy, cc):
        return (grp, (zz * 4 + yy) * 2 + cc)

    other = device(g, z, y, 1 - core)
    to_yp, to_ym = (device(g, z, b, core) for b in (yp, ym))
    to_zp, to_zm = (device(g, b, y, core) for b in (zp, zm))
    before = lax.rem(chip + 15, 16)
    after = lax.rem(chip + 1, 16)
    result_low = (gp, chip * 2)
    result_high = (gp, before * 2 + 1)

    barrier = pltpu.get_barrier_semaphore()

    def greet(dev):
        pl.semaphore_signal(barrier, inc=1, device_id=dev, device_id_type=MESH)

    for dev in (other, to_yp, to_ym, to_zp, to_zm):
        greet(dev)
    for cc in (0, 1):
        greet(device(gm, z, y, cc))
        greet(device(gp, z, y, cc))
    greet(result_high)

    @pl.when(core == 1)
    def _():
        greet((gm, after * 2))
        greet((gm, after * 2 + 1))

    pl.semaphore_wait(barrier, 10 + 2 * core)

    def remote(src, dst, ssem, rsem, dev):
        return pltpu.make_async_remote_copy(
            src_ref=src, dst_ref=dst, send_sem=ssem, recv_sem=rsem, device_id=dev, device_id_type=MESH
        )

    def columns(half, width):
        return pl.ds(pl.multiple_of(half * width, 128), width)

    aq, ak, av = (aq0, aq1), (ak0, ak1), (av0, av1)
    tensors = [(src, dst[half], half) for src, dst in ((aq_hbm, aq), (ak_hbm, ak), (av_hbm, av)) for half in (0, 1)]
    tensors.append((mk_own, mk, None))

    def along(on_y, on_z):
        return on_y * (1 - core) + on_z * core

    u, up, um = along(y, z), along(yp, zp), along(ym, zm)
    to_up = device(g, along(z, zp), along(yp, y), core)
    to_um = device(g, along(z, zm), along(ym, y), core)
    def ring(stage):
        src, row = av_hbm, v_row
        low, high = row.at[um, pl.ds(0, 32)], row.at[up, pl.ds(32, 32)]
        plan = ((src, row.at[u], to_up), (src, row.at[u], to_um)) if stage == 0 else ((low, low, to_up), (high, high, to_um))
        return [
            remote(a, b, p_send.at[2 * stage + n], p_recv.at[2 * stage + n], dev) for n, (a, b, dev) in enumerate(plan)
        ]

    def ring_own():
        return pltpu.make_async_copy(av_hbm, v_row.at[u], p_local)

    def x_copies(t, sender):
        src, dst, half = tensors[t]
        copies = []
        for cc in (0, 1):
            if half is None:
                a, b = src, dst.at[sender, z, y]
            elif t < 4:
                a, b = src.at[:, pl.ds(cc * 768 + half * 384, 384)], dst.at[sender, z, y]
            else:
                a = v_row.at[:, :, pl.ds(cc * 768 + half * 384, 384)]
                b = dst.at[0, z] if sender == 0 else dst.at[1, :, y]
            copies.append(remote(a, b, x_send.at[t, cc], x_recv.at[t, sender], device(gm, z, y, cc)))
        return copies

    def x_start(t):
        if t < 4 or t == 6:
            start(x_copies(t, core))
            return
        for cc in (0, 1):

            @pl.when(core == cc)
            def _():
                start(x_copies(t, cc))

    here_already = set()

    def x_wait(t):
        if t in here_already:
            return
        here_already.add(t)
        for cc in (0, 1):
            x_copies(t, cc)[0].wait_recv()

    def gather(t, stage):
        x = tensors[t][1]
        rows = 16 if t == 6 else 32
        low, high = pl.ds(0, rows), pl.ds(rows, rows)
        first, last = pl.ds(0, 2), pl.ds(2, 2)
        plan = (
            (x.at[0, z, y], to_yp),
            (x.at[0, z, y], to_ym),
            (x.at[1, z, y], to_zp),
            (x.at[1, z, y], to_zm),
        ), (
            (x.at[0, z, ym, low], to_yp),
            (x.at[0, z, yp, high], to_ym),
            (x.at[1, zm, y, low], to_zp),
            (x.at[1, zp, y, high], to_zm),
        ), (
            (x.at[0, z], to_zp),
            (x.at[0, z], to_zm),
            (x.at[1, :, y], to_yp),
            (x.at[1, :, y], to_ym),
        ), (
            (x.at[0, zm, first], to_zp),
            (x.at[0, zp, last], to_zm),
            (x.at[1, first, ym], to_yp),
            (x.at[1, last, yp], to_ym),
        )
        return [
            remote(ref, ref, g_send.at[t, stage * 4 + i], g_recv.at[t, stage * 4 + i], dev)
            for i, (ref, dev) in enumerate(plan[stage])
        ]

    def start(copies):
        for copy in copies:
            copy.start()

    def arrive(copies):
        for copy in copies:
            copy.wait_recv()

    def sent(copies):
        for copy in copies:
            copy.wait_send()

    video = ((vk_hbm, vk), (vv_hbm, vv), (vq_hbm, vq))
    own_rows = pl.ds(pl.multiple_of(core * 512, 512), 512)
    other_rows = pl.ds(pl.multiple_of((1 - core) * 512, 512), 512)

    def swap(i):
        src, dst = video[i]
        return (
            remote(src.at[:, columns(1 - core, 768)], dst.at[own_rows], v_send.at[i], v_recv.at[i], other),
            pltpu.make_async_copy(src.at[:, columns(core, 768)], dst.at[own_rows], v_local.at[i]),
        )

    def swap_start(i):
        away, here = swap(i)
        away.start()
        here.start()

    def swap_wait(i):
        away, here = swap(i)
        away.wait_recv()
        here.wait()

    def swap_marks():
        return remote(ve.at[own_rows], ve.at[own_rows], v_send.at[3], v_recv.at[3], other)

    x_start(0)
    start(ring(0))
    ring_own().start()
    swap_start(0)
    swap_start(1)

    numbers = (audio_clip[...] - gm * CLIPS).astype(F32)
    numbers = jnp.concatenate([numbers, numbers], axis=1)
    mk_own[...] = jnp.broadcast_to(numbers, (32, HD)).astype(BF)
    x_start(6)
    clips = lax.broadcasted_iota(jnp.int32, (HD, HD), 0)
    for i in range(4):
        same = video_clip[i : i + 1, :] - g * CLIPS == clips
        at = pl.multiple_of(core * 512 + i * HD, HD)
        ve[pl.ds(at, HD), :] = jnp.where(same, 0.0, FAR).T.astype(BF)
    swap_marks().start()

    lanes = clips.astype(F32)

    def expand(i, carry):
        bz, by = i // 4, lax.rem(i, 4)
        for cc in (0, 1):
            numbers = mk[cc, bz, by, pl.ds(0, 16), :].astype(F32)[0:1]
            am[cc, bz, by] = jnp.where(numbers == lanes, 1.0, 0.0).T[0:64].astype(BF)
        return carry

    first = jnp.where(core == 0, clip_smem[0], clip_smem[511] - 1) - g * CLIPS

    def block(i):
        return jnp.bitwise_and(first + i, 15)

    def pieces(ref, i, h):
        b, a = block(i - 1), block(i)
        where = (1, b // 4, jnp.bitwise_and(b, 3)), (0, a // 4, jnp.bitwise_and(a, 3))
        if h is None:
            return [ref[at] for at in where]
        cols = pl.ds(pl.multiple_of(lax.rem(h, 3) * HD, HD), HD)
        return [ref[(*at, slice(None), cols)] for at in where]

    def packed(top, total):
        high = total.astype(BF).astype(F32)
        gap = jnp.zeros((1, HD), F32)
        return jnp.concatenate([top, gap, total - high, gap, high, jnp.zeros((5, HD), F32)], axis=0)

    lane = lax.broadcasted_iota(jnp.int32, (HD, HD), 1)

    def audio_step(unit_scores, unit_weights, unit_values):
        if unit_scores is not None:
            u, buf, ref = unit_scores
            cols = pl.ds(pl.multiple_of(u // 2 * HD, HD), HD)
            blocks = [5 * lax.rem(u, 2) + i for i in range(5)]
            q = jnp.concatenate([piece for i in blocks for piece in pieces(ref, i, u // 2)], axis=0)
            mark = jnp.concatenate([piece for i in blocks for piece in pieces(am, i, None)], axis=0)
            q = jnp.concatenate([q, mark], axis=1)
        if unit_values is not None:
            h, tile, weights, high = unit_values[0] // 2, lax.rem(unit_values[0], 2), unit_values[1], unit_values[2]
            v = jnp.concatenate([vv[:, pl.ds(pl.multiple_of(h * HD, HD), HD)], jnp.ones((1024, HD), BF)], axis=1)
            out = jnp.dot(weights[...], v, preferred_element_type=F32)
        row = 0
        for c in range(4):
            if unit_scores is not None:
                rows = pl.ds(c * 256, 256)
                k = jnp.concatenate([vk[rows, cols], ve[rows, :]], axis=1)
                buf[:, c * 256 : (c + 1) * 256] = lax.dot_general(
                    q, k, (((1,), (1,)), ((), ())), preferred_element_type=F32
                )
            if unit_weights is not None:
                scores_w, weights_w, high_w = unit_weights
                for _ in range(10):
                    scores = scores_w[row : row + 16, :]
                    top = jnp.maximum(jnp.max(scores, axis=1, keepdims=True) * SCALE, LOW).astype(BF).astype(F32)
                    weights_w[row : row + 16, :] = jnp.exp2(scores * SCALE - top).astype(BF)
                    high_w[row : row + 16, :] = jnp.broadcast_to(top, (16, HD))
                    row += 16
        if unit_values is not None:
            where = pl.ds(pl.multiple_of(lax.rem(h, 3) * HD, HD), HD)
            for b in range(5):
                rows = slice(b * HD, (b + 1) * HD)
                window[h // 3, 5 * tile + b, where, :] = out[rows, :HD].T.astype(BF)
                stats = jnp.where(lane < 8, high[rows, :], out[rows, HD:]).T
                tops[h, 5 * tile + b] = stats[0:8]
                sums[h, 5 * tile + b] = stats[8:16]

    def audio(events):
        even, odd = (buf_c, wt_c, high_c), (buf_d, wt_d, high_d)

        def body(ref, lo, hi, i, carry):
            u = 2 * i
            audio_step((u + 2, buf_c, ref), odd, (u, wt_c, high_c))
            run_events(u, events, range(lo, hi, 2))
            audio_step((u + 3, buf_d, ref), even, (u + 1, wt_d, high_d))
            run_events(u + 1, events, range(lo + 1, hi, 2))
            return carry

        audio_step((0, buf_c, aq[0]), None, None)
        run_now(-2, events)
        audio_step((1, buf_d, aq[0]), even, None)
        run_now(-1, events)
        lax.fori_loop(0, 2, functools.partial(body, aq[0], 0, 4), 0)
        lax.fori_loop(2, 5, functools.partial(body, aq[1], 4, 10), 0)
        audio_step(None, odd, (10, wt_c, high_c))
        audio_step(None, None, (11, wt_d, high_d))

    def run_now(at, events):
        for where, event in events:
            if where == at:
                event()

    def run_events(i, events, steps_here):
        for at in sorted({at for at, _ in events if at in steps_here}):

            @pl.when(i == at)
            def _():
                run_now(at, events)

    empty = jnp.where(lax.broadcasted_iota(jnp.int32, (16, HD), 0) < 3, LOW, 0.0)

    def place_block(half, b):
        at = jnp.bitwise_and(b - first, 15)
        inside = (at < BLOCKS).astype(F32)
        at = jnp.minimum(at, BLOCKS - 1)
        bz, by = b // 4, lax.rem(b, 4)
        body = window[half, at, :, :].astype(F32)
        part[half, bz, by, pl.ds(0, STAT), :] = (body * inside).astype(BF)
        top = jnp.concatenate([tops[half * 3 + hh, at][0:1] for hh in range(3)], axis=0)
        total = jnp.concatenate([sums[half * 3 + hh, at][0:1] for hh in range(3)], axis=0)
        stats = packed(top, total)
        part[half, bz, by, pl.ds(STAT, 16), :] = (stats * inside + empty * (1.0 - inside)).astype(BF)

    def place_all(half):
        def body(b, carry):
            place_block(half, b)
            return carry

        lax.fori_loop(0, 16, body, 0)

    def slab(half, where, lo):
        if half == 0:
            return part.at[0, where, pl.ds(lo, 2)]
        return part.at[1, pl.ds(lo, 2), where]

    axes = ((z, zp, zm, z2, to_zp, to_zm), (y, yp, ym, y2, to_yp, to_ym))
    turn_by = 1 + 2 * core

    def cross(at, two):
        p, m = lax.rem(at + turn_by, 4), lax.rem(at + 4 - turn_by, 4)
        return at, p, m, two

    crosses = (cross(y, y2), cross(z, z2))

    def reduce1(half):
        _, p, m, two, to_p, to_m = axes[half]
        plan = (
            (slab(half, two, 0), to_p), (slab(half, two, 2), to_m),
            (slab(half, p, 2), to_p), (slab(half, m, 0), to_m),
            (slab(half, p, 0), to_p), (slab(half, m, 2), to_m),
        )
        return [
            remote(ref, got1.at[half, i], r_send.at[half, i], r_recv.at[half, i], dev)
            for i, (ref, dev) in enumerate(plan)
        ]

    def one(half, u):
        if half == 0:
            return part.at[0, z, u]
        return part.at[1, u, y]

    def reduce2(half):
        _, p, m, two = crosses[half]
        to_p, to_m = (device(g, z, u, core) if half == 0 else device(g, u, y, core) for u in (p, m))
        return [
            remote(one(half, u), got2.at[half, i], r_send.at[half, 6 + i], r_recv.at[half, 6 + i], dev)
            for i, (u, dev) in enumerate(((two, to_p), (m, to_m), (p, to_p)))
        ]

    def merged(refs):
        stats = [ref[pl.ds(STAT, 16), :].astype(F32) for ref in refs]
        tops = [x[0:3] for x in stats]
        top = tops[0]
        for x in tops[1:]:
            top = jnp.maximum(top, x)
        factors = [jnp.exp2(x - top) for x in tops]
        total = sum((x[8:11] + x[4:7]) * f for x, f in zip(stats, factors))
        outs = [
            sum(ref[pl.ds(hh * HD, HD), :].astype(F32) * f[hh : hh + 1] for ref, f in zip(refs, factors))
            for hh in range(3)
        ]
        return outs, top, total

    def merge_into(target, sources):
        outs, top, total = merged([target] + sources)
        for hh in range(3):
            target[pl.ds(hh * HD, HD), :] = outs[hh].astype(BF)
        target[pl.ds(STAT, 16), :] = packed(top, total).astype(BF)

    def merge_slab(half, where, lo, slots):
        def body(i, carry):
            target = part.at[0, where, lo + i] if half == 0 else part.at[1, lo + i, where]
            merge_into(target, [got1.at[half, slot, i] for slot in slots])
            return carry

        lax.fori_loop(0, 2, body, 0)

    def reduce_start(half):
        start(reduce1(half)[:4])

    def reduce_pass(half):
        _, p, m, *_ = axes[half]
        copies = reduce1(half)
        copies[0].wait_recv()
        merge_slab(half, p, 0, (0,))
        copies[4].start()
        copies[1].wait_recv()
        merge_slab(half, m, 2, (1,))
        copies[5].start()

    def reduce_cross(half):
        own = axes[half][0]
        arrive(reduce1(half)[2:])
        merge_slab(half, own, 0, (3, 4))
        merge_slab(half, own, 2, (2, 5))
        start(reduce2(half)[:2])

    def reduce_cross_pass(half):
        copies = reduce2(half)
        copies[0].wait_recv()
        merge_into(one(half, crosses[half][1]), [got2.at[half, 0]])
        copies[2].start()

    def reduce_end(half):
        own = crosses[half][0]
        arrive(reduce2(half)[1:])
        outs, _, total = merged([one(half, own)] + [got2.at[half, i] for i in (1, 2)])
        scale = 1.0 / total
        for hh in range(3):
            done = (outs[hh] * scale[hh : hh + 1]).T
            ao[:, pl.ds((half * 3 + hh) * HD, HD)] = done.astype(BF)

    def results(half):
        mine = pl.ds(pl.multiple_of(core * 768 + half * 384, 128), 384)
        cols = pl.ds(half * 384, 384)
        return [
            remote(
                ao.at[rows, cols], aout_hbm.at[:, mine], o_send.at[half, i], o_recv.at[half, core], dev
            )
            for i, (rows, dev) in enumerate(((pl.ds(64, 64), result_low), (pl.ds(0, 64), result_high)))
        ]

    def rows_of(ref, i, h):
        return jnp.concatenate(pieces(ref, 2 * i, h) + pieces(ref, 2 * i + 1, h), axis=0)

    def video_unit(u):
        cols = pl.ds(pl.multiple_of(u // 2 * HD, HD), HD)
        return cols, pl.ds(pl.multiple_of(lax.rem(u, 2) * 512, 512), 512)

    def video_both(u_scores, ref, u_out, buf_scores, buf_out):
        cols, here = video_unit(u_scores)
        q = jnp.concatenate([vq[here, cols], ve[here, :]], axis=1)
        row = 0
        for c in range(5):
            k = jnp.concatenate([rows_of(ref, c, u_scores // 2), rows_of(am, c, None)], axis=1)
            buf_scores[:, c * 256 : (c + 1) * 256] = lax.dot_general(
                q, k, (((1,), (1,)), ((), ())), preferred_element_type=F32
            )
            if u_out is not None:
                for _ in range(7 if c < 2 else 6):
                    scores = buf_out[row : row + 16, :]
                    top = jnp.max(scores, axis=1, keepdims=True) * SCALE
                    wb[u_out, row : row + 16, :] = jnp.exp2(scores * SCALE - top).astype(BF)
                    row += 16

    def video_weights(events):
        def body(refs, lo, hi, i, carry):
            u = 2 * i
            video_both(u + 1, refs[0], u, buf_b, buf_a)
            run_events(u, events, range(lo, hi, 2))
            video_both(jnp.minimum(u + 2, 11), refs[1], u + 1, buf_a, buf_b)
            run_events(u + 1, events, range(lo + 1, hi, 2))
            return carry

        video_both(0, ak[0], None, buf_a, None)
        run_now(-1, events)
        lax.fori_loop(0, 2, functools.partial(body, (ak[0], ak[0]), 0, 4), 0)
        lax.fori_loop(2, 3, functools.partial(body, (ak[0], ak[1]), 4, 6), 0)
        lax.fori_loop(3, 6, functools.partial(body, (ak[1], ak[1]), 6, 12), 0)

    def video_values(events):
        def body(ref, lo, hi, i, carry):
            cols, _ = video_unit(2 * i)
            v = jnp.concatenate([rows_of(ref, c, i) for c in range(5)], axis=0)
            v = jnp.concatenate([v, jnp.ones((BLOCKS * HD, HD), BF)], axis=1)
            for j in range(2):
                out = jnp.dot(wb[2 * i + j], v, preferred_element_type=F32)
                vo[pl.ds(j * 512, 512), cols] = (out[:, :HD] / out[:, HD:]).astype(BF)
            run_events(i, events, range(lo, hi))
            return carry

        lax.fori_loop(0, 3, functools.partial(body, av[0], 0, 3), 0)
        lax.fori_loop(3, 6, functools.partial(body, av[1], 3, 6), 0)

    def video_copies(i):
        cols = pl.ds(i * 256, 256)
        mine = pl.ds(pl.multiple_of(core * 768 + i * 256, 128), 256)
        return (
            remote(vo.at[other_rows, cols], vout_hbm.at[:, mine], w_send.at[i], w_recv.at[i], other),
            pltpu.make_async_copy(vo.at[own_rows, cols], vout_hbm.at[:, mine], w_local.at[i]),
        )

    def take(t, stage):
        for tensor in (6, 0) if t == 0 else (t,):
            if stage == 0 or stage == 2 and 4 <= t < 6:
                x_wait(tensor)
            else:
                arrive(gather(tensor, stage - 1))
            start(gather(tensor, stage))

    def x_next(t):
        x_wait(t - 1)
        if t == 4:
            arrive(ring(1))
            ring_own().wait()
        x_start(t)

    def ring_next():
        arrive(ring(0))
        start(ring(1))

    def make_marks():
        arrive(gather(6, 3))
        lax.fori_loop(0, 16, expand, 0)

    def ready_audio():
        swap_wait(0)
        swap_wait(1)
        swap_marks().wait_recv()
        arrive(gather(0, 3))

    def ready_video():
        swap_wait(2)
        arrive(gather(2, 3))

    def finish_half(half):
        reduce_end(half)
        start(results(half))

    steps = {
        "fV": ring_next, "vqs": lambda: swap_start(2), "ex": make_marks, "rQ1": lambda: arrive(gather(1, 3)), "rK1": lambda: arrive(gather(3, 3)),
        "tw0": lambda: arrive(gather(4, 3)), "tw1": lambda: arrive(gather(5, 3)),
        "w0": lambda: start(video_copies(0)), "w1": lambda: start(video_copies(1)), "w2": lambda: start(video_copies(2)),
    }
    for t, name in enumerate(("Q0", "Q1", "K0", "K1", "V0", "V1")):
        steps[f"s{name}"] = lambda t=t: x_next(t)
        for stage in range(4):
            steps[f"{stage + 1}{name}"] = lambda t=t, stage=stage: take(t, stage)
    for half in range(2):
        steps[f"p{half}"] = lambda half=half: place_all(half)
        steps[f"r1_{half}"] = lambda half=half: reduce_start(half)
        steps[f"r2_{half}"] = lambda half=half: reduce_pass(half)
        steps[f"ca_{half}"] = lambda half=half: reduce_cross(half)
        steps[f"cb_{half}"] = lambda half=half: reduce_cross_pass(half)
        steps[f"o_{half}"] = lambda half=half: finish_half(half)

    parts = {"": [], "A": [], "B": [], "X": [], "T": [], "Y": []}
    part_now, at = "", None
    for name in ORDER:
        if isinstance(name, int):
            at = name
        elif name in parts:
            part_now, at = name, None
        else:
            parts[part_now].append((at, steps[name]))

    def run(name):
        for _, step in parts[name]:
            step()

    run("")
    ready_audio()
    audio(parts["A"])
    run("B")
    ready_video()
    video_weights(parts["X"])
    run("T")
    video_values(parts["Y"])

    for t in range(7):
        sent(x_copies(t, 0))
        for stage in (2, 3) if 4 <= t < 6 else range(4):
            sent(gather(t, stage))
    sent(ring(0))
    sent(ring(1))
    for i in range(3):
        swap(i)[0].wait_send()
    swap_marks().wait_send()
    for half in range(2):
        sent(reduce1(half))
        sent(reduce2(half))
        sent(results(half))
        for cc in (0, 1):
            mine = pl.ds(cc * 768 + half * 384, 384)
            remote(
                ao.at[pl.ds(0, 64), pl.ds(half * 384, 384)], aout_hbm.at[:, mine], o_send.at[half, 0],
                o_recv.at[half, cc], result_low,
            ).wait_recv()
    for i in range(3):
        away, here = video_copies(i)
        here.wait()
        away.wait()


def hand_over(video_from, audio_from, video_to, audio_to, video, audio, sem_in, sem_out):
    pieces = [(video_from.at[r], video.at[r], video_to.at[r]) for r in (pl.ds(i * 128, 128) for i in range(4))]
    pieces.append((audio_from, audio, audio_to))
    arriving = [pltpu.make_async_copy(a, b, sem_in.at[i]) for i, (a, b, _) in enumerate(pieces)]
    leaving = [pltpu.make_async_copy(b, c, sem_out.at[i]) for i, (_, b, c) in enumerate(pieces)]
    for copy in arriving:
        copy.start()
    for into, out in zip(arriving, leaving):
        into.wait()
        out.start()
    for copy in leaving:
        copy.wait()


def on_device(video_q, video_k, video_v, audio_q, audio_k, audio_v, video_clip, audio_clip):
    anywhere = pl.BlockSpec(memory_space=pl.ANY)
    dma = pltpu.SemaphoreType.DMA
    results = (jax.ShapeDtypeStruct(video_q.shape, BF), jax.ShapeDtypeStruct(audio_k.shape, BF))
    made = pl.pallas_call(
        kernel,
        out_shape=results,
        in_specs=[
            pl.BlockSpec(memory_space=pltpu.SMEM),
            pl.BlockSpec(memory_space=pltpu.VMEM),
            pl.BlockSpec(memory_space=pltpu.VMEM),
        ]
        + [anywhere] * 6,
        out_specs=(anywhere, anywhere),
        scratch_shapes=[
            pltpu.VMEM((1024, 768), BF),
            pltpu.VMEM((1024, 768), BF),
            pltpu.VMEM((1024, 768), BF),
            pltpu.VMEM((1024, HD), BF),
            pltpu.VMEM((2, 4, 4, 64, 384), BF),
            pltpu.VMEM((2, 4, 4, 64, 384), BF),
            pltpu.VMEM((2, 4, 4, 64, 384), BF),
            pltpu.VMEM((2, 4, 4, 64, 384), BF),
            pltpu.VMEM((2, 4, 4, 64, 384), BF),
            pltpu.VMEM((2, 4, 4, 64, 384), BF),
            pltpu.VMEM((4, 64, 1536), BF),
            pltpu.VMEM((2, 4, 4, 32, HD), BF),
            pltpu.VMEM((2, 4, 4, 64, HD), BF),
            pltpu.VMEM((32, HD), BF),
            pltpu.VMEM((640, 1024), F32),
            pltpu.VMEM((640, 1024), F32),
            pltpu.VMEM((640, 1024), BF),
            pltpu.VMEM((640, 1024), BF),
            pltpu.VMEM((640, HD), F32),
            pltpu.VMEM((640, HD), F32),
            pltpu.VMEM((512, BLOCKS * HD), F32),
            pltpu.VMEM((512, BLOCKS * HD), F32),
            pltpu.VMEM((12, 512, BLOCKS * HD), BF),
            pltpu.VMEM((6, BLOCKS, 8, HD), F32),
            pltpu.VMEM((6, BLOCKS, 8, HD), F32),
            pltpu.VMEM((2, BLOCKS, STAT, HD), BF),
            pltpu.VMEM((2, 4, 4, ROWS, HD), BF),
            pltpu.VMEM((2, 6, 2, ROWS, HD), BF),
            pltpu.VMEM((2, 3, ROWS, HD), BF),
            pltpu.VMEM((1024, 768), BF),
            pltpu.VMEM((HD, 768), BF),
            dma((7, 2)),
            dma((7, 2)),
            dma((4,)),
            dma((4,)),
            dma,
            dma((7, 16)),
            dma((7, 16)),
            dma((4,)),
            dma((4,)),
            dma((3,)),
            dma((2, 9)),
            dma((2, 9)),
            dma((2, 2)),
            dma((2, 2)),
            dma((3,)),
            dma((3,)),
            dma((3,)),
        ],
        compiler_params=pltpu.CompilerParams(
            collective_id=0, has_side_effects=True, vmem_limit_bytes=60 * 1024 * 1024
        ),
    )(
        video_clip, video_clip.reshape(4, HD), audio_clip.reshape(1, 64), video_q, video_k, video_v, audio_q, audio_k,
        audio_v,
    )
    return pl.pallas_call(
        hand_over,
        out_shape=results,
        in_specs=[anywhere] * 2,
        out_specs=(anywhere, anywhere),
        scratch_shapes=[pltpu.VMEM((512, 1536), BF), pltpu.VMEM((64, 1536), BF), dma((5,)), dma((5,))],
    )(*made)


def solution(mesh):
    spread = P(("grp", "seq"), None)
    return jax.shard_map(
        on_device,
        mesh=mesh,
        in_specs=(spread,) * 6 + (P(("grp", "seq")),) * 2,
        out_specs=(spread, spread),
        check_vma=False,
    )
```

```python
import functools
import math

import jax
import jax.numpy as jnp
from jax import lax
from jax.experimental import pallas as pl
from jax.experimental.pallas import tpu as pltpu
from jax.sharding import PartitionSpec as P

MESH = pl.DeviceIdType.MESH
BF = jnp.bfloat16
F32 = jnp.float32
HD = 128
CLIPS = 9
SCALE = math.log2(math.e) / math.sqrt(HD)
FAR = -1048576.0
LOW = -32768.0
BLOCKS = 10
STAT = 3 * HD
ROWS = STAT + 16


ORDER = (
    "1Q0", "sQ1", "fV", "2Q0", "1Q1", "sK0", "3Q0", "sK1", "2Q1", "1K0", "3Q1", "1K1", "4Q0", "sV0", "2K0",
    "4Q1", "vqs", "2K1", "ex", "A", -2, "3K0", -1, "rQ1", 1, "3K1", 5, "4K0", 6, "3V0", "p0", "4K1", 7,
    "sV1", "r1_0", "B", "p1", "r1_1", "X", 3, "3V1", 4, "rK1", 5, "r2_0", "r2_1", 10, "4V0", "ca_0", "ca_1",
    "T", "4V1", "tw0", "Y", 1, "w0", "cb_0", 2, "cb_1", "tw1", 3, "w1", "o_0", 5, "w2", "o_1",
)


def kernel(
    clip_smem, video_clip, audio_clip, vq_hbm, vk_hbm, vv_hbm, aq_hbm, ak_hbm, av_hbm,
    vout_hbm, aout_hbm,
    vq, vk, vv, ve, aq0, aq1, ak0, ak1, av0, av1, v_row, mk, am, mk_own, buf_c, buf_d, wt_c, wt_d, high_c, high_d, buf_a, buf_b, wb, tops, sums, window, part, got1, got2, vo, ao,
    x_send, x_recv, p_send, p_recv, p_local, g_send, g_recv, v_send, v_recv, v_local, r_send, r_recv, o_send, o_recv, w_send, w_recv, w_local,
):
    g = lax.axis_index("grp")
    s = lax.axis_index("seq")
    core = lax.rem(s, 2)
    chip = s // 2
    z, y = chip // 4, lax.rem(chip, 4)
    zp, zm, z2 = lax.rem(z + 1, 4), lax.rem(z + 3, 4), lax.rem(z + 2, 4)
    yp, ym, y2 = lax.rem(y + 1, 4), lax.rem(y + 3, 4), lax.rem(y + 2, 4)
    gp, gm = lax.rem(g + 1, 4), lax.rem(g + 3, 4)

    def device(grp, zz, yy, cc):
        return (grp, (zz * 4 + yy) * 2 + cc)

    other = device(g, z, y, 1 - core)
    to_yp, to_ym = (device(g, z, b, core) for b in (yp, ym))
    to_zp, to_zm = (device(g, b, y, core) for b in (zp, zm))
    before = lax.rem(chip + 15, 16)
    after = lax.rem(chip + 1, 16)
    result_low = (gp, chip * 2)
    result_high = (gp, before * 2 + 1)

    barrier = pltpu.get_barrier_semaphore()

    def greet(dev):
        pl.semaphore_signal(barrier, inc=1, device_id=dev, device_id_type=MESH)

    for dev in (other, to_yp, to_ym, to_zp, to_zm):
        greet(dev)
    for cc in (0, 1):
        greet(device(gm, z, y, cc))
        greet(device(gp, z, y, cc))
    greet(result_high)

    @pl.when(core == 1)
    def _():
        greet((gm, after * 2))
        greet((gm, after * 2 + 1))

    pl.semaphore_wait(barrier, 10 + 2 * core)

    def remote(src, dst, ssem, rsem, dev):
        return pltpu.make_async_remote_copy(
            src_ref=src, dst_ref=dst, send_sem=ssem, recv_sem=rsem, device_id=dev, device_id_type=MESH
        )

    def columns(half, width):
        return pl.ds(pl.multiple_of(half * width, 128), width)

    aq, ak, av = (aq0, aq1), (ak0, ak1), (av0, av1)
    tensors = [(src, dst[half], half) for src, dst in ((aq_hbm, aq), (ak_hbm, ak), (av_hbm, av)) for half in (0, 1)]
    tensors.append((mk_own, mk, None))

    def along(on_y, on_z):
        return on_y * (1 - core) + on_z * core

    u, up, um = along(y, z), along(yp, zp), along(ym, zm)
    to_up = device(g, along(z, zp), along(yp, y), core)
    to_um = device(g, along(z, zm), along(ym, y), core)
    def ring(stage):
        src, row = av_hbm, v_row
        low, high = row.at[um, pl.ds(0, 32)], row.at[up, pl.ds(32, 32)]
        plan = ((src, row.at[u], to_up), (src, row.at[u], to_um)) if stage == 0 else ((low, low, to_up), (high, high, to_um))
        return [
            remote(a, b, p_send.at[2 * stage + n], p_recv.at[2 * stage + n], dev) for n, (a, b, dev) in enumerate(plan)
        ]

    def ring_own():
        return pltpu.make_async_copy(av_hbm, v_row.at[u], p_local)

    def x_copies(t, sender):
        src, dst, half = tensors[t]
        copies = []
        for cc in (0, 1):
            if half is None:
                a, b = src, dst.at[sender, z, y]
            elif t < 4:
                a, b = src.at[:, pl.ds(cc * 768 + half * 384, 384)], dst.at[sender, z, y]
            else:
                a = v_row.at[:, :, pl.ds(cc * 768 + half * 384, 384)]
                b = dst.at[0, z] if sender == 0 else dst.at[1, :, y]
            copies.append(remote(a, b, x_send.at[t, cc], x_recv.at[t, sender], device(gm, z, y, cc)))
        return copies

    def x_start(t):
        if t < 4 or t == 6:
            start(x_copies(t, core))
            return
        for cc in (0, 1):

            @pl.when(core == cc)
            def _():
                start(x_copies(t, cc))

    here_already = set()

    def x_wait(t):
        if t in here_already:
            return
        here_already.add(t)
        for cc in (0, 1):
            x_copies(t, cc)[0].wait_recv()

    def gather(t, stage):
        x = tensors[t][1]
        rows = 16 if t == 6 else 32
        low, high = pl.ds(0, rows), pl.ds(rows, rows)
        first, last = pl.ds(0, 2), pl.ds(2, 2)
        plan = (
            (x.at[0, z, y], to_yp),
            (x.at[0, z, y], to_ym),
            (x.at[1, z, y], to_zp),
            (x.at[1, z, y], to_zm),
        ), (
            (x.at[0, z, ym, low], to_yp),
            (x.at[0, z, yp, high], to_ym),
            (x.at[1, zm, y, low], to_zp),
            (x.at[1, zp, y, high], to_zm),
        ), (
            (x.at[0, z], to_zp),
            (x.at[0, z], to_zm),
            (x.at[1, :, y], to_yp),
            (x.at[1, :, y], to_ym),
        ), (
            (x.at[0, zm, first], to_zp),
            (x.at[0, zp, last], to_zm),
            (x.at[1, first, ym], to_yp),
            (x.at[1, last, yp], to_ym),
        )
        return [
            remote(ref, ref, g_send.at[t, stage * 4 + i], g_recv.at[t, stage * 4 + i], dev)
            for i, (ref, dev) in enumerate(plan[stage])
        ]

    def start(copies):
        for copy in copies:
            copy.start()

    def arrive(copies):
        for copy in copies:
            copy.wait_recv()

    def sent(copies):
        for copy in copies:
            copy.wait_send()

    video = ((vk_hbm, vk), (vv_hbm, vv), (vq_hbm, vq))
    own_rows = pl.ds(pl.multiple_of(core * 512, 512), 512)
    other_rows = pl.ds(pl.multiple_of((1 - core) * 512, 512), 512)

    def swap(i):
        src, dst = video[i]
        return (
            remote(src.at[:, columns(1 - core, 768)], dst.at[own_rows], v_send.at[i], v_recv.at[i], other),
            pltpu.make_async_copy(src.at[:, columns(core, 768)], dst.at[own_rows], v_local.at[i]),
        )

    def swap_start(i):
        away, here = swap(i)
        away.start()
        here.start()

    def swap_wait(i):
        away, here = swap(i)
        away.wait_recv()
        here.wait()

    def swap_marks():
        return remote(ve.at[own_rows], ve.at[own_rows], v_send.at[3], v_recv.at[3], other)

    x_start(0)
    start(ring(0))
    ring_own().start()
    swap_start(0)
    swap_start(1)

    numbers = (audio_clip[...] - gm * CLIPS).astype(F32)
    numbers = jnp.concatenate([numbers, numbers], axis=1)
    mk_own[...] = jnp.broadcast_to(numbers, (32, HD)).astype(BF)
    x_start(6)
    clips = lax.broadcasted_iota(jnp.int32, (HD, HD), 0)
    for i in range(4):
        same = video_clip[i : i + 1, :] - g * CLIPS == clips
        at = pl.multiple_of(core * 512 + i * HD, HD)
        ve[pl.ds(at, HD), :] = jnp.where(same, 0.0, FAR).T.astype(BF)
    swap_marks().start()

    lanes = clips.astype(F32)

    def expand(i, carry):
        bz, by = i // 4, lax.rem(i, 4)
        for cc in (0, 1):
            numbers = mk[cc, bz, by, pl.ds(0, 16), :].astype(F32)[0:1]
            am[cc, bz, by] = jnp.where(numbers == lanes, 1.0, 0.0).T[0:64].astype(BF)
        return carry

    first = jnp.where(core == 0, clip_smem[0], clip_smem[511] - 1) - g * CLIPS

    def block(i):
        return jnp.bitwise_and(first + i, 15)

    def pieces(ref, i, h):
        b, a = block(i - 1), block(i)
        where = (1, b // 4, jnp.bitwise_and(b, 3)), (0, a // 4, jnp.bitwise_and(a, 3))
        if h is None:
            return [ref[at] for at in where]
        cols = pl.ds(pl.multiple_of(lax.rem(h, 3) * HD, HD), HD)
        return [ref[(*at, slice(None), cols)] for at in where]

    def packed(top, total):
        high = total.astype(BF).astype(F32)
        gap = jnp.zeros((1, HD), F32)
        return jnp.concatenate([top, gap, total - high, gap, high, jnp.zeros((5, HD), F32)], axis=0)

    lane = lax.broadcasted_iota(jnp.int32, (HD, HD), 1)

    def audio_step(unit_scores, unit_weights, unit_values):
        if unit_scores is not None:
            u, buf, ref = unit_scores
            cols = pl.ds(pl.multiple_of(u // 2 * HD, HD), HD)
            blocks = [5 * lax.rem(u, 2) + i for i in range(5)]
            q = jnp.concatenate([piece for i in blocks for piece in pieces(ref, i, u // 2)], axis=0)
            mark = jnp.concatenate([piece for i in blocks for piece in pieces(am, i, None)], axis=0)
            q = jnp.concatenate([q, mark], axis=1)
        if unit_values is not None:
            h, tile, weights, high = unit_values[0] // 2, lax.rem(unit_values[0], 2), unit_values[1], unit_values[2]
            v = jnp.concatenate([vv[:, pl.ds(pl.multiple_of(h * HD, HD), HD)], jnp.ones((1024, HD), BF)], axis=1)
            out = jnp.dot(weights[...], v, preferred_element_type=F32)
        row = 0
        for c in range(4):
            if unit_scores is not None:
                rows = pl.ds(c * 256, 256)
                k = jnp.concatenate([vk[rows, cols], ve[rows, :]], axis=1)
                buf[:, c * 256 : (c + 1) * 256] = lax.dot_general(
                    q, k, (((1,), (1,)), ((), ())), preferred_element_type=F32
                )
            if unit_weights is not None:
                scores_w, weights_w, high_w = unit_weights
                for _ in range(10):
                    scores = scores_w[row : row + 16, :]
                    top = jnp.maximum(jnp.max(scores, axis=1, keepdims=True) * SCALE, LOW).astype(BF).astype(F32)
                    weights_w[row : row + 16, :] = jnp.exp2(scores * SCALE - top).astype(BF)
                    high_w[row : row + 16, :] = jnp.broadcast_to(top, (16, HD))
                    row += 16
        if unit_values is not None:
            where = pl.ds(pl.multiple_of(lax.rem(h, 3) * HD, HD), HD)
            for b in range(5):
                rows = slice(b * HD, (b + 1) * HD)
                window[h // 3, 5 * tile + b, where, :] = out[rows, :HD].T.astype(BF)
                stats = jnp.where(lane < 8, high[rows, :], out[rows, HD:]).T
                tops[h, 5 * tile + b] = stats[0:8]
                sums[h, 5 * tile + b] = stats[8:16]

    def audio(events):
        even, odd = (buf_c, wt_c, high_c), (buf_d, wt_d, high_d)

        def body(ref, lo, hi, i, carry):
            u = 2 * i
            audio_step((u + 2, buf_c, ref), odd, (u, wt_c, high_c))
            run_events(u, events, range(lo, hi, 2))
            audio_step((u + 3, buf_d, ref), even, (u + 1, wt_d, high_d))
            run_events(u + 1, events, range(lo + 1, hi, 2))
            return carry

        audio_step((0, buf_c, aq[0]), None, None)
        run_now(-2, events)
        audio_step((1, buf_d, aq[0]), even, None)
        run_now(-1, events)
        lax.fori_loop(0, 2, functools.partial(body, aq[0], 0, 4), 0)
        lax.fori_loop(2, 5, functools.partial(body, aq[1], 4, 10), 0)
        audio_step(None, odd, (10, wt_c, high_c))
        audio_step(None, None, (11, wt_d, high_d))

    def run_now(at, events):
        for where, event in events:
            if where == at:
                event()

    def run_events(i, events, steps_here):
        for at in sorted({at for at, _ in events if at in steps_here}):

            @pl.when(i == at)
            def _():
                run_now(at, events)

    empty = jnp.where(lax.broadcasted_iota(jnp.int32, (16, HD), 0) < 3, LOW, 0.0)

    def place_block(half, b):
        at = jnp.bitwise_and(b - first, 15)
        inside = (at < BLOCKS).astype(F32)
        at = jnp.minimum(at, BLOCKS - 1)
        bz, by = b // 4, lax.rem(b, 4)
        body = window[half, at, :, :].astype(F32)
        part[half, bz, by, pl.ds(0, STAT), :] = (body * inside).astype(BF)
        top = jnp.concatenate([tops[half * 3 + hh, at][0:1] for hh in range(3)], axis=0)
        total = jnp.concatenate([sums[half * 3 + hh, at][0:1] for hh in range(3)], axis=0)
        stats = packed(top, total)
        part[half, bz, by, pl.ds(STAT, 16), :] = (stats * inside + empty * (1.0 - inside)).astype(BF)

    def place_all(half):
        def body(b, carry):
            place_block(half, b)
            return carry

        lax.fori_loop(0, 16, body, 0)

    def slab(half, where, lo):
        if half == 0:
            return part.at[0, where, pl.ds(lo, 2)]
        return part.at[1, pl.ds(lo, 2), where]

    axes = ((z, zp, zm, z2, to_zp, to_zm), (y, yp, ym, y2, to_yp, to_ym))
    turn_by = 1 + 2 * core

    def cross(at, two):
        p, m = lax.rem(at + turn_by, 4), lax.rem(at + 4 - turn_by, 4)
        return at, p, m, two

    crosses = (cross(y, y2), cross(z, z2))

    def reduce1(half):
        _, p, m, two, to_p, to_m = axes[half]
        plan = (
            (slab(half, two, 0), to_p), (slab(half, two, 2), to_m),
            (slab(half, p, 2), to_p), (slab(half, m, 0), to_m),
            (slab(half, p, 0), to_p), (slab(half, m, 2), to_m),
        )
        return [
            remote(ref, got1.at[half, i], r_send.at[half, i], r_recv.at[half, i], dev)
            for i, (ref, dev) in enumerate(plan)
        ]

    def one(half, u):
        if half == 0:
            return part.at[0, z, u]
        return part.at[1, u, y]

    def reduce2(half):
        _, p, m, two = crosses[half]
        to_p, to_m = (device(g, z, u, core) if half == 0 else device(g, u, y, core) for u in (p, m))
        return [
            remote(one(half, u), got2.at[half, i], r_send.at[half, 6 + i], r_recv.at[half, 6 + i], dev)
            for i, (u, dev) in enumerate(((two, to_p), (m, to_m), (p, to_p)))
        ]

    def merged(refs):
        stats = [ref[pl.ds(STAT, 16), :].astype(F32) for ref in refs]
        tops = [x[0:3] for x in stats]
        top = tops[0]
        for x in tops[1:]:
            top = jnp.maximum(top, x)
        factors = [jnp.exp2(x - top) for x in tops]
        total = sum((x[8:11] + x[4:7]) * f for x, f in zip(stats, factors))
        outs = [
            sum(ref[pl.ds(hh * HD, HD), :].astype(F32) * f[hh : hh + 1] for ref, f in zip(refs, factors))
            for hh in range(3)
        ]
        return outs, top, total

    def merge_into(target, sources):
        outs, top, total = merged([target] + sources)
        for hh in range(3):
            target[pl.ds(hh * HD, HD), :] = outs[hh].astype(BF)
        target[pl.ds(STAT, 16), :] = packed(top, total).astype(BF)

    def merge_slab(half, where, lo, slots):
        def body(i, carry):
            target = part.at[0, where, lo + i] if half == 0 else part.at[1, lo + i, where]
            merge_into(target, [got1.at[half, slot, i] for slot in slots])
            return carry

        lax.fori_loop(0, 2, body, 0)

    def reduce_start(half):
        start(reduce1(half)[:4])

    def reduce_pass(half):
        _, p, m, *_ = axes[half]
        copies = reduce1(half)
        copies[0].wait_recv()
        merge_slab(half, p, 0, (0,))
        copies[4].start()
        copies[1].wait_recv()
        merge_slab(half, m, 2, (1,))
        copies[5].start()

    def reduce_cross(half):
        own = axes[half][0]
        arrive(reduce1(half)[2:])
        merge_slab(half, own, 0, (3, 4))
        merge_slab(half, own, 2, (2, 5))
        start(reduce2(half)[:2])

    def reduce_cross_pass(half):
        copies = reduce2(half)
        copies[0].wait_recv()
        merge_into(one(half, crosses[half][1]), [got2.at[half, 0]])
        copies[2].start()

    def reduce_end(half):
        own = crosses[half][0]
        arrive(reduce2(half)[1:])
        outs, _, total = merged([one(half, own)] + [got2.at[half, i] for i in (1, 2)])
        scale = 1.0 / total
        for hh in range(3):
            done = (outs[hh] * scale[hh : hh + 1]).T
            ao[:, pl.ds((half * 3 + hh) * HD, HD)] = done.astype(BF)

    def results(half):
        mine = pl.ds(pl.multiple_of(core * 768 + half * 384, 128), 384)
        cols = pl.ds(half * 384, 384)
        return [
            remote(
                ao.at[rows, cols], aout_hbm.at[:, mine], o_send.at[half, i], o_recv.at[half, core], dev
            )
            for i, (rows, dev) in enumerate(((pl.ds(64, 64), result_low), (pl.ds(0, 64), result_high)))
        ]

    def rows_of(ref, i, h):
        return jnp.concatenate(pieces(ref, 2 * i, h) + pieces(ref, 2 * i + 1, h), axis=0)

    def video_unit(u):
        cols = pl.ds(pl.multiple_of(u // 2 * HD, HD), HD)
        return cols, pl.ds(pl.multiple_of(lax.rem(u, 2) * 512, 512), 512)

    def video_both(u_scores, ref, u_out, buf_scores, buf_out):
        if u_scores is not None:
            cols, here = video_unit(u_scores)
            q = jnp.concatenate([vq[here, cols], ve[here, :]], axis=1)
        row = 0
        for c in range(5):
            if u_scores is not None:
                k = jnp.concatenate([rows_of(ref, c, u_scores // 2), rows_of(am, c, None)], axis=1)
                buf_scores[:, c * 256 : (c + 1) * 256] = lax.dot_general(
                    q, k, (((1,), (1,)), ((), ())), preferred_element_type=F32
                )
            if u_out is not None:
                for _ in range(7 if c < 2 else 6):
                    scores = buf_out[row : row + 16, :]
                    top = jnp.max(scores, axis=1, keepdims=True) * SCALE
                    wb[u_out, row : row + 16, :] = jnp.exp2(scores * SCALE - top).astype(BF)
                    row += 16

    def video_weights(events):
        def body(refs, lo, hi, i, carry):
            u = 2 * i
            video_both(u + 1, refs[0], u, buf_b, buf_a)
            run_events(u, events, range(lo, hi, 2))
            video_both(u + 2, refs[1], u + 1, buf_a, buf_b)
            run_events(u + 1, events, range(lo + 1, hi, 2))
            return carry

        video_both(0, ak[0], None, buf_a, None)
        run_now(-1, events)
        lax.fori_loop(0, 2, functools.partial(body, (ak[0], ak[0]), 0, 4), 0)
        lax.fori_loop(2, 3, functools.partial(body, (ak[0], ak[1]), 4, 6), 0)
        lax.fori_loop(3, 5, functools.partial(body, (ak[1], ak[1]), 6, 10), 0)
        video_both(11, ak[1], 10, buf_b, buf_a)
        run_now(10, events)
        video_both(None, None, 11, None, buf_b)
        run_now(11, events)

    def video_values(events):
        def body(ref, lo, hi, i, carry):
            cols, _ = video_unit(2 * i)
            v = jnp.concatenate([rows_of(ref, c, i) for c in range(5)], axis=0)
            v = jnp.concatenate([v, jnp.ones((BLOCKS * HD, HD), BF)], axis=1)
            for j in range(2):
                out = jnp.dot(wb[2 * i + j], v, preferred_element_type=F32)
                vo[pl.ds(j * 512, 512), cols] = (out[:, :HD] / out[:, HD:]).astype(BF)
            run_events(i, events, range(lo, hi))
            return carry

        lax.fori_loop(0, 3, functools.partial(body, av[0], 0, 3), 0)
        lax.fori_loop(3, 6, functools.partial(body, av[1], 3, 6), 0)

    def video_copies(i):
        cols = pl.ds(i * 256, 256)
        mine = pl.ds(pl.multiple_of(core * 768 + i * 256, 128), 256)
        return (
            remote(vo.at[other_rows, cols], vout_hbm.at[:, mine], w_send.at[i], w_recv.at[i], other),
            pltpu.make_async_copy(vo.at[own_rows, cols], vout_hbm.at[:, mine], w_local.at[i]),
        )

    def take(t, stage):
        for tensor in (6, 0) if t == 0 else (t,):
            if stage == 0 or stage == 2 and 4 <= t < 6:
                x_wait(tensor)
            else:
                arrive(gather(tensor, stage - 1))
            start(gather(tensor, stage))

    def x_next(t):
        x_wait(t - 1)
        if t == 4:
            arrive(ring(1))
            ring_own().wait()
        x_start(t)

    def ring_next():
        arrive(ring(0))
        start(ring(1))

    def make_marks():
        arrive(gather(6, 3))
        lax.fori_loop(0, 16, expand, 0)

    def ready_audio():
        swap_wait(0)
        swap_wait(1)
        swap_marks().wait_recv()
        arrive(gather(0, 3))

    def ready_video():
        swap_wait(2)
        arrive(gather(2, 3))

    def finish_half(half):
        reduce_end(half)
        start(results(half))

    steps = {
        "fV": ring_next, "vqs": lambda: swap_start(2), "ex": make_marks, "rQ1": lambda: arrive(gather(1, 3)), "rK1": lambda: arrive(gather(3, 3)),
        "tw0": lambda: arrive(gather(4, 3)), "tw1": lambda: arrive(gather(5, 3)),
        "w0": lambda: start(video_copies(0)), "w1": lambda: start(video_copies(1)), "w2": lambda: start(video_copies(2)),
    }
    for t, name in enumerate(("Q0", "Q1", "K0", "K1", "V0", "V1")):
        steps[f"s{name}"] = lambda t=t: x_next(t)
        for stage in range(4):
            steps[f"{stage + 1}{name}"] = lambda t=t, stage=stage: take(t, stage)
    for half in range(2):
        steps[f"p{half}"] = lambda half=half: place_all(half)
        steps[f"r1_{half}"] = lambda half=half: reduce_start(half)
        steps[f"r2_{half}"] = lambda half=half: reduce_pass(half)
        steps[f"ca_{half}"] = lambda half=half: reduce_cross(half)
        steps[f"cb_{half}"] = lambda half=half: reduce_cross_pass(half)
        steps[f"o_{half}"] = lambda half=half: finish_half(half)

    parts = {"": [], "A": [], "B": [], "X": [], "T": [], "Y": []}
    part_now, at = "", None
    for name in ORDER:
        if isinstance(name, int):
            at = name
        elif name in parts:
            part_now, at = name, None
        else:
            parts[part_now].append((at, steps[name]))

    def run(name):
        for _, step in parts[name]:
            step()

    run("")
    ready_audio()
    audio(parts["A"])
    run("B")
    ready_video()
    video_weights(parts["X"])
    run("T")
    video_values(parts["Y"])

    for t in range(7):
        sent(x_copies(t, 0))
        for stage in (2, 3) if 4 <= t < 6 else range(4):
            sent(gather(t, stage))
    sent(ring(0))
    sent(ring(1))
    for i in range(3):
        swap(i)[0].wait_send()
    swap_marks().wait_send()
    for half in range(2):
        sent(reduce1(half))
        sent(reduce2(half))
        sent(results(half))
        for cc in (0, 1):
            mine = pl.ds(cc * 768 + half * 384, 384)
            remote(
                ao.at[pl.ds(0, 64), pl.ds(half * 384, 384)], aout_hbm.at[:, mine], o_send.at[half, 0],
                o_recv.at[half, cc], result_low,
            ).wait_recv()
    for i in range(3):
        away, here = video_copies(i)
        here.wait()
        away.wait()


def hand_over(video_from, audio_from, video_to, audio_to, video, audio, sem_in, sem_out):
    pieces = [(video_from.at[r], video.at[r], video_to.at[r]) for r in (pl.ds(i * 128, 128) for i in range(4))]
    pieces.append((audio_from, audio, audio_to))
    arriving = [pltpu.make_async_copy(a, b, sem_in.at[i]) for i, (a, b, _) in enumerate(pieces)]
    leaving = [pltpu.make_async_copy(b, c, sem_out.at[i]) for i, (_, b, c) in enumerate(pieces)]
    for copy in arriving:
        copy.start()
    for into, out in zip(arriving, leaving):
        into.wait()
        out.start()
    for copy in leaving:
        copy.wait()


def on_device(video_q, video_k, video_v, audio_q, audio_k, audio_v, video_clip, audio_clip):
    anywhere = pl.BlockSpec(memory_space=pl.ANY)
    dma = pltpu.SemaphoreType.DMA
    results = (jax.ShapeDtypeStruct(video_q.shape, BF), jax.ShapeDtypeStruct(audio_k.shape, BF))
    made = pl.pallas_call(
        kernel,
        out_shape=results,
        in_specs=[
            pl.BlockSpec(memory_space=pltpu.SMEM),
            pl.BlockSpec(memory_space=pltpu.VMEM),
            pl.BlockSpec(memory_space=pltpu.VMEM),
        ]
        + [anywhere] * 6,
        out_specs=(anywhere, anywhere),
        scratch_shapes=[
            pltpu.VMEM((1024, 768), BF),
            pltpu.VMEM((1024, 768), BF),
            pltpu.VMEM((1024, 768), BF),
            pltpu.VMEM((1024, HD), BF),
            pltpu.VMEM((2, 4, 4, 64, 384), BF),
            pltpu.VMEM((2, 4, 4, 64, 384), BF),
            pltpu.VMEM((2, 4, 4, 64, 384), BF),
            pltpu.VMEM((2, 4, 4, 64, 384), BF),
            pltpu.VMEM((2, 4, 4, 64, 384), BF),
            pltpu.VMEM((2, 4, 4, 64, 384), BF),
            pltpu.VMEM((4, 64, 1536), BF),
            pltpu.VMEM((2, 4, 4, 32, HD), BF),
            pltpu.VMEM((2, 4, 4, 64, HD), BF),
            pltpu.VMEM((32, HD), BF),
            pltpu.VMEM((640, 1024), F32),
            pltpu.VMEM((640, 1024), F32),
            pltpu.VMEM((640, 1024), BF),
            pltpu.VMEM((640, 1024), BF),
            pltpu.VMEM((640, HD), F32),
            pltpu.VMEM((640, HD), F32),
            pltpu.VMEM((512, BLOCKS * HD), F32),
            pltpu.VMEM((512, BLOCKS * HD), F32),
            pltpu.VMEM((12, 512, BLOCKS * HD), BF),
            pltpu.VMEM((6, BLOCKS, 8, HD), F32),
            pltpu.VMEM((6, BLOCKS, 8, HD), F32),
            pltpu.VMEM((2, BLOCKS, STAT, HD), BF),
            pltpu.VMEM((2, 4, 4, ROWS, HD), BF),
            pltpu.VMEM((2, 6, 2, ROWS, HD), BF),
            pltpu.VMEM((2, 3, ROWS, HD), BF),
            pltpu.VMEM((1024, 768), BF),
            pltpu.VMEM((HD, 768), BF),
            dma((7, 2)),
            dma((7, 2)),
            dma((4,)),
            dma((4,)),
            dma,
            dma((7, 16)),
            dma((7, 16)),
            dma((4,)),
            dma((4,)),
            dma((3,)),
            dma((2, 9)),
            dma((2, 9)),
            dma((2, 2)),
            dma((2, 2)),
            dma((3,)),
            dma((3,)),
            dma((3,)),
        ],
        compiler_params=pltpu.CompilerParams(
            collective_id=0, has_side_effects=True, vmem_limit_bytes=60 * 1024 * 1024
        ),
    )(
        video_clip, video_clip.reshape(4, HD), audio_clip.reshape(1, 64), video_q, video_k, video_v, audio_q, audio_k,
        audio_v,
    )
    return pl.pallas_call(
        hand_over,
        out_shape=results,
        in_specs=[anywhere] * 2,
        out_specs=(anywhere, anywhere),
        scratch_shapes=[pltpu.VMEM((512, 1536), BF), pltpu.VMEM((64, 1536), BF), dma((5,)), dma((5,))],
    )(*made)


def solution(mesh):
    spread = P(("grp", "seq"), None)
    return jax.shard_map(
        on_device,
        mesh=mesh,
        in_specs=(spread,) * 6 + (P(("grp", "seq")),) * 2,
        out_specs=(spread, spread),
        check_vma=False,
    )
```
